256 devices in a mesh: node: 64 (over y_hi, z, x), feat: 4 (over y_lo, core).
Axes of the slice: x: 4, y: 4 (y_hi: 2, y_lo: 2; y = y_hi * 2 + y_lo), z: 8, core: 2. Of those that a mesh axis runs over, the one named last changes fastest.
Arguments:
- features: bfloat16 [65536, 256], P('node', 'feat'), may hold values from -6 to 6
- w_self: bfloat16 [256, 256], P('feat'), may hold values from -0.375 to 0.375
- w_neigh: bfloat16 [256, 256], P('feat'), may hold values from -0.375 to 0.375
- tile_rows: int32 [16384], P('node'), may hold values from 0 to 7
- tile_cols: int32 [16384], P('node'), may hold values from 0 to 511
- tile_count: int32 [64], P('node'), may hold values from 64 to 256, as said below
- edge_bits: int32 [16384, 16, 128], P('node'), may hold values from 0 to 255, as said below
- cotangent: float32 [65536, 256], P('node', 'feat'), may hold values from -6 to 6
Outputs:
- activated: float32 [65536, 256], P('node', 'feat')
- grad_features: float32 [65536, 256], P('node', 'feat')
- grad_self: float32 [256, 256], P('feat')
- grad_neigh: float32 [256, 256], P('feat')
The draws below stay inside these ranges and needn't reach their ends.
Inputs may be any that keep to these rules, and one draw needn't show every extreme that they name: `tile_count`: slots of a block at or beyond its count are ignored; some block is full in every draw. `edge_bits`: bits 0 to 7 of each word hold edges as in the reference program; higher bits are 0.
All inputs are finite; a program needn't handle non-finite values.
Results may differ from the reference program's by a relative error of at most 0.0028.
Values may be sent and summed in bfloat16 or wider, within the bound.
A program may use at most 128 MiB of HBM per device.

```python
import jax
import jax.numpy as jnp
from jax import lax

F = 256
TILE = 128
ROW_TILES = 8
TPB = 256
NODES = 65536
NTILES = 512
TILES = 16384


def draw_tile_count(key, part):
    key = jax.random.fold_in(key, 7)
    first, second = jax.random.split(key)
    counts = jax.random.randint(first, (TILES // TPB,), TPB // 4, TPB + 1).astype(jnp.int32)
    where = jax.random.randint(second, (), 0, TILES // TPB)
    return counts.at[where].set(TPB)


def draw_edge_bits(key, part):
    key = jax.random.fold_in(key, 11)
    first, second, third = jax.random.split(key, 3)
    pick = jax.random.randint(first, (TILES // TPB, TILE), 0, 32).astype(jnp.int32)
    level = jnp.where(pick == 0, 0, jnp.left_shift(jnp.int32(60), pick % 4)).astype(jnp.int32)
    level = jnp.repeat(level, TPB, axis=0)
    span = 8 * TILE * TPB // ROW_TILES

    def add_bit(index, words):
        draws = jax.random.randint(jax.random.fold_in(second, index), (TILES, TILE // 8, TILE), 0, span).astype(jnp.int32)
        bit = (draws < level[:, None, :]).astype(jnp.int32)
        return words + jnp.left_shift(bit, index)
    words = lax.fori_loop(0, 8, add_bit, jnp.zeros((TILES, TILE // 8, TILE), jnp.int32))
    slot_key, word_key, column_key = jax.random.split(third, 3)
    slot = jax.random.randint(slot_key, (), 0, TILES).astype(jnp.int32)
    word = jax.random.randint(word_key, (), 0, TILE // 8).astype(jnp.int32)
    column = jax.random.randint(column_key, (), 0, TILE).astype(jnp.int32)
    return words.at[slot, word, column].set(jnp.int32(255))


def touch_ends(values, own_key, least, largest):
    shape = values.shape
    place = [jax.random.randint(jax.random.fold_in(own_key, axis), (), 0, shape[axis]) for axis in range(len(shape))]
    values = values.at[tuple(place)].set(least)
    longest = shape.index(max(shape))
    place[longest] = (place[longest] + 1) % shape[longest]
    return values.at[tuple(place)].set(largest)


def block_levels(stream_key, extent, cuts, least, high):
    level = 1.0
    for position, parts in cuts:
        steps = jax.random.uniform(jax.random.fold_in(jax.random.fold_in(stream_key, 6), position), (parts,), jnp.float32, least / len(cuts), high / len(cuts))
        level = level * jnp.repeat(jnp.exp(steps), extent[position] // parts).reshape((-1,) + (1,) * (len(extent) - 1 - position))
    return level


def centred(key, shape, deviation, most, cuts=(), kind=jnp.bfloat16):
    entries = deviation * jax.random.normal(key, shape, jnp.float32)
    if cuts:
        entries = entries * block_levels(key, shape, cuts, -0.22, 0.18)
    return jnp.clip(entries, -most, most).astype(kind)


def setup_inputs(seed: int = 0) -> dict:
    seeds = jax.random.split(jax.random.key(seed), 9)
    features = centred(seeds[0], (NODES, F), 1.0, 6.0, ((0, 64), (1, 4)))
    w_self = centred(seeds[1], (F, F), F ** -0.5, 0.375, ((0, 4),))
    w_neigh = centred(seeds[2], (F, F), F ** -0.5, 0.375, ((0, 4),))
    tile_rows = touch_ends(jax.random.randint(seeds[3], (TILES,), 0, ROW_TILES), jax.random.fold_in(seeds[3], 1), 0, ROW_TILES - 1).astype(jnp.int32)
    tile_cols = touch_ends(jax.random.randint(seeds[4], (TILES,), 0, NTILES), jax.random.fold_in(seeds[4], 1), 0, NTILES - 1).astype(jnp.int32)
    tile_count = draw_tile_count(jax.random.fold_in(seeds[8], 71), 0)
    edge_bits = draw_edge_bits(jax.random.fold_in(seeds[8], 71), 0)
    cotangent = centred(seeds[7], (NODES, F), 1.0, 6.0, ((0, 64), (1, 4)), jnp.float32)
    return {"features": features, "w_self": w_self, "w_neigh": w_neigh, "tile_rows": tile_rows, "tile_cols": tile_cols, "tile_count": tile_count, "edge_bits": edge_bits, "cotangent": cotangent}


def unpack_bits(words):
    shifts = jnp.arange(8, dtype=jnp.int32)
    planes = jnp.bitwise_and(jnp.right_shift(words[:, :, None, :], shifts[None, None, :, None]), 1)
    return planes.reshape(words.shape[0], words.shape[1] * 8, words.shape[2])


def block_slots(tile_rows, tile_cols, tile_count, edge_bits, block):
    start = (block * TPB).astype(jnp.int32)
    rows = lax.dynamic_slice_in_dim(tile_rows, start, TPB)
    picks = lax.dynamic_slice_in_dim(tile_cols, start, TPB)
    words = lax.dynamic_slice_in_dim(edge_bits, start, TPB, 0)
    live_tiles = (jnp.arange(TPB, dtype=jnp.int32) < tile_count[block]).astype(jnp.float32)
    mask_t = unpack_bits(words).astype(jnp.float32) * live_tiles[:, None, None]
    return rows, picks, mask_t


def reference(features, w_self, w_neigh, tile_rows, tile_cols, tile_count, edge_bits, cotangent):
    hi = lax.Precision.HIGHEST
    blocks = NTILES // ROW_TILES
    tiled = features.reshape(NTILES, TILE, F)

    def gather_block(block):
        rows, picks, mask_t = block_slots(tile_rows, tile_cols, tile_count, edge_bits, block)
        picked = tiled[picks].astype(jnp.float32)
        products = jnp.einsum("tqp,tqf->tpf", mask_t, picked, precision=hi)
        rowhot = (rows[:, None] == jnp.arange(ROW_TILES, dtype=jnp.int32)[None, :]).astype(jnp.float32)
        summed = jnp.einsum("tr,tpf->rpf", rowhot, products, precision=hi)
        counts = jnp.einsum("tr,tp->rp", rowhot, jnp.sum(mask_t, axis=1), precision=hi)
        return summed, counts

    summed, counts = lax.map(gather_block, jnp.arange(blocks, dtype=jnp.int32))
    summed = summed.reshape(NODES, F)
    degree = jnp.maximum(counts.reshape(NODES), 1.0)
    averaged = (summed / degree[:, None]).astype(jnp.bfloat16)
    pre = jnp.dot(features, w_self, preferred_element_type=jnp.float32) + jnp.dot(averaged, w_neigh, preferred_element_type=jnp.float32)
    sigmoid_z = jax.nn.sigmoid(pre)
    activated = pre * sigmoid_z
    grad_pre = cotangent * sigmoid_z * (1.0 + pre * (1.0 - sigmoid_z))
    grad_self = jnp.dot(features.astype(jnp.float32).T, grad_pre, precision=hi)
    grad_neigh = jnp.dot(averaged.astype(jnp.float32).T, grad_pre, precision=hi)
    scaled = jnp.dot(grad_pre, w_neigh.astype(jnp.float32).T, precision=hi) / degree[:, None]
    direct = jnp.dot(grad_pre, w_self.astype(jnp.float32).T, precision=hi)
    scaled_tiles = scaled.reshape(blocks, ROW_TILES, TILE, F)

    def scatter_block(block, accum):
        rows, picks, mask_t = block_slots(tile_rows, tile_cols, tile_count, edge_bits, block)
        own = lax.dynamic_index_in_dim(scaled_tiles, block, 0, keepdims=False)
        source = own[rows]
        contrib = jnp.einsum("tqp,tpf->tqf", mask_t, source, precision=hi)
        return accum.at[picks].add(contrib)

    accum = lax.fori_loop(0, blocks, scatter_block, jnp.zeros((NTILES, TILE, F), jnp.float32))
    grad_features = direct + accum.reshape(NODES, F)
    return activated, grad_features, grad_self, grad_neigh
```

```python
import jax
import jax.numpy as jnp
from jax import lax
from jax.experimental import pallas as pl
from jax.experimental.pallas import tpu as pltpu
from jax.sharding import PartitionSpec as P

MESH = pl.DeviceIdType.MESH
BF = jnp.bfloat16
F32 = jnp.float32
NY, NZ, NX = 2, 8, 4
TPN = 8
TA = 3
TB = TPN - TA
FC = 64
TILE = 128
ROWS = TPN * TILE
SLOTS = 256
UNROLL = 8
ANY = pl.BlockSpec(memory_space=pl.ANY)
VMEM = pl.BlockSpec(memory_space=pltpu.VMEM)
SMEM = pl.BlockSpec(memory_space=pltpu.SMEM)
NEAR_FIRST = ((0,), (1, 7), (2, 6), (3, 5), (4,))


def place():
    node, feat = lax.axis_index("node"), lax.axis_index("feat")
    return node // (NZ * NX), lax.rem(node // NX, NZ), lax.rem(node, NX), feat


def node_of(y, z, x):
    return (y * NZ + z) * NX + x


def across(feat):
    return lax.rem(feat + 2, 4)


def sibling(feat):
    return feat + 1 - 2 * lax.rem(feat, 2)


def meet(peers):
    barrier = pltpu.get_barrier_semaphore()
    for peer in peers:
        pl.semaphore_signal(barrier, inc=1, device_id=peer, device_id_type=MESH)
    pl.semaphore_wait(barrier, len(peers))


def remote(src, dst, send, recv, peer):
    return pltpu.make_async_remote_copy(
        src_ref=src, dst_ref=dst, send_sem=send, recv_sem=recv, device_id=peer, device_id_type=MESH
    )


def feat_gather(mine, full, feat, node, sems, send, recv):
    one, two = (node, across(feat)), (node, sibling(feat))
    a = remote(mine, full.at[feat], send.at[sems], recv.at[sems], one)
    b = remote(mine, full.at[feat], send.at[sems + 1], recv.at[sems + 1], two)
    a.start()
    b.start()

    def step():
        far = across(feat)
        remote(full.at[far], full.at[far], send.at[sems], recv.at[sems], one).wait_recv()
        c = remote(full.at[far], full.at[far], send.at[sems + 2], recv.at[sems + 2], two)
        c.start()

        def finish():
            near = sibling(feat)
            diag = across(near)
            remote(full.at[near], full.at[near], send.at[sems + 1], recv.at[sems + 1], two).wait_recv()
            remote(full.at[diag], full.at[diag], send.at[sems + 2], recv.at[sems + 2], two).wait_recv()
            a.wait_send()
            b.wait_send()
            c.wait_send()

        return finish

    return step


def gather_kernel(own, xown, wown, full, xfull, wfull,
                  bzs, bzr, bxs, bxr, axs, axr, azs, azr, ys, yr, fs, fr, ls):
    y, z, x, feat = place()
    node = node_of(y, z, x)
    oy = 1 - y

    def zof(k):
        return lax.rem(z + k + 2 * NZ, NZ)

    def xof(k):
        return lax.rem(x + k + 2 * NX, NX)

    def yof(j):
        return y + j - 2 * j * y

    def zdev(s):
        return (node_of(y, zof(s), x), feat)

    def xdev(s):
        return (node_of(y, z, xof(s)), feat)

    ydev = (node_of(oy, z, x), feat)
    meet([zdev(1), zdev(-1), xdev(1), xdev(-1), ydev, (node, across(feat)), (node, sibling(feat))])

    def slab(ref, lead, part, half):
        t = pl.ds(0, TA) if part == 0 else pl.ds(TA, TB)
        if half is None:
            return ref.at[(*lead, t)]
        return ref.at[(*lead, t, pl.ds(half * (FC // 2), FC // 2))]

    def move(j, zr, xr, part, s, half, send, recv, dev):
        lead = (yof(j), zof(zr), xof(xr))
        dst = slab(full, lead, part, half)
        return remote(dst, dst, send, recv, dev)

    def h(s, last):
        return (0 if s > 0 else 1) if last else None

    def bz(s, j, d, arriving=False):
        i = (0 if s > 0 else 1, j, d - 1)
        zr = -s * d if arriving else -s * (d - 1)
        return move(j, zr, 0, 1, s, h(s, d == 4), bzs.at[i], bzr.at[i], zdev(s))

    def bx(s, j, zr, d, arriving=False):
        i = (0 if s > 0 else 1, j, lax.rem(zr + NZ, NZ), d - 1)
        xr = -s * d if arriving else -s * (d - 1)
        return move(j, zr, xr, 1, s, h(s, d == 2), bxs.at[i], bxr.at[i], xdev(s))

    def ax(s, j, d, arriving=False):
        i = (0 if s > 0 else 1, j, d - 1)
        xr = -s * d if arriving else -s * (d - 1)
        return move(j, 0, xr, 0, s, h(s, d == 2), axs.at[i], axr.at[i], xdev(s))

    def az(s, j, xr, d, arriving=False):
        i = (0 if s > 0 else 1, j, lax.rem(xr + NX, NX), d - 1)
        zr = -s * d if arriving else -s * (d - 1)
        return move(j, zr, xr, 0, s, h(s, d == 4), azs.at[i], azr.at[i], zdev(s))

    local = pltpu.make_async_copy(own, full.at[y, z, x], ls.at[0])
    local.start()
    yput = remote(own, full.at[y, z, x], ys.at[0], yr.at[0], ydev)
    yput.start()
    local.wait()
    both = (1, -1)
    for j in range(2):
        if j == 1:
            remote(own, full.at[oy, z, x], ys.at[0], yr.at[0], ydev).wait_recv()
        for s in both:
            ax(s, j, 1).start()
            bz(s, j, 1).start()
        for s in both:
            bx(s, j, 0, 1).start()
            az(s, j, 0, 1).start()
        if j == 0:
            xlocal = pltpu.make_async_copy(xown, xfull.at[feat], ls.at[1])
            xlocal.start()
            wlocal = pltpu.make_async_copy(wown, wfull.at[feat], ls.at[2])
            wlocal.start()
            xstep = feat_gather(xown, xfull, feat, node, 0, fs, fr)
            wstep = feat_gather(wown, wfull, feat, node, 3, fs, fr)
    for j in range(2):
        for s in both:
            ax(s, j, 1, True).wait_recv()
        for s in both:
            az(s, j, -1, 1).start()
            az(s, j, 1, 1).start()
            ax(s, j, 2).start()
    for j in range(2):
        for s in both:
            ax(s, j, 2, True).wait_recv()
        for s in both:
            az(s, j, 2, 1).start()
    xfinish, wfinish = xstep(), wstep()

    for d in range(1, 5):
        for j in range(2):
            for s in both:
                bz(s, j, d, True).wait_recv()
                if d < 4:
                    bz(s, j, d + 1).start()
            for s in both:
                if d < 4:
                    bx(s, j, -d, 1).start()
                    bx(s, j, d, 1).start()
                else:
                    bx(s, j, 4, 1).start()

        def aunit(k, _, d=d):
            j, xr = k // NX, lax.rem(k, NX)
            for s in both:
                az(s, j, xr, d, True).wait_recv()
                if d < 4:
                    az(s, j, xr, d + 1).start()
            return 0

        lax.fori_loop(0, 2 * NX, aunit, 0)
        for j in range(2):
            for zr in sorted({-(d - 1), d - 1}):
                for s in both:
                    bx(s, j, zr, 1, True).wait_recv()
                    bx(s, j, zr, 2).start()
    for j in range(2):
        for s in both:
            bx(s, j, 4, 1, True).wait_recv()
            bx(s, j, 4, 2).start()
    for j in range(2):
        def xunit(zr, _, j=j):
            for s in both:
                bx(s, j, zr, 2, True).wait_recv()
                for d in (1, 2):
                    bx(s, j, zr, d).wait_send()
            return 0

        lax.fori_loop(0, NZ, xunit, 0)

        def zunit(xr, _, j=j):
            for s in both:
                for d in range(1, 5):
                    az(s, j, xr, d).wait_send()
            return 0

        lax.fori_loop(0, NX, zunit, 0)
        for s in both:
            for d in range(1, 5):
                bz(s, j, d).wait_send()
            for d in (1, 2):
                ax(s, j, d).wait_send()
    xfinish()
    wfinish()
    xlocal.wait()
    wlocal.wait()
    yput.wait_send()


def gather(own, xown, wown):
    dma = pltpu.SemaphoreType.DMA
    return pl.pallas_call(
        gather_kernel,
        out_shape=(
            jax.ShapeDtypeStruct((NY, NZ, NX, TPN, FC, TILE), BF),
            jax.ShapeDtypeStruct((4, *xown.shape), BF),
            jax.ShapeDtypeStruct((4, *wown.shape), BF),
        ),
        in_specs=[ANY] * 3,
        out_specs=(ANY,) * 3,
        scratch_shapes=[
            dma((2, 2, 4)), dma((2, 2, 4)), dma((2, 2, NZ, 2)), dma((2, 2, NZ, 2)),
            dma((2, 2, 2)), dma((2, 2, 2)), dma((2, 2, NX, 4)), dma((2, 2, NX, 4)),
            dma((1,)), dma((1,)), dma((6,)), dma((6,)), dma((3,)),
        ],
        compiler_params=pltpu.CompilerParams(collective_id=0, has_side_effects=True),
        name="gather",
    )(own, xown, wown)


def planes_of(words):
    return jnp.concatenate(
        [jnp.bitwise_and(jnp.right_shift(words, b), 1).astype(F32) for b in range(8)], axis=0
    )


def live_words(edges, slot, count):
    return edges[slot] * (slot < count).astype(jnp.int32)


def forward_kernel(rows, cols, count, edges, full, avg, deg, acc, cnt):
    acc[...] = jnp.zeros_like(acc)
    cnt[...] = jnp.zeros_like(cnt)
    limit = count[0]

    def group(g, _):
        for u in range(UNROLL):
            slot = g * UNROLL + u
            planes = planes_of(live_words(edges, slot, limit))
            part = jnp.dot(full[cols[slot]], planes.astype(BF), preferred_element_type=F32)
            row = rows[slot]
            acc[row] += part
            cnt[row] += jnp.sum(planes.reshape(16, 8, TILE), axis=0)
        return 0

    lax.fori_loop(0, SLOTS // UNROLL, group, 0)
    for r in range(TPN):
        degree = jnp.maximum(jnp.sum(cnt[r], axis=0, keepdims=True), 1.0)
        deg[:, r * TILE:(r + 1) * TILE] = degree
        avg[:, r * TILE:(r + 1) * TILE] = (acc[r] / degree).astype(BF)


def forward(rows, cols, count, edges, full):
    return pl.pallas_call(
        forward_kernel,
        out_shape=(
            jax.ShapeDtypeStruct((FC, ROWS), BF),
            jax.ShapeDtypeStruct((1, ROWS), F32),
        ),
        in_specs=[SMEM, SMEM, SMEM, VMEM, VMEM],
        out_specs=(VMEM, VMEM),
        scratch_shapes=[pltpu.VMEM((TPN, FC, TILE), F32), pltpu.VMEM((TPN, 8, TILE), F32)],
        compiler_params=pltpu.CompilerParams(vmem_limit_bytes=40 * 2**20),
        name="forward_sums",
    )(rows, cols, count, edges, full)


def nt(a, b):
    return lax.dot_general(a, b, (((1,), (1,)), ((), ())), preferred_element_type=F32)


def dense_kernel(avg, xfull, wfull, wself, wneigh, deg, cot, act, direct, scaled, wgrad,
                 av, gr, send, recv):
    y, z, x, feat = place()
    node = node_of(y, z, x)
    meet([(node, across(feat)), (node, sibling(feat))])
    av[feat] = avg[...]
    step = feat_gather(avg, av, feat, node, 0, send, recv)
    off = pl.multiple_of(feat * FC, FC)

    def cols_of(k, which):
        return wfull[k, pl.ds(which * 256 + off, FC), :]

    def dot(a, b):
        return jnp.dot(a, b, preferred_element_type=F32)

    pre = dot(cols_of(0, 0), xfull[0])
    for k in range(1, 4):
        pre += dot(cols_of(k, 0), xfull[k])
    step()()
    for k in range(4):
        pre += dot(cols_of(k, 1), av[k])
    sig = jax.nn.sigmoid(pre)
    act[...] = pre * sig
    grad = cot[...] * sig * (1.0 + pre * (1.0 - sig))
    gr[feat] = grad.astype(BF)
    step = feat_gather(gr.at[feat], gr, feat, node, 3, send, recv)
    step()()
    sums = dot(wneigh[:, 0:FC], gr[0])
    straight = dot(wself[:, 0:FC], gr[0])
    for k in range(1, 4):
        sums += dot(wneigh[:, k * FC:(k + 1) * FC], gr[k])
        straight += dot(wself[:, k * FC:(k + 1) * FC], gr[k])
    direct[...] = straight
    sums = (sums / deg[...]).astype(BF)
    for r in range(TPN):
        scaled[r] = sums[:, r * TILE:(r + 1) * TILE]
    mine = xfull[feat]
    for k in range(4):
        wgrad[0:FC, k * FC:(k + 1) * FC] = nt(mine, gr[k])
        wgrad[FC:2 * FC, k * FC:(k + 1) * FC] = nt(avg[...], gr[k])


def dense(avg, xfull, wfull, wself, wneigh, deg, cot):
    dma = pltpu.SemaphoreType.DMA
    return pl.pallas_call(
        dense_kernel,
        out_shape=(
            jax.ShapeDtypeStruct((FC, ROWS), F32),
            jax.ShapeDtypeStruct((FC, ROWS), F32),
            jax.ShapeDtypeStruct((TPN, FC, TILE), BF),
            jax.ShapeDtypeStruct((2 * FC, 4 * FC), F32),
        ),
        in_specs=[VMEM] * 7,
        out_specs=(VMEM,) * 4,
        scratch_shapes=[
            pltpu.VMEM((4, FC, ROWS), BF), pltpu.VMEM((4, FC, ROWS), BF), dma((6,)), dma((6,)),
        ],
        compiler_params=pltpu.CompilerParams(
            collective_id=1, has_side_effects=True, vmem_limit_bytes=40 * 2**20
        ),
        name="dense",
    )(avg, xfull, wfull, wself, wneigh, deg, cot)


def backward_kernel(rows, cols, count, edges, source, out, acc):
    acc[...] = jnp.zeros_like(acc)
    limit = count[0]

    def group(g, _):
        for u in range(UNROLL):
            slot = g * UNROLL + u
            mask = planes_of(live_words(edges, slot, limit)).astype(BF)
            part = nt(source[rows[slot]], mask)
            acc[cols[slot]] += part
        return 0

    lax.fori_loop(0, SLOTS // UNROLL, group, 0)

    def narrow(i, _):
        out[pl.ds(i * 8, 8)] = acc[pl.ds(i * 8, 8)].astype(BF)
        return 0

    lax.fori_loop(0, acc.shape[0] // 8, narrow, 0)


def backward(rows, cols, count, edges, source):
    tiles = NY * NZ * NX * TPN
    return pl.pallas_call(
        backward_kernel,
        out_shape=jax.ShapeDtypeStruct((tiles, FC, TILE), BF),
        in_specs=[SMEM, SMEM, SMEM, VMEM, VMEM],
        out_specs=VMEM,
        scratch_shapes=[pltpu.VMEM((tiles, FC, TILE), F32)],
        compiler_params=pltpu.CompilerParams(vmem_limit_bytes=48 * 2**20),
        name="backward_sums",
    )(rows, cols, count, edges, source)


def scatter_kernel(part, wgrad, out, wout,
                   rbx, rbz, rax, raz, ry, w1, w2,
                   bzs, bzr, bxs, bxr, axs, axr, azs, azr, ys, yr, ws, wr):
    y, z, x, feat = place()
    oy = 1 - y

    def zof(k):
        return lax.rem(z + k + 2 * NZ, NZ)

    def xof(k):
        return lax.rem(x + k + 2 * NX, NX)

    def yof(j):
        return y + j - 2 * j * y

    def zdev(s):
        return (node_of(y, zof(s), x), feat)

    def xdev(s):
        return (node_of(y, z, xof(s)), feat)

    plane = y * NX + x

    def pof(k):
        return lax.rem(plane + k, NY * NX)

    def pdev(k):
        p = pof(k)
        return (node_of(p // NX, z, lax.rem(p, NX)), feat)

    meet([zdev(k) for k in range(1, NZ)] + [pdev(k) for k in range(1, NY * NX)])
    ydev = (node_of(oy, z, x), feat)

    PA, PB = pl.ds(0, TA), pl.ds(TA, TB)
    both = (1, -1)

    def di(s):
        return 0 if s > 0 else 1

    def cut(half):
        return pl.ds(half * (FC // 2), FC // 2)

    def hop(buf, i, d, last, half, src, send, recv, dev):
        if d == last:
            return remote(src.at[:, cut(half)], buf.at[i].at[:, cut(half)], send.at[i], recv.at[i], dev)
        return remote(src, buf.at[i], send.at[i], recv.at[i], dev)

    def bx(s, j, zr, d):
        i = (di(s), j, lax.rem(zr + NZ, NZ), d - 1)
        src = part.at[yof(j), zof(zr), xof(2 * s), PB] if d == 2 else rbx.at[di(s), j, lax.rem(zr + NZ, NZ), 1]
        return hop(rbx, i, d, 2, di(s), src, bxs, bxr, xdev(s))

    def az(s, j, xr, d):
        i = (di(s), j, lax.rem(xr + NX, NX), d - 1)
        src = part.at[yof(j), zof(4 * s), xof(xr), PA] if d == 4 else raz.at[di(s), j, lax.rem(xr + NX, NX), d]
        return hop(raz, i, d, 4, di(s), src, azs, azr, zdev(s))

    def bz(s, j, d):
        i = (di(s), j, d - 1)
        src = rbx.at[0, j, 4, 0] if d == 4 else rbz.at[di(s), j, d]
        return hop(rbz, i, d, 4, di(s), src, bzs, bzr, zdev(s))

    def ax(s, j, d):
        i = (di(s), j, d - 1)
        src = raz.at[0, j, 2, 0] if d == 2 else rax.at[di(s), j, 1]
        return hop(rax, i, d, 2, di(s), src, axs, axr, xdev(s))

    def add(buf, i, term, first, s):
        if first:
            a, b = cut(di(s)), cut(1 - di(s))
            buf[(*i, slice(None), a)] = (
                buf[(*i, slice(None), a)].astype(F32) + term[:, a].astype(F32)
            ).astype(BF)
            buf[(*i, slice(None), b)] = term[:, b]
        else:
            buf[i] = (buf[i].astype(F32) + term[...].astype(F32)).astype(BF)

    def total(buf, i, term):
        one, two = (0, *i, 0), (1, *i, 0)
        buf[one] = (buf[one].astype(F32) + buf[two].astype(F32) + term[...].astype(F32)).astype(BF)

    def bx_first(j, zr):
        for s in both:
            bx(s, j, zr, 2).start()

    def bx_next(j, zr):
        r = lax.rem(zr + NZ, NZ)
        for s in both:
            bx(s, j, zr, 2).wait_recv()
            add(rbx, (di(s), j, r, 1), part.at[yof(j), zof(zr), xof(s), PB], True, s)
            bx(s, j, zr, 1).start()

    def bx_last(j, zr):
        r = lax.rem(zr + NZ, NZ)
        for s in both:
            bx(s, j, zr, 1).wait_recv()
        total(rbx, (j, r), part.at[yof(j), zof(zr), x, PB])

    def az_next(d):
        def unit(k, _):
            j, xr = 1 - k // NX, lax.rem(k + 2, NX)
            for s in both:
                az(s, j, xr, d).wait_recv()
                add(raz, (di(s), j, xr, d - 1), part.at[yof(j), zof(s * (d - 1)), xof(xr), PA], d == 4, s)
                az(s, j, xr, d - 1).start()
            return 0

        lax.fori_loop(0, 2 * NX, unit, 0)

    def bz_next(d):
        for j in (1, 0):
            for s in both:
                bz(s, j, d).wait_recv()
                add(rbz, (di(s), j, d - 1), rbx.at[0, j, lax.rem(s * (d - 1) + NZ, NZ), 0], d == 4, s)
                bz(s, j, d - 1).start()

    def wcopy(phase, k):
        i = phase * 7 + k - 1
        if phase == 0:
            return remote(wgrad.at[pl.ds(pl.multiple_of(zof(k) * 16, 16), 16)], w1.at[k - 1], ws.at[i], wr.at[i], zdev(k))
        if phase == 1:
            return remote(w2.at[plane], w2.at[plane], ws.at[i], wr.at[i], pdev(k))
        rows = pl.ds(pl.multiple_of(z * 16, 16), 16)
        return remote(wout.at[rows], wout.at[rows], ws.at[i], wr.at[i], zdev(k))

    def wexpect(phase, k):
        i = phase * 7 + k - 1
        if phase == 0:
            dst = w1.at[k - 1]
        elif phase == 1:
            dst = w2.at[lax.rem(plane + NY * NX - k, NY * NX)]
        else:
            dst = wout.at[pl.ds(pl.multiple_of(zof(-k) * 16, 16), 16)]
        return remote(dst, dst, ws.at[i], wr.at[i], zdev(k))

    def units(r):
        return NEAR_FIRST[4 - r]

    for r in range(2):
        for j in (1, 0):
            for zr in units(r):
                bx_first(j, zr)
        if r == 0:
            def begin(k, _):
                j, xr = 1 - k // NX, lax.rem(k + 2, NX)
                for s in both:
                    az(s, j, xr, 4).start()
                return 0

            lax.fori_loop(0, 2 * NX, begin, 0)
            for k in range(1, NZ):
                wcopy(0, k).start()
    for r in range(6):
        if r < 5:
            for j in (1, 0):
                for zr in units(r):
                    bx_next(j, zr)
                if r + 2 < 5:
                    for zr in units(r + 2):
                        bx_first(j, zr)
        if r >= 1:
            for j in (1, 0):
                for zr in units(r - 1):
                    bx_last(j, zr)
        if r == 1:
            for j in (1, 0):
                for s in both:
                    bz(s, j, 4).start()
        if 2 <= r <= 4:
            bz_next(6 - r)
        if r <= 2:
            az_next(4 - r)
        if r == 0:
            for k in range(1, NZ):
                wexpect(0, k).wait_recv()
            acc = wgrad[pl.ds(pl.multiple_of(z * 16, 16), 16)]
            for k in range(1, NZ):
                acc += w1[k - 1]
            w2[plane] = acc
            for k in range(1, NY * NX):
                wcopy(1, k).start()
        if r == 2:
            for k in range(1, NY * NX):
                wexpect(1, k).wait_recv()
            acc = w2[0]
            for k in range(1, NY * NX):
                acc += w2[k]
            wout[pl.ds(pl.multiple_of(z * 16, 16), 16)] = acc
            for k in range(1, NZ):
                wcopy(2, k).start()
        if r == 3:
            def alast(k, _):
                j, xr = 1 - k // NX, lax.rem(k + 2, NX)
                for s in both:
                    az(s, j, xr, 1).wait_recv()
                total(raz, (j, xr), part.at[yof(j), z, xof(xr), PA])
                return 0

            lax.fori_loop(0, 2 * NX, alast, 0)
            for j in (1, 0):
                for s in both:
                    ax(s, j, 2).start()
        if r == 4:
            for j in (1, 0):
                for s in both:
                    ax(s, j, 2).wait_recv()
                    add(rax, (di(s), j, 1), raz.at[0, j, lax.rem(s + NX, NX), 0], True, s)
                    ax(s, j, 1).start()
        if r == 5:
            for j in (1, 0):
                for s in both:
                    bz(s, j, 1).wait_recv()
                    ax(s, j, 1).wait_recv()
                total(rbz, (j,), rbx.at[0, j, 0, 0])
                total(rax, (j,), raz.at[0, j, 0, 0])
                if j == 1:
                    aput = remote(rax.at[0, 1, 0], ry.at[PA], ys.at[0], yr.at[0], ydev)
                    bput = remote(rbz.at[0, 1, 0], ry.at[PB], ys.at[1], yr.at[1], ydev)
                    aput.start()
                    bput.start()
    aput.wait_recv()
    bput.wait_recv()
    out[PA] = rax[0, 0, 0].astype(F32) + ry[PA].astype(F32)
    out[PB] = rbz[0, 0, 0].astype(F32) + ry[PB].astype(F32)

    for k in range(1, NZ):
        wexpect(2, k).wait_recv()
    for j in range(2):
        def xunit(zr, _, j=j):
            for s in both:
                for d in (1, 2):
                    bx(s, j, zr, d).wait_send()
            return 0

        lax.fori_loop(0, NZ, xunit, 0)

        def zunit(xr, _, j=j):
            for s in both:
                for d in range(1, 5):
                    az(s, j, xr, d).wait_send()
            return 0

        lax.fori_loop(0, NX, zunit, 0)
        for s in both:
            for d in range(1, 5):
                bz(s, j, d).wait_send()
            for d in (1, 2):
                ax(s, j, d).wait_send()
    aput.wait_send()
    bput.wait_send()
    for phase in range(3):
        for k in range(1, 8):
            wcopy(phase, k).wait_send()


def scatter(part, wgrad):
    dma = pltpu.SemaphoreType.DMA
    return pl.pallas_call(
        scatter_kernel,
        out_shape=(
            jax.ShapeDtypeStruct((TPN, FC, TILE), F32),
            jax.ShapeDtypeStruct(wgrad.shape, F32),
        ),
        in_specs=[VMEM, VMEM],
        out_specs=(VMEM, VMEM),
        scratch_shapes=[
            pltpu.VMEM((2, 2, NZ, 2, TB, FC, TILE), BF),
            pltpu.VMEM((2, 2, 4, TB, FC, TILE), BF),
            pltpu.VMEM((2, 2, 2, TA, FC, TILE), BF),
            pltpu.VMEM((2, 2, NX, 4, TA, FC, TILE), BF),
            pltpu.VMEM((TPN, FC, TILE), BF),
            pltpu.VMEM((NZ - 1, 16, 256), F32),
            pltpu.VMEM((NY * NX, 16, 256), F32),
            dma((2, 2, 4)), dma((2, 2, 4)), dma((2, 2, NZ, 2)), dma((2, 2, NZ, 2)),
            dma((2, 2, 2)), dma((2, 2, 2)), dma((2, 2, NX, 4)), dma((2, 2, NX, 4)),
            dma((2,)), dma((2,)), dma((21,)), dma((21,)),
        ],
        compiler_params=pltpu.CompilerParams(
            collective_id=2, has_side_effects=True, vmem_limit_bytes=48 * 2**20
        ),
        name="scatter",
    )(part, wgrad)


def local(features, w_self, w_neigh, tile_rows, tile_cols, tile_count, edge_bits, cotangent):
    own = features.reshape(TPN, TILE // 8, 8, FC).transpose(0, 3, 2, 1).reshape(TPN, FC, TILE)
    wt = jnp.concatenate([w_self.T, w_neigh.T], axis=0)
    full, xfull, wfull = gather(own, features.T, wt)
    avg, deg = forward(tile_rows, tile_cols, tile_count, edge_bits, full.reshape(-1, FC, TILE))
    act, direct, scaled, wgrad = dense(avg, xfull, wfull, w_self, w_neigh, deg, cotangent.T)
    part = backward(tile_rows, tile_cols, tile_count, edge_bits, scaled)
    back, wsum = scatter(part.reshape(NY, NZ, NX, TPN, FC, TILE), wgrad)
    back = back.reshape(TPN, FC, 8, TILE // 8).transpose(0, 3, 2, 1).reshape(ROWS, FC)
    return act.T, direct.T + back, wsum[:FC], wsum[FC:]


def solution(mesh):
    placed = (
        P("node", "feat"),
        P("feat", None),
        P("feat", None),
        P("node"),
        P("node"),
        P("node"),
        P("node", None, None),
        P("node", "feat"),
    )
    return jax.shard_map(
        local,
        mesh=mesh,
        in_specs=placed,
        out_specs=(P("node", "feat"), P("node", "feat"), P("feat", None), P("feat", None)),
        check_vma=False,
    )
```

```python
import jax
import jax.numpy as jnp
from jax import lax
from jax.experimental import pallas as pl
from jax.experimental.pallas import tpu as pltpu
from jax.sharding import PartitionSpec as P

MESH = pl.DeviceIdType.MESH
BF = jnp.bfloat16
F32 = jnp.float32
NY, NZ, NX = 2, 8, 4
TPN = 8
FC = 64
TILE = 128
ROWS = TPN * TILE
SLOTS = 256
WORDS = 16
CNT = 8
BOTH = (1, -1)
UNROLL = 8
ANY = pl.BlockSpec(memory_space=pl.ANY)
VMEM = pl.BlockSpec(memory_space=pltpu.VMEM)
SMEM = pl.BlockSpec(memory_space=pltpu.SMEM)
OUT = pltpu.VMEM


def place():
    node, feat = lax.axis_index("node"), lax.axis_index("feat")
    return node // (NZ * NX), lax.rem(node // NX, NZ), lax.rem(node, NX), feat


def side(s):
    return 0 if s > 0 else 1


def node_of(y, z, x):
    return (y * NZ + z) * NX + x


def across(feat):
    return lax.rem(feat + 2, 4)


def sibling(feat):
    return feat + 1 - 2 * lax.rem(feat, 2)


def meet(peers):
    barrier = pltpu.get_barrier_semaphore()
    for peer in peers:
        pl.semaphore_signal(barrier, inc=1, device_id=peer, device_id_type=MESH)
    pl.semaphore_wait(barrier, len(peers))


def remote(src, dst, send, recv, peer):
    return pltpu.make_async_remote_copy(
        src_ref=src, dst_ref=dst, send_sem=send, recv_sem=recv, device_id=peer, device_id_type=MESH
    )


def exchange(mine, slot, feat, node, sems, send, recv):
    one, two = (node, across(feat)), (node, sibling(feat))
    far, near = across(feat), sibling(feat)
    diag = across(near)
    a = remote(mine, slot(feat), send.at[sems], recv.at[sems], one)
    b = remote(mine, slot(feat), send.at[sems + 1], recv.at[sems + 1], two)
    c = remote(slot(far), slot(far), send.at[sems + 2], recv.at[sems + 2], two)
    a.start()
    b.start()

    def step():
        remote(slot(far), slot(far), send.at[sems], recv.at[sems], one).wait_recv()
        c.start()

    def finish():
        remote(slot(near), slot(near), send.at[sems + 1], recv.at[sems + 1], two).wait_recv()
        remote(slot(diag), slot(diag), send.at[sems + 2], recv.at[sems + 2], two).wait_recv()
        a.wait_send()
        b.wait_send()
        c.wait_send()

    return step, finish


def dot(a, b):
    return jnp.dot(a, b, preferred_element_type=F32)


def nt(a, b):
    return lax.dot_general(a, b, (((1,), (1,)), ((), ())), preferred_element_type=F32)


def iota(shape, dim):
    return lax.broadcasted_iota(jnp.int32, shape, dim)


def order():
    old = iota((TILE, TILE), 1)
    new = jnp.bitwise_and(old, 7) * WORDS + lax.shift_right_logical(old, 3)
    return (iota((TILE, TILE), 0) == new).astype(F32).astype(BF)


def gather_kernel(feats, wself, wneigh, rows, cols, count, words, full, xfull, wfull, edges, listed,
                  raw, wt, codes, marks,
                  zs, zr, es, er, bs, br, cs, cr, ys, yr, fs, fr, ls):
    y, z, x, feat = place()
    node = node_of(y, z, x)
    oy = 1 - y

    def zof(k):
        return lax.rem(z + k + 2 * NZ, NZ)

    def xof(k):
        return lax.rem(x + k + 2 * NX, NX)

    def yof(j):
        return y + j - 2 * j * y

    def zdev(s):
        return (node_of(y, zof(s), x), feat)

    def xdev(s):
        return (node_of(y, z, xof(s)), feat)

    ydev = (node_of(oy, z, x), feat)
    beside = (node, sibling(feat))
    peers = [zdev(1), zdev(-1), xdev(1), xdev(-1), xdev(2), ydev, (node, across(feat)), beside]
    barrier = pltpu.get_barrier_semaphore()
    for peer in peers:
        pl.semaphore_signal(barrier, inc=1, device_id=peer, device_id_type=MESH)

    half = lax.rem(feat, 2) * (SLOTS // 2)
    other = SLOTS // 2 - half
    PART = SLOTS // 8

    def load(c):
        base = half + c * PART if c < 4 else other
        span = pl.ds(base, PART if c < 4 else SLOTS // 2)
        return pltpu.make_async_copy(words.at[span], raw.at[span], ls.at[c])

    for c in range(5):
        load(c).start()
    perm = order()
    for t in range(TPN):
        full[y, z, t] = dot(perm, feats[t * TILE:(t + 1) * TILE, :]).T.astype(BF)
    pl.semaphore_wait(barrier, len(peers))

    def chunk(ref, c):
        return ref.at[pl.ds(c * (TPN // 2), TPN // 2)]

    def yhop(c, arriving=False):
        at = chunk(full.at[oy if arriving else y, z], c)
        return remote(at, at, ys.at[c], yr.at[c], ydev)

    def zhop(s, j, c, d, arriving=False):
        i = (side(s), j, c, d - 1)
        at = chunk(full.at[yof(j), zof(-s * d if arriving else -s * (d - 1))], c)
        return remote(at, at, zs.at[i], zr.at[i], zdev(s))

    def ehop(s, c, d, arriving=False):
        i = (side(s), c, d - 1)
        at = edges.at[xof(-s * d if arriving else -s * (d - 1)), pl.ds(half + c * PART, PART)]
        return remote(at, at, es.at[i], er.at[i], xdev(s))

    def ehand(s, c, d, arriving=False):
        i = (side(s), c, d - 1)
        at = edges.at[xof(-s * d), pl.ds((other if arriving else half) + c * PART, PART)]
        return remote(at, at, bs.at[i], br.at[i], beside)

    def nth(s, i):
        return i if s > 0 else (i + 2) % 4

    def chop(k, arriving=False):
        at = marks.at[xof(-k) if arriving else x]
        return remote(codes if not arriving else at, at, cs.at[k - 1], cr.at[k - 1], xdev(k))

    for c in range(2):
        yhop(c).start()
        for s in BOTH:
            zhop(s, 0, c, 1).start()
    for i in range(4):
        load(i).wait()
        span = pl.ds(half + i * PART, PART)
        edges[x, span] = raw[span].astype(jnp.int16)
        if i == 1:
            for k in (0, 1):
                ehop(1, nth(1, k), 1).start()
    for k in range(4):
        ehop(-1, nth(-1, k), 1).start()
        if k > 1:
            ehop(1, nth(1, k), 1).start()
    limit = count[0]
    at = iota((2, TILE), 0) * TILE + iota((2, TILE), 1)
    codes[...] = jnp.full_like(codes, -1)
    codes[0:2] = jnp.where(at < limit, rows[...] * 65536 + cols[...], -1)
    marks[x] = codes[...]
    for k in range(1, NX):
        chop(k).start()
    for c in range(2):
        yhop(c, True).wait_recv()
        for s in BOTH:
            zhop(s, 1, c, 1).start()
    wt[0:256] = wself[...].astype(F32).T.astype(BF)
    wt[256:512] = wneigh[...].astype(F32).T.astype(BF)
    xstep, xfinish = exchange(full.at[y, z], lambda k: xfull.at[k], feat, node, 0, fs, fr)
    wstep, wfinish = exchange(wt, lambda k: wfull.at[k], feat, node, 3, fs, fr)
    xfull[feat] = full[y, z]
    wfull[feat] = wt[...]

    def zround(d):
        for j in range(2):
            for c in range(2):
                for s in BOTH:
                    if d < 4 or c == side(s):
                        zhop(s, j, c, d, True).wait_recv()
                        if d < 3 or (d == 3 and c == side(s)):
                            zhop(s, j, c, d + 1).start()

    def eround(i):
        for s in BOTH:
            c = nth(s, i)
            ehop(s, c, 1, True).wait_recv()
            if i < 2:
                ehop(s, c, 2).start()
            ehand(s, c, 1).start()

    zround(1)
    eround(0)
    load(4).wait()
    span = pl.ds(other, SLOTS // 2)
    edges[x, span] = raw[span].astype(jnp.int16)
    for k in range(1, NX):
        chop(k, True).wait_recv()
    xstep()
    wstep()
    eround(1)
    zround(2)
    code = jnp.concatenate([marks[b, 0:2] for b in range(NX)], axis=0)
    col = jnp.bitwise_and(code, 511)
    mine = jnp.where(
        jnp.logical_and(code >= 0, jnp.bitwise_and(lax.shift_right_logical(col, 3), 3) == x), 1.0, 0.0
    )
    slot = iota((8, TILE), 0) * TILE + iota((8, TILE), 1)
    row = lax.shift_right_logical(slot, 8) * TPN + jnp.bitwise_and(lax.shift_right_arithmetic(code, 16), 7)
    near = lax.shift_left(lax.shift_right_logical(col, 5), 3) + jnp.bitwise_and(col, 7)
    upto = jnp.where(iota((TILE, TILE), 0) <= iota((TILE, TILE), 1), 1.0, 0.0).astype(BF)
    prefix = dot(mine.astype(BF), upto)
    pos = jnp.where(mine > 0.0, prefix - 1.0, -1.0e6)
    base = jnp.zeros((1, 1), F32)
    shifted = []
    for r in range(8):
        shifted.append(pos[r:r + 1] + base)
        base = base + prefix[r:r + 1, TILE - 1:TILE]
    pos = jnp.concatenate(shifted + [jnp.zeros((TILE - 8, TILE), F32)], axis=0).T
    eround(2)
    wide = iota((TILE, 8 * TILE), 1).astype(F32)
    picked = jnp.zeros((8, 8 * TILE), F32)
    fields = (jnp.bitwise_and(slot, 255), lax.shift_right_logical(slot, 8), row, near)
    for r in range(8):
        hot = jnp.where(pos[:, r:r + 1] == wide, 1.0, 0.0).astype(BF)
        stack = jnp.concatenate([f[r:r + 1].astype(F32) for f in fields] + [jnp.zeros((4, TILE), F32)], axis=0)
        picked += dot(stack.astype(BF), hot)
    items = (picked[0:1] + 256.0 * picked[1:2] + 1024.0 * picked[2:3] + 32768.0 * picked[3:4]).astype(jnp.int32)
    for r in range(8):
        listed[r:r + 1] = items[:, r * TILE:(r + 1) * TILE]
    listed[8:16] = jnp.broadcast_to(base, (8, TILE)).astype(jnp.int32)
    eround(3)
    zround(3)
    for i in range(2):
        for s in BOTH:
            c = nth(s, i)
            ehop(s, c, 2, True).wait_recv()
            ehand(s, c, 2).start()
    zround(4)
    for s in BOTH:
        for i in range(4):
            c = nth(s, i)
            for d in (1, 2) if i < 2 else (1,):
                ehand(s, c, d, True).wait_recv()
                ehand(s, c, d).wait_send()
                ehop(s, c, d).wait_send()
        for j in range(2):
            for c in range(2):
                for d in range(1, 5 if c == side(s) else 4):
                    zhop(s, j, c, d).wait_send()
    for k in range(1, NX):
        chop(k).wait_send()
    xfinish()
    wfinish()
    for c in range(2):
        yhop(c).wait_send()


def gather(feats, wself, wneigh, rows, cols, count, words):
    dma = pltpu.SemaphoreType.DMA
    return pl.pallas_call(
        gather_kernel,
        out_shape=(
            OUT((NY, NZ, TPN, FC, TILE), BF),
            OUT((4, TPN, FC, TILE), BF),
            OUT((4, 512, FC), BF),
            OUT((NX, *words.shape), jnp.int16),
            jax.ShapeDtypeStruct((16, TILE), jnp.int32),
        ),
        in_specs=[VMEM] * 5 + [SMEM, ANY],
        out_specs=(VMEM,) * 5,
        scratch_shapes=[
            pltpu.VMEM(words.shape, jnp.int32), pltpu.VMEM((512, FC), BF),
            pltpu.VMEM((8, TILE), jnp.int32), pltpu.VMEM((NX, 8, TILE), jnp.int32),
            dma((2, 2, 2, 4)), dma((2, 2, 2, 4)), dma((2, 4, 2)), dma((2, 4, 2)), dma((2, 4, 2)), dma((2, 4, 2)),
            dma((3,)), dma((3,)), dma((2,)), dma((2,)), dma((6,)), dma((6,)), dma((5,)),
        ],
        compiler_params=pltpu.CompilerParams(
            collective_id=0, has_side_effects=True, vmem_limit_bytes=24 * 2**20
        ),
        name="gather",
    )(feats, wself, wneigh, rows, cols, count, words)


def planes_of(words):
    return jnp.concatenate(
        [jnp.bitwise_and(jnp.right_shift(words, b), 1).astype(F32) for b in range(8)], axis=0
    )


def entry(slots, group, u, count, edges):
    item = slots[lax.shift_right_logical(group, 4), jnp.bitwise_and(group, 15) * UNROLL + u]
    live = (group * UNROLL + u < count).astype(jnp.int32)
    words = edges[jnp.bitwise_and(lax.shift_right_logical(item, 8), 3), jnp.bitwise_and(item, 255)]
    planes = planes_of(words.astype(jnp.int32) * live)
    return jnp.bitwise_and(lax.shift_right_logical(item, 10), 31), lax.shift_right_logical(item, 15), planes


def forward_kernel(slots, edges, full, acc):
    acc[...] = jnp.zeros_like(acc)
    count = slots[8, 0]

    def group(g, _):
        for u in range(UNROLL):
            row, col, planes = entry(slots, g, u, count, edges)
            near, t = lax.shift_right_logical(col, 3), jnp.bitwise_and(col, 7)
            block, tile = lax.shift_right_logical(row, 3), jnp.bitwise_and(row, 7)
            source = full[lax.shift_right_logical(near, 3), jnp.bitwise_and(near, 7), t]
            acc[block, tile, 0:FC] += dot(source, planes.astype(BF))
            acc[block, tile, FC:FC + CNT] += jnp.sum(planes.reshape(TILE // CNT, CNT, TILE), axis=0)
        return 0

    lax.fori_loop(0, (count + UNROLL - 1) // UNROLL, group, 0)


def forward(slots, edges, full):
    return pl.pallas_call(
        forward_kernel,
        out_shape=OUT((NX, TPN, FC + CNT, TILE), F32),
        in_specs=[SMEM, VMEM, VMEM],
        out_specs=VMEM,
        compiler_params=pltpu.CompilerParams(vmem_limit_bytes=24 * 2**20),
        name="forward_sums",
    )(slots, edges, full)


def dense_kernel(part, xfull, wfull, wself, wneigh, cot, act, direct, scaled, wgrad,
                 rx, xn, av, gr, send, recv, rs, rr, ss, sr):
    y, z, x, feat = place()
    node = node_of(y, z, x)
    HALF = TPN // 2
    SPAN = ROWS // 2

    def xof(k):
        return lax.rem(x + k + 2 * NX, NX)

    def xdev(s):
        return (node_of(y, z, xof(s)), feat)

    meet([xdev(1), xdev(-1), (node, across(feat)), (node, sibling(feat))])

    def cut(s):
        return pl.ds(side(s) * HALF, HALF)

    def hop(s, step):
        i = (side(s), step)
        if step == 0:
            src, dst = part.at[xof(2 * s), cut(s)], rx.at[side(s), 1]
        elif step == 1:
            src, dst = part.at[xof(s), cut(-s)], rx.at[2 + side(s), 1]
        else:
            src, dst = rx.at[side(s), 1], rx.at[side(s), 0]
        return remote(src, dst, rs.at[i], rr.at[i], xdev(s))

    for step in range(2):
        for s in BOTH:
            hop(s, step).start()

    off = pl.multiple_of(feat * FC, FC)

    def cols_of(k, which):
        return wfull[k, pl.ds(which * 256 + off, FC), :]

    perm = order()
    for k in range(4):
        for t in range(TPN):
            xn[k, :, t * TILE:(t + 1) * TILE] = dot(xfull[k, t], perm).astype(BF)
    for s in BOTH:
        hop(s, 0).wait_recv()
        rx[side(s), 1] += part[xof(s), cut(s)]
        hop(s, 2).start()
    pre = dot(cols_of(0, 0), xn[0])
    for k in range(1, 4):
        pre += dot(cols_of(k, 0), xn[k])
    for s in BOTH:
        hop(s, 1).wait_recv()
        hop(s, 2).wait_recv()

    def share(ref, sems, c):
        return exchange(ref.at[feat, c], lambda k: ref.at[k, c], feat, node, sems, send, recv)

    degrees, first = [], []
    for r in range(TPN):
        near, far = (0, 1) if r < HALF else (1, 0)
        q = r % HALF
        total = part[x, r] + rx[near, 0, q] + rx[2 + far, 1, q]
        degree = jnp.maximum(jnp.sum(total[FC:], axis=0, keepdims=True), 1.0)
        degrees.append(degree)
        av[feat, r // HALF, :, q * TILE:(q + 1) * TILE] = (total[:FC] / degree).astype(BF)
        if q == HALF - 1:
            first.append(share(av, 3 * (r // HALF), r // HALF))
    for step, _ in first:
        step()
    second = []
    for c in range(2):
        first[c][1]()
        span = slice(c * SPAN, (c + 1) * SPAN)
        own = pre[:, span]
        for k in range(4):
            own += dot(cols_of(k, 1), av[k, c])
        sig = jax.nn.sigmoid(own)
        grad = cot[:, span] * sig * (1.0 + own * (1.0 - sig))
        gr[feat, c] = grad.astype(BF)
        second.append(share(gr, 6 + 3 * c, c))
        act[:, span] = own * sig
    for step, _ in second:
        step()

    def shop(s, c, d, arriving=False):
        i = (side(s), c, d - 1)
        at = scaled.at[xof(-s * d if arriving else -s * (d - 1)), pl.ds(c * HALF, HALF)]
        return remote(at, at, ss.at[i], sr.at[i], xdev(s))

    for c in range(2):
        second[c][1]()
        sums = dot(wneigh[:, 0:FC], gr[0, c])
        for k in range(1, 4):
            sums += dot(wneigh[:, k * FC:(k + 1) * FC], gr[k, c])
        for q in range(HALF):
            r = c * HALF + q
            scaled[x, r] = (sums[:, q * TILE:(q + 1) * TILE] / degrees[r]).astype(BF)
        for s in BOTH:
            shop(s, c, 1).start()
    for c in range(2):
        straight = dot(wself[:, 0:FC], gr[0, c])
        for k in range(1, 4):
            straight += dot(wself[:, k * FC:(k + 1) * FC], gr[k, c])
        direct[:, c * SPAN:(c + 1) * SPAN] = straight
    for c in range(2):
        for s in BOTH:
            shop(s, c, 1, True).wait_recv()
            if c == side(s):
                shop(s, c, 2).start()
    for k in range(4):
        lanes = slice(k * FC, (k + 1) * FC)
        wgrad[0:FC, lanes] = nt(xn[feat, :, 0:SPAN], gr[k, 0]) + nt(xn[feat, :, SPAN:ROWS], gr[k, 1])
        wgrad[FC:2 * FC, lanes] = nt(av[feat, 0], gr[k, 0]) + nt(av[feat, 1], gr[k, 1])
    for s in BOTH:
        shop(s, side(s), 2, True).wait_recv()
        shop(s, side(s), 2).wait_send()
        for c in range(2):
            shop(s, c, 1).wait_send()
        for step in range(3):
            hop(s, step).wait_send()


def dense(part, xfull, wfull, wself, wneigh, cot):
    dma = pltpu.SemaphoreType.DMA
    return pl.pallas_call(
        dense_kernel,
        out_shape=(
            jax.ShapeDtypeStruct((FC, ROWS), F32),
            jax.ShapeDtypeStruct((FC, ROWS), F32),
            OUT((NX, TPN, FC, TILE), BF),
            OUT((2 * FC, 4 * FC), F32),
        ),
        in_specs=[VMEM] * 6,
        out_specs=(VMEM,) * 4,
        scratch_shapes=[
            pltpu.VMEM((4, 2, TPN // 2, FC + CNT, TILE), F32), pltpu.VMEM((4, FC, ROWS), BF),
            pltpu.VMEM((4, 2, FC, ROWS // 2), BF), pltpu.VMEM((4, 2, FC, ROWS // 2), BF),
            dma((12,)), dma((12,)), dma((2, 3)), dma((2, 3)), dma((2, 2, 2)), dma((2, 2, 2)),
        ],
        compiler_params=pltpu.CompilerParams(
            collective_id=1, has_side_effects=True, vmem_limit_bytes=24 * 2**20
        ),
        name="dense",
    )(part, xfull, wfull, wself, wneigh, cot)


def backward_kernel(slots, edges, source, out, acc):
    acc[...] = jnp.zeros_like(acc)
    count = slots[8, 0]

    def group(g, _):
        for u in range(UNROLL):
            row, col, planes = entry(slots, g, u, count, edges)
            block, tile = lax.shift_right_logical(row, 3), jnp.bitwise_and(row, 7)
            acc[col] += nt(source[block, tile], planes.astype(BF))
        return 0

    lax.fori_loop(0, (count + UNROLL - 1) // UNROLL, group, 0)
    for y in range(NY):
        for z in range(NZ):
            base = (y * NZ + z) * TPN
            out[y, z] = acc[base:base + TPN].astype(BF)


def backward(slots, edges, source):
    return pl.pallas_call(
        backward_kernel,
        out_shape=OUT((NY, NZ, TPN, FC, TILE), BF),
        in_specs=[SMEM, VMEM, VMEM],
        out_specs=VMEM,
        scratch_shapes=[pltpu.VMEM((NY * NZ * TPN, FC, TILE), F32)],
        compiler_params=pltpu.CompilerParams(vmem_limit_bytes=24 * 2**20),
        name="backward_sums",
    )(slots, edges, source)


def scatter_kernel(part, wgrad, out, wout, rz, ry, w1, w2, zs, zr, ys, yr, ws, wr):
    y, z, x, feat = place()
    oy = 1 - y
    HALF = TPN // 2

    def zof(k):
        return lax.rem(z + k + 2 * NZ, NZ)

    def yof(j):
        return y + j - 2 * j * y

    def zdev(s):
        return (node_of(y, zof(s), x), feat)

    plane = y * NX + x

    def pdev(k):
        p = lax.rem(plane + k, NY * NX)
        return (node_of(p // NX, z, lax.rem(p, NX)), feat)

    meet([zdev(k) for k in range(1, NZ)] + [pdev(k) for k in range(1, NY * NX)])
    ydev = (node_of(oy, z, x), feat)

    def starts(s, c, d):
        return d == (4 if c == side(s) else 3)

    def hop(s, j, c, d):
        i = (side(s), j, c, d - 1)
        src = rz.at[side(s), j, c, min(d, 3)]
        if starts(s, c, d):
            src = part.at[yof(j), zof(s * d), pl.ds(c * HALF, HALF)]
        return remote(src, rz.at[i], zs.at[i], zr.at[i], zdev(s))

    def yhop(c):
        return remote(rz.at[0, 1, c, 0], ry.at[c], ys.at[c], yr.at[c], ydev)

    def wcopy(phase, k):
        i = phase * 7 + k - 1
        if phase == 0:
            return remote(wgrad.at[pl.ds(pl.multiple_of(zof(k) * 16, 16), 16)], w1.at[k - 1], ws.at[i], wr.at[i], zdev(k))
        if phase == 1:
            return remote(w2.at[plane], w2.at[plane], ws.at[i], wr.at[i], pdev(k))
        rows = pl.ds(pl.multiple_of(z * 16, 16), 16)
        return remote(wout.at[rows], wout.at[rows], ws.at[i], wr.at[i], zdev(k))

    def wexpect(phase, k):
        i = phase * 7 + k - 1
        if phase == 0:
            dst = w1.at[k - 1]
        elif phase == 1:
            dst = w2.at[lax.rem(plane + NY * NX - k, NY * NX)]
        else:
            dst = wout.at[pl.ds(pl.multiple_of(zof(-k) * 16, 16), 16)]
        return remote(dst, dst, ws.at[i], wr.at[i], zdev(k))

    for j in (1, 0):
        for s in BOTH:
            hop(s, j, side(s), 4).start()
    for k in range(1, NZ):
        wcopy(0, k).start()
    for j in (1, 0):
        for s in BOTH:
            hop(s, j, 1 - side(s), 3).start()
    for d in (4, 3, 2):
        for j in (1, 0):
            for c in range(2):
                for s in BOTH:
                    if d == 4 and c != side(s):
                        continue
                    hop(s, j, c, d).wait_recv()
                    i = (side(s), j, c, d - 1)
                    term = part[yof(j), zof(s * (d - 1)), c * HALF:(c + 1) * HALF]
                    rz[i] = (rz[i].astype(F32) + term.astype(F32)).astype(BF)
                    hop(s, j, c, d - 1).start()
        if d == 4:
            for k in range(1, NZ):
                wexpect(0, k).wait_recv()
            acc = wgrad[pl.ds(pl.multiple_of(z * 16, 16), 16)]
            for k in range(1, NZ):
                acc += w1[k - 1]
            w2[plane] = acc
            for k in range(1, NY * NX):
                wcopy(1, k).start()
        if d == 3:
            for k in range(1, NY * NX):
                wexpect(1, k).wait_recv()
            acc = w2[0]
            for k in range(1, NY * NX):
                acc += w2[k]
            wout[pl.ds(pl.multiple_of(z * 16, 16), 16)] = acc
            for k in range(1, NZ):
                wcopy(2, k).start()

    def total(j, c):
        for s in BOTH:
            hop(s, j, c, 1).wait_recv()
        mine = part[yof(j), z, c * HALF:(c + 1) * HALF].astype(F32)
        return mine + rz[0, j, c, 0].astype(F32) + rz[1, j, c, 0].astype(F32)

    for c in range(2):
        rz[0, 1, c, 0] = total(1, c).astype(BF)
        yhop(c).start()
    for c in range(2):
        mine = total(0, c)
        yhop(c).wait_recv()
        out[c * HALF:(c + 1) * HALF] = mine + ry[c].astype(F32)
    for k in range(1, NZ):
        wexpect(2, k).wait_recv()
    for s in BOTH:
        for j in range(2):
            for c in range(2):
                for d in range(1, 5 if c == side(s) else 4):
                    hop(s, j, c, d).wait_send()
    for c in range(2):
        yhop(c).wait_send()
    for phase in range(3):
        for k in range(1, 8):
            wcopy(phase, k).wait_send()


def scatter(part, wgrad):
    dma = pltpu.SemaphoreType.DMA
    return pl.pallas_call(
        scatter_kernel,
        out_shape=(
            jax.ShapeDtypeStruct((TPN, FC, TILE), F32),
            jax.ShapeDtypeStruct((2 * FC, 4 * FC), F32),
        ),
        in_specs=[VMEM, VMEM],
        out_specs=(VMEM, VMEM),
        scratch_shapes=[
            pltpu.VMEM((2, 2, 2, 4, TPN // 2, FC, TILE), BF),
            pltpu.VMEM((2, TPN // 2, FC, TILE), BF),
            pltpu.VMEM((NZ - 1, 16, 256), F32),
            pltpu.VMEM((NY * NX, 16, 256), F32),
            dma((2, 2, 2, 4)), dma((2, 2, 2, 4)), dma((2,)), dma((2,)), dma((21,)), dma((21,)),
        ],
        compiler_params=pltpu.CompilerParams(
            collective_id=2, has_side_effects=True, vmem_limit_bytes=24 * 2**20
        ),
        name="scatter",
    )(part, wgrad)


def local(features, w_self, w_neigh, tile_rows, tile_cols, tile_count, edge_bits, cotangent):
    rows, cols = tile_rows.reshape(2, TILE), tile_cols.reshape(2, TILE)
    full, xfull, wfull, edges, slots = gather(features, w_self, w_neigh, rows, cols, tile_count, edge_bits)
    part = forward(slots, edges, full)
    act, direct, scaled, wgrad = dense(part, xfull, wfull, w_self, w_neigh, cotangent.T)
    part = backward(slots, edges, scaled)
    back, wsum = scatter(part, wgrad)
    back = back.reshape(TPN, FC, 8, TILE // 8).transpose(0, 3, 2, 1).reshape(ROWS, FC)
    return act.T, direct.T + back, wsum[:FC], wsum[FC:]


def solution(mesh):
    placed = (
        P("node", "feat"),
        P("feat", None),
        P("feat", None),
        P("node"),
        P("node"),
        P("node"),
        P("node", None, None),
        P("node", "feat"),
    )
    return jax.shard_map(
        local,
        mesh=mesh,
        in_specs=placed,
        out_specs=(P("node", "feat"), P("node", "feat"), P("feat", None), P("feat", None)),
        check_vma=False,
    )
```

```python
import jax
import jax.numpy as jnp
from jax import lax
from jax.experimental import pallas as pl
from jax.experimental.pallas import tpu as pltpu
from jax.sharding import PartitionSpec as P

MESH = pl.DeviceIdType.MESH
BF = jnp.bfloat16
F32 = jnp.float32
NY, NZ, NX = 2, 8, 4
TPN = 8
FC = 64
TILE = 128
ROWS = TPN * TILE
SLOTS = 256
WORDS = 16
CNT = 16
BOTH = (1, -1)
UNROLL = 8
HBM = pl.BlockSpec(memory_space=pltpu.HBM)
VMEM = pl.BlockSpec(memory_space=pltpu.VMEM)
SMEM = pl.BlockSpec(memory_space=pltpu.SMEM)
OUT = pltpu.VMEM


def place():
    node, feat = lax.axis_index("node"), lax.axis_index("feat")
    return node // (NZ * NX), lax.rem(node // NX, NZ), lax.rem(node, NX), feat


def side(s):
    return 0 if s > 0 else 1


def node_of(y, z, x):
    return (y * NZ + z) * NX + x


def across(feat):
    return lax.rem(feat + 2, 4)


def sibling(feat):
    return feat + 1 - 2 * lax.rem(feat, 2)


def meet(peers):
    barrier = pltpu.get_barrier_semaphore()
    for peer in peers:
        pl.semaphore_signal(barrier, inc=1, device_id=peer, device_id_type=MESH)
    pl.semaphore_wait(barrier, len(peers))


def remote(src, dst, send, recv, peer):
    return pltpu.make_async_remote_copy(
        src_ref=src, dst_ref=dst, send_sem=send, recv_sem=recv, device_id=peer, device_id_type=MESH
    )


def exchange(mine, slot, feat, node, sems, send, recv):
    one, two = (node, across(feat)), (node, sibling(feat))
    far, near = across(feat), sibling(feat)
    diag = across(near)
    a = remote(mine, slot(feat), send.at[sems], recv.at[sems], one)
    b = remote(mine, slot(feat), send.at[sems + 1], recv.at[sems + 1], two)
    c = remote(slot(far), slot(far), send.at[sems + 2], recv.at[sems + 2], two)
    a.start()
    b.start()

    def step():
        remote(slot(far), slot(far), send.at[sems], recv.at[sems], one).wait_recv()
        c.start()

    def finish():
        remote(slot(near), slot(near), send.at[sems + 1], recv.at[sems + 1], two).wait_recv()
        remote(slot(diag), slot(diag), send.at[sems + 2], recv.at[sems + 2], two).wait_recv()
        a.wait_send()
        b.wait_send()
        c.wait_send()

    return step, finish


def dot(a, b):
    return jnp.dot(a, b, preferred_element_type=F32)


def nt(a, b):
    return lax.dot_general(a, b, (((1,), (1,)), ((), ())), preferred_element_type=F32)


def iota(shape, dim):
    return lax.broadcasted_iota(jnp.int32, shape, dim)


def order():
    old = iota((TILE, TILE), 1)
    new = jnp.bitwise_and(old, 7) * WORDS + lax.shift_right_logical(old, 3)
    return (iota((TILE, TILE), 0) == new).astype(F32).astype(BF)


ORDER = (
    "s0", "s1", "s2", "s3", "z21", "y", "z01", "e0", "z11", "e1", "z22", "z02", "c",
    "l0", "l1", "l2", "e2", "z12", "l3", "l4", "x", "z23", "e3", "l5", "z03", "h0",
    "l6", "z13", "l7", "i", "z24", "h1", "z04", "z14",
)


def gather_kernel(feats, wself, wneigh, rows, cols, count, words, full, xfull, wfull, edges, listed,
                  raw, ids, codes, marks,
                  zs, zr, es, er, bs, br, cs, cr, ys, yr, fs, fr, ls):
    y, z, x, feat = place()
    node = node_of(y, z, x)
    oy = 1 - y
    HALF = TPN // 2

    def zof(k):
        return lax.rem(z + k + 2 * NZ, NZ)

    def xof(k):
        return lax.rem(x + k + 2 * NX, NX)

    def zdev(s):
        return (node_of(y, zof(s), x), feat)

    def xdev(s):
        return (node_of(y, z, xof(s)), feat)

    ydev = (node_of(oy, z, x), feat)
    beside = (node, sibling(feat))
    peers = [zdev(1), zdev(-1), xdev(1), xdev(-1), xdev(2), ydev, (node, across(feat)), beside]
    barrier = pltpu.get_barrier_semaphore()
    for peer in peers:
        pl.semaphore_signal(barrier, inc=1, device_id=peer, device_id_type=MESH)

    half = lax.rem(feat, 2) * (SLOTS // 2)
    other = SLOTS // 2 - half
    PART = SLOTS // 8

    def load(c):
        base = half + c * PART if c < 4 else other
        span = pl.ds(base, PART if c < 4 else SLOTS // 2)
        return pltpu.make_async_copy(words.at[span], raw.at[span], ls.at[c])

    small = [
        pltpu.make_async_copy(a, b, ls.at[5 + i])
        for i, (a, b) in enumerate((
            (feats, xfull.at[feat]), (wself, wfull.at[feat, 0]), (wneigh, wfull.at[feat, 1]),
            (rows, ids.at[0]), (cols, ids.at[1]),
        ))
    ]
    small[0].start()
    for c in range(5):
        load(c).start()
    for copy in small[1:]:
        copy.start()
    perm = order()
    small[0].wait()
    for t in range(TPN):
        full[y, z, t] = nt(xfull[feat, :, t * TILE:(t + 1) * TILE], perm).astype(BF)
    for i in range(4):
        load(i).wait()
        span = pl.ds(half + i * PART, PART)
        edges[x, span] = raw[span].astype(jnp.int16)
    for copy in small[3:]:
        copy.wait()
    at = iota((2, TILE), 0) * TILE + iota((2, TILE), 1)
    codes[...] = jnp.full_like(codes, -1)
    codes[0:2] = jnp.where(at < count[0], ids[0] * 65536 + ids[1], -1)
    marks[x] = codes[...]
    pl.semaphore_wait(barrier, len(peers))

    def block(u, zr, d, s):
        base = (0, 0, HALF)[u] + (side(s) * (HALF // 2) if d == 4 else 0)
        return full.at[oy if u == 1 else y, zof(zr), pl.ds(base, HALF // 2 if d == 4 else HALF)]

    def zhop(s, u, d, arriving=False):
        i = (side(s), u, d - 1)
        at = block(u, -s * d if arriving else -s * (d - 1), d, s)
        return remote(at, at, zs.at[i], zr.at[i], zdev(s))

    def yhop(s, d, arriving=False):
        i = d if d < 1 else 1 + side(s) * 4 + d - 1
        i = 9 if d < 0 else i
        who = oy if arriving else y
        base = 0 if d < 0 else HALF
        base = base + (side(s) * (HALF // 2) if d == 4 else 0)
        at = full.at[who, zof(-s * max(d, 0)), pl.ds(base, HALF // 2 if d == 4 else HALF)]
        return remote(at, at, ys.at[i], yr.at[i], ydev)

    def ehop(s, c, d, arriving=False):
        i = (side(s), c, d - 1)
        at = edges.at[xof(-s * d if arriving else -s * (d - 1)), pl.ds(half + c * PART, PART)]
        return remote(at, at, es.at[i], er.at[i], xdev(s))

    def ehand(s, c, d, arriving=False):
        i = (side(s), c, d - 1)
        at = edges.at[xof(-s * d), pl.ds((other if arriving else half) + c * PART, PART)]
        return remote(at, at, bs.at[i], br.at[i], beside)

    def nth(s, i):
        return i if s > 0 else (i + 2) % 4

    def chop(k, arriving=False):
        at = marks.at[xof(-k) if arriving else x]
        return remote(codes if not arriving else at, at, cs.at[k - 1], cr.at[k - 1], xdev(k))

    yhop(1, -1).start()
    for s in BOTH:
        zhop(s, 2, 1).start()
        zhop(s, 0, 1).start()
    for k in range(1, NX):
        chop(k).start()
    yhop(1, 0).start()
    xstep, xfinish = exchange(feats, lambda k: xfull.at[k], feat, node, 0, fs, fr)
    wstep, wfinish = exchange(wself, lambda k: wfull.at[k, 0], feat, node, 3, fs, fr)
    vstep, vfinish = exchange(wneigh, lambda k: wfull.at[k, 1], feat, node, 6, fs, fr)
    small[1].wait()
    small[2].wait()

    def zpass(u, d):
        for s in BOTH:
            zhop(s, u, d, True).wait_recv()
            if d < 4:
                zhop(s, u, d + 1).start()
            if u == 2:
                yhop(s, d).start()

    def eround(i):
        for s in BOTH:
            c = nth(s, i)
            ehop(s, c, 1, True).wait_recv()
            if i < 2:
                ehop(s, c, 2).start()
            ehand(s, c, 1).start()

    def efar(i):
        for s in BOTH:
            c = nth(s, i)
            ehop(s, c, 2, True).wait_recv()
            ehand(s, c, 2).start()

    def efirst(i):
        for s in BOTH:
            ehop(s, nth(s, i), 1).start()

    def ycross():
        yhop(1, -1, True).wait_recv()
        for s in BOTH:
            zhop(s, 1, 1).start()

    def passon():
        for step in (xstep, wstep, vstep):
            step()

    state = {}

    def prepare():
        load(4).wait()
        span = pl.ds(other, SLOTS // 2)
        edges[x, span] = raw[span].astype(jnp.int16)
        for k in range(1, NX):
            chop(k, True).wait_recv()
        code = jnp.concatenate([marks[b, 0:2] for b in range(NX)], axis=0)
        col = jnp.bitwise_and(code, 511)
        mine = jnp.where(
            jnp.logical_and(code >= 0, jnp.bitwise_and(lax.shift_right_logical(col, 3), 3) == x), 1.0, 0.0
        )
        slot = iota((8, TILE), 0) * TILE + iota((8, TILE), 1)
        row = lax.shift_right_logical(slot, 8) * TPN + jnp.bitwise_and(lax.shift_right_arithmetic(code, 16), 7)
        near = lax.shift_left(lax.shift_right_logical(col, 5), 3) + jnp.bitwise_and(col, 7)
        upto = jnp.where(iota((TILE, TILE), 0) <= iota((TILE, TILE), 1), 1.0, 0.0).astype(BF)
        prefix = dot(mine.astype(BF), upto)
        pos = jnp.where(mine > 0.0, prefix - 1.0, -1.0e6)
        base = jnp.zeros((1, 1), F32)
        shifted = []
        for r in range(8):
            shifted.append(pos[r:r + 1] + base)
            base = base + prefix[r:r + 1, TILE - 1:TILE]
        pos = jnp.concatenate(shifted + [jnp.zeros((TILE - 8, TILE), F32)], axis=0).T
        wide = iota((TILE, 8 * TILE), 1).astype(F32)
        picked = jnp.zeros((8, 8 * TILE), F32)
        fields = (jnp.bitwise_and(slot, 255), lax.shift_right_logical(slot, 8), row, near)
        state.update(pos=pos, base=base, wide=wide, picked=picked, fields=fields)

    def pick(r):
        pos, wide, fields = state["pos"], state["wide"], state["fields"]
        hot = jnp.where(pos[:, r:r + 1] == wide, 1.0, 0.0).astype(BF)
        stack = jnp.concatenate([f[r:r + 1].astype(F32) for f in fields] + [jnp.zeros((4, TILE), F32)], axis=0)
        state["picked"] += dot(stack.astype(BF), hot)

    def enlist():
        picked, base = state["picked"], state["base"]
        items = (picked[0:1] + 256.0 * picked[1:2] + 1024.0 * picked[2:3] + 32768.0 * picked[3:4]).astype(jnp.int32)
        for r in range(8):
            listed[r:r + 1] = items[:, r * TILE:(r + 1) * TILE]
        listed[8:16] = jnp.broadcast_to(base, (8, TILE)).astype(jnp.int32)

    steps = {"z": zpass, "e": eround, "h": efar, "s": efirst, "y": ycross, "x": passon, "c": prepare, "l": pick, "i": enlist}
    for step in ORDER:
        steps[step[0]](*(int(digit) for digit in step[1:]))
    for s in BOTH:
        for i in range(4):
            c = nth(s, i)
            for d in (1, 2) if i < 2 else (1,):
                ehand(s, c, d, True).wait_recv()
                ehand(s, c, d).wait_send()
                ehop(s, c, d).wait_send()
        for d in range(1, 5):
            for u in range(3):
                zhop(s, u, d).wait_send()
            yhop(s, d, True).wait_recv()
            yhop(s, d).wait_send()
    yhop(1, 0, True).wait_recv()
    yhop(1, 0).wait_send()
    yhop(1, -1).wait_send()
    for k in range(1, NX):
        chop(k).wait_send()
    xfinish()
    wfinish()
    vfinish()


def gather(feats, wself, wneigh, rows, cols, count, words):
    dma = pltpu.SemaphoreType.DMA
    return pl.pallas_call(
        gather_kernel,
        out_shape=(
            OUT((NY, NZ, TPN, FC, TILE), BF),
            OUT((4, FC, ROWS), BF),
            OUT((4, 2, FC, 4 * FC), BF),
            OUT((NX, *words.shape), jnp.int16),
            jax.ShapeDtypeStruct((16, TILE), jnp.int32),
        ),
        in_specs=[HBM] * 5 + [SMEM, HBM],
        out_specs=(VMEM,) * 5,
        scratch_shapes=[
            pltpu.VMEM(words.shape, jnp.int32), pltpu.VMEM((2, 2, TILE), jnp.int32),
            pltpu.VMEM((8, TILE), jnp.int32), pltpu.VMEM((NX, 8, TILE), jnp.int32),
            dma((2, 3, 4)), dma((2, 3, 4)), dma((2, 4, 2)), dma((2, 4, 2)), dma((2, 4, 2)), dma((2, 4, 2)),
            dma((3,)), dma((3,)), dma((10,)), dma((10,)), dma((9,)), dma((9,)), dma((10,)),
        ],
        compiler_params=pltpu.CompilerParams(
            collective_id=0, has_side_effects=True, vmem_limit_bytes=24 * 2**20
        ),
        name="gather",
    )(feats, wself, wneigh, rows, cols, count, words)


def planes_of(words):
    one, zero = jnp.ones(words.shape, BF), jnp.zeros(words.shape, BF)
    return jnp.concatenate(
        [jnp.where(jnp.bitwise_and(words, jnp.int16(1 << b)) != 0, one, zero) for b in range(8)], axis=0
    )


def entry(slots, group, u, count, edges):
    item = slots[lax.shift_right_logical(group, 4), jnp.bitwise_and(group, 15) * UNROLL + u]
    words = edges[jnp.bitwise_and(lax.shift_right_logical(item, 8), 3), jnp.bitwise_and(item, 255)]
    planes = planes_of(jnp.where(group * UNROLL + u < count, words, jnp.zeros_like(words)))
    return jnp.bitwise_and(lax.shift_right_logical(item, 10), 31), lax.shift_right_logical(item, 15), planes


def forward_kernel(slots, edges, full, acc):
    acc[...] = jnp.zeros_like(acc)
    count = slots[8, 0]
    ones = jnp.ones((CNT, TILE), BF)

    def group(g, _):
        for u in range(UNROLL):
            row, col, planes = entry(slots, g, u, count, edges)
            near, t = lax.shift_right_logical(col, 3), jnp.bitwise_and(col, 7)
            block, tile = lax.shift_right_logical(row, 3), jnp.bitwise_and(row, 7)
            source = full[lax.shift_right_logical(near, 3), jnp.bitwise_and(near, 7), t]
            acc[block, tile] += dot(jnp.concatenate([source, ones], axis=0), planes)
        return 0

    lax.fori_loop(0, (count + UNROLL - 1) // UNROLL, group, 0)


def forward(slots, edges, full):
    return pl.pallas_call(
        forward_kernel,
        out_shape=OUT((NX, TPN, FC + CNT, TILE), F32),
        in_specs=[SMEM, VMEM, VMEM],
        out_specs=VMEM,
        compiler_params=pltpu.CompilerParams(vmem_limit_bytes=24 * 2**20),
        name="forward_sums",
    )(slots, edges, full)


def dense_kernel(part, xfull, wfull, wself, wneigh, cot, act, direct, scaled, wgrad,
                 pq, pm, rq, rm, av, gr, send, recv, rs, rr, ss, sr):
    y, z, x, feat = place()
    node = node_of(y, z, x)
    HALF = TPN // 2
    SPAN = ROWS // 2

    def xof(k):
        return lax.rem(x + k + 2 * NX, NX)

    def xdev(s):
        return (node_of(y, z, xof(s)), feat)

    peers = [xdev(1), xdev(-1), xdev(2), (node, across(feat)), (node, sibling(feat))]
    barrier = pltpu.get_barrier_semaphore()
    for peer in peers:
        pl.semaphore_signal(barrier, inc=1, device_id=peer, device_id_type=MESH)

    def pack(c, k):
        block = xof(k)
        for q in range(HALF):
            r = c * HALF + q
            sums = part[block, r, 0:FC]
            most = jnp.maximum(jnp.max(jnp.abs(sums), axis=0, keepdims=True), 1e-30)
            pq[c, k - 1, q] = jnp.round(sums * (32766.0 / most)).astype(jnp.int32).astype(jnp.int16)
            pm[c, k - 1, q:q + 1] = most * (1.0 / 32766.0)
            pm[c, k - 1, HALF + q:HALF + q + 1] = part[block, r, FC:FC + 1]

    def hop(c, k, what):
        i = (c, k - 1, what)
        src, dst = ((pq, rq), (pm, rm))[what]
        return remote(src.at[c, k - 1], dst.at[c, k - 1], rs.at[i], rr.at[i], xdev(k))

    ORDER = (2, 1, 3)
    for k in ORDER:
        pack(0, k)
    pl.semaphore_wait(barrier, len(peers))
    for c in range(2):
        for k in ORDER:
            if c == 1:
                pack(1, k)
            hop(c, k, 1).start()
            hop(c, k, 0).start()

    choose = (iota((FC, 4 * FC), 1) == iota((FC, 4 * FC), 0) + feat * FC).astype(F32).astype(BF)

    def cols_of(k, which):
        return nt(choose, wfull[k, which]).astype(BF)

    pre = dot(cols_of(0, 0), xfull[0])
    for k in range(1, 4):
        pre += dot(cols_of(k, 0), xfull[k])
    neigh = [cols_of(k, 1) for k in range(4)]

    def share(ref, sems, c):
        return exchange(ref.at[feat, c], lambda k: ref.at[k, c], feat, node, sems, send, recv)

    degrees, first = [], []
    for c in range(2):
        for k in ORDER:
            for what in (1, 0):
                hop(c, k, what).wait_recv()
        for q in range(HALF):
            r = c * HALF + q
            total = part[x, r, 0:FC]
            degree = part[x, r, FC:FC + 1]
            for k in range(3):
                total += rq[c, k, q].astype(jnp.int32).astype(F32) * rm[c, k, q:q + 1]
                degree += rm[c, k, HALF + q:HALF + q + 1]
            degree = jnp.maximum(degree, 1.0)
            degrees.append(degree)
            av[feat, c, :, q * TILE:(q + 1) * TILE] = (total / degree).astype(BF)
        first.append(share(av, 3 * c, c))
    for step, _ in first:
        step()
    second = []
    for c in range(2):
        first[c][1]()
        span = slice(c * SPAN, (c + 1) * SPAN)
        own = pre[:, span]
        for k in range(4):
            own += dot(neigh[k], av[k, c])
        sig = jax.nn.sigmoid(own)
        grad = cot[:, span] * sig * (1.0 + own * (1.0 - sig))
        gr[feat, c] = grad.astype(BF)
        second.append(share(gr, 6 + 3 * c, c))
        act[:, span] = own * sig
    for step, _ in second:
        step()

    def shop(s, c, d, arriving=False):
        i = (side(s), c, d - 1)
        at = scaled.at[xof(-s * d if arriving else -s * (d - 1)), pl.ds(c * HALF, HALF)]
        return remote(at, at, ss.at[i], sr.at[i], xdev(s))

    for c in range(2):
        second[c][1]()
        sums = dot(wneigh[:, 0:FC], gr[0, c])
        for k in range(1, 4):
            sums += dot(wneigh[:, k * FC:(k + 1) * FC], gr[k, c])
        for q in range(HALF):
            r = c * HALF + q
            scaled[x, r] = (sums[:, q * TILE:(q + 1) * TILE] / degrees[r]).astype(BF)
        for s in BOTH:
            shop(s, c, 1).start()
    for c in range(2):
        straight = dot(wself[:, 0:FC], gr[0, c])
        for k in range(1, 4):
            straight += dot(wself[:, k * FC:(k + 1) * FC], gr[k, c])
        direct[:, c * SPAN:(c + 1) * SPAN] = straight
    for c in range(2):
        for s in BOTH:
            shop(s, c, 1, True).wait_recv()
            if c == side(s):
                shop(s, c, 2).start()
    for k in range(4):
        lanes = slice(k * FC, (k + 1) * FC)
        wgrad[0:FC, lanes] = nt(xfull[feat, :, 0:SPAN], gr[k, 0]) + nt(xfull[feat, :, SPAN:ROWS], gr[k, 1])
        wgrad[FC:2 * FC, lanes] = nt(av[feat, 0], gr[k, 0]) + nt(av[feat, 1], gr[k, 1])
    for s in BOTH:
        shop(s, side(s), 2, True).wait_recv()
        shop(s, side(s), 2).wait_send()
        for c in range(2):
            shop(s, c, 1).wait_send()
    for c in range(2):
        for k in ORDER:
            for what in range(2):
                hop(c, k, what).wait_send()


def dense(part, xfull, wfull, wself, wneigh, cot):
    dma = pltpu.SemaphoreType.DMA
    return pl.pallas_call(
        dense_kernel,
        out_shape=(
            jax.ShapeDtypeStruct((FC, ROWS), F32),
            OUT((FC, ROWS), F32),
            OUT((NX, TPN, FC, TILE), BF),
            OUT((2 * FC, 4 * FC), F32),
        ),
        in_specs=[VMEM] * 6,
        out_specs=(VMEM,) * 4,
        scratch_shapes=[
            pltpu.VMEM((2, 3, TPN // 2, FC, TILE), jnp.int16), pltpu.VMEM((2, 3, 8, TILE), F32),
            pltpu.VMEM((2, 3, TPN // 2, FC, TILE), jnp.int16), pltpu.VMEM((2, 3, 8, TILE), F32),
            pltpu.VMEM((4, 2, FC, ROWS // 2), BF), pltpu.VMEM((4, 2, FC, ROWS // 2), BF),
            dma((12,)), dma((12,)), dma((2, 3, 2)), dma((2, 3, 2)), dma((2, 2, 2)), dma((2, 2, 2)),
        ],
        compiler_params=pltpu.CompilerParams(
            collective_id=1, has_side_effects=True, vmem_limit_bytes=24 * 2**20
        ),
        name="dense",
    )(part, xfull, wfull, wself, wneigh, cot)


def backward_kernel(slots, edges, source, act, out, acted, acc):
    acted[...] = act[...]
    acc[...] = jnp.zeros_like(acc)
    count = slots[8, 0]

    def group(g, _):
        for u in range(UNROLL):
            row, col, planes = entry(slots, g, u, count, edges)
            block, tile = lax.shift_right_logical(row, 3), jnp.bitwise_and(row, 7)
            acc[col] += nt(source[block, tile], planes)
        return 0

    lax.fori_loop(0, (count + UNROLL - 1) // UNROLL, group, 0)
    for y in range(NY):
        for z in range(NZ):
            base = (y * NZ + z) * TPN
            out[y, z] = acc[base:base + TPN].astype(BF)


def backward(slots, edges, source, act):
    return pl.pallas_call(
        backward_kernel,
        out_shape=(OUT((NY, NZ, TPN, FC, TILE), BF), jax.ShapeDtypeStruct((FC, ROWS), F32)),
        in_specs=[SMEM, VMEM, VMEM, VMEM],
        out_specs=(VMEM, VMEM),
        scratch_shapes=[pltpu.VMEM((NY * NZ * TPN, FC, TILE), F32)],
        compiler_params=pltpu.CompilerParams(vmem_limit_bytes=24 * 2**20),
        name="backward_sums",
    )(slots, edges, source, act)


def scatter_kernel(part, wgrad, direct, out, wout, rz, ry, rl, w1, w2, zs, zr, ys, yr, ws, wr):
    y, z, x, feat = place()
    oy = 1 - y
    HALF = TPN // 2
    CUT = HALF // 2

    def zof(k):
        return lax.rem(z + k + 2 * NZ, NZ)

    def zdev(s):
        return (node_of(y, zof(s), x), feat)

    plane = y * NX + x

    def pdev(k):
        p = lax.rem(plane + k, NY * NX)
        return (node_of(p // NX, z, lax.rem(p, NX)), feat)

    meet([zdev(k) for k in range(1, NZ)] + [pdev(k) for k in range(1, NY * NX)])
    ydev = (node_of(oy, z, x), feat)

    def term(u, k):
        if u == 2:
            return ry.at[(k + NZ) % NZ]
        return part.at[oy if u == 1 else y, zof(k), pl.ds(0, HALF)]

    def hop(s, u, d):
        i = (side(s), u, d - 1)
        if d == 4:
            cut = pl.ds(side(s) * CUT, CUT)
            return remote(term(u, 4).at[cut], rz.at[i].at[cut], zs.at[i], zr.at[i], zdev(s))
        return remote(rz.at[side(s), u, d], rz.at[i], zs.at[i], zr.at[i], zdev(s))

    def yhop(k):
        return remote(part.at[oy, zof(k), pl.ds(HALF, HALF)], ry.at[(k + NZ) % NZ],
                      ys.at[(k + NZ) % NZ], yr.at[(k + NZ) % NZ], ydev)

    def join(k):
        yhop(k).wait_recv()
        at = (k + NZ) % NZ
        ry[at] = (ry[at].astype(F32) + part[y, zof(k), HALF:TPN].astype(F32)).astype(BF)

    last = remote(rz.at[0, 1, 0], rl, ys.at[NZ], yr.at[NZ], ydev)

    def wcopy(phase, k):
        i = phase * 7 + k - 1
        if phase == 0:
            return remote(wgrad.at[pl.ds(pl.multiple_of(zof(k) * 16, 16), 16)], w1.at[k - 1], ws.at[i], wr.at[i], zdev(k))
        if phase == 1:
            return remote(w2.at[plane], w2.at[plane], ws.at[i], wr.at[i], pdev(k))
        rows = pl.ds(pl.multiple_of(z * 16, 16), 16)
        return remote(wout.at[rows], wout.at[rows], ws.at[i], wr.at[i], zdev(k))

    def wexpect(phase, k):
        i = phase * 7 + k - 1
        if phase == 0:
            dst = w1.at[k - 1]
        elif phase == 1:
            dst = w2.at[lax.rem(plane + NY * NX - k, NY * NX)]
        else:
            dst = wout.at[pl.ds(pl.multiple_of(zof(-k) * 16, 16), 16)]
        return remote(dst, dst, ws.at[i], wr.at[i], zdev(k))

    for k in (4, 3, -3):
        yhop(k).start()
    for u in (1, 0):
        for s in BOTH:
            hop(s, u, 4).start()
    for k in (2, -2, 1, -1, 0):
        yhop(k).start()
    for k in range(1, NZ):
        wcopy(0, k).start()
    join(4)
    for s in BOTH:
        hop(s, 2, 4).start()
    for d in (4, 3, 2):
        for u in (1, 0, 2):
            if u == 2:
                join(d - 1)
                join(1 - d)
            for s in BOTH:
                hop(s, u, d).wait_recv()
                i = (side(s), u, d - 1)
                more = term(u, s * (d - 1))
                if d == 4:
                    a, b = pl.ds(side(s) * CUT, CUT), pl.ds((1 - side(s)) * CUT, CUT)
                    rz[(*i, a)] = (rz[(*i, a)].astype(F32) + more[a].astype(F32)).astype(BF)
                    rz[(*i, b)] = more[b]
                else:
                    rz[i] = (rz[i].astype(F32) + more[...].astype(F32)).astype(BF)
                hop(s, u, d - 1).start()
        if d == 4:
            for k in range(1, NZ):
                wexpect(0, k).wait_recv()
            acc = wgrad[pl.ds(pl.multiple_of(z * 16, 16), 16)]
            for k in range(1, NZ):
                acc += w1[k - 1]
            w2[plane] = acc
            for k in range(1, NY * NX):
                wcopy(1, k).start()
        if d == 3:
            for k in range(1, NY * NX):
                wexpect(1, k).wait_recv()
            acc = w2[0]
            for k in range(1, NY * NX):
                acc += w2[k]
            wout[pl.ds(pl.multiple_of(z * 16, 16), 16)] = acc
            for k in range(1, NZ):
                wcopy(2, k).start()

    def total(u):
        for s in BOTH:
            hop(s, u, 1).wait_recv()
        return term(u, 0)[...].astype(F32) + rz[0, u, 0].astype(F32) + rz[1, u, 0].astype(F32)

    perm = order().astype(F32)

    def finish(t, sums):
        back = jnp.dot(sums, perm, preferred_element_type=F32, precision=lax.Precision.HIGHEST)
        lanes = slice(t * TILE, (t + 1) * TILE)
        out[:, lanes] = direct[:, lanes] + back

    rz[0, 1, 0] = total(1).astype(BF)
    last.start()
    join(0)
    sums = total(2)
    for t in range(HALF):
        finish(HALF + t, sums[t])
    sums = total(0)
    last.wait_recv()
    sums += rl[...].astype(F32)
    for t in range(HALF):
        finish(t, sums[t])
    for k in range(1, NZ):
        wexpect(2, k).wait_recv()
    for s in BOTH:
        for u in range(3):
            for d in range(1, 5):
                hop(s, u, d).wait_send()
    for k in range(NZ):
        yhop(k).wait_send()
    last.wait_send()
    for phase in range(3):
        for k in range(1, 8):
            wcopy(phase, k).wait_send()


def scatter(part, wgrad, direct):
    dma = pltpu.SemaphoreType.DMA
    return pl.pallas_call(
        scatter_kernel,
        out_shape=(
            jax.ShapeDtypeStruct((FC, ROWS), F32),
            jax.ShapeDtypeStruct((2 * FC, 4 * FC), F32),
        ),
        in_specs=[VMEM, VMEM, VMEM],
        out_specs=(VMEM, VMEM),
        scratch_shapes=[
            pltpu.VMEM((2, 3, 4, TPN // 2, FC, TILE), BF),
            pltpu.VMEM((NZ, TPN // 2, FC, TILE), BF),
            pltpu.VMEM((TPN // 2, FC, TILE), BF),
            pltpu.VMEM((NZ - 1, 16, 256), F32),
            pltpu.VMEM((NY * NX, 16, 256), F32),
            dma((2, 3, 4)), dma((2, 3, 4)), dma((NZ + 1,)), dma((NZ + 1,)), dma((21,)), dma((21,)),
        ],
        compiler_params=pltpu.CompilerParams(
            collective_id=2, has_side_effects=True, vmem_limit_bytes=24 * 2**20
        ),
        name="scatter",
    )(part, wgrad, direct)


def local(features, w_self, w_neigh, tile_rows, tile_cols, tile_count, edge_bits, cotangent):
    rows, cols = tile_rows.reshape(2, TILE), tile_cols.reshape(2, TILE)
    given = [
        pltpu.with_memory_space_constraint(a, pltpu.HBM)
        for a in (features.T, w_self, w_neigh, rows, cols, edge_bits)
    ]
    full, xfull, wfull, edges, slots = gather(*given[:5], tile_count, given[5])
    part = forward(slots, edges, full)
    act, direct, scaled, wgrad = dense(part, xfull, wfull, w_self, w_neigh, cotangent.T)
    part, act = backward(slots, edges, scaled, act)
    grad, wsum = scatter(part, wgrad, direct)
    return act.T, grad.T, wsum[:FC], wsum[FC:]


def solution(mesh):
    placed = (
        P("node", "feat"),
        P("feat", None),
        P("feat", None),
        P("node"),
        P("node"),
        P("node"),
        P("node", None, None),
        P("node", "feat"),
    )
    return jax.shard_map(
        local,
        mesh=mesh,
        in_specs=placed,
        out_specs=(P("node", "feat"), P("node", "feat"), P("feat", None), P("feat", None)),
        check_vma=False,
    )
```

```python
import jax
import jax.numpy as jnp
from jax import lax
from jax.experimental import pallas as pl
from jax.experimental.pallas import tpu as pltpu
from jax.sharding import PartitionSpec as P

MESH = pl.DeviceIdType.MESH
BF = jnp.bfloat16
F32 = jnp.float32
NY, NZ, NX = 2, 8, 4
TPN = 8
FC = 64
TILE = 128
ROWS = TPN * TILE
SLOTS = 256
WORDS = 16
CNT = 16
BOTH = (1, -1)
PARTS = 4
UNROLL = 8
HBM = pl.BlockSpec(memory_space=pltpu.HBM)
VMEM = pl.BlockSpec(memory_space=pltpu.VMEM)
SMEM = pl.BlockSpec(memory_space=pltpu.SMEM)
OUT = pltpu.VMEM


def place():
    node, feat = lax.axis_index("node"), lax.axis_index("feat")
    return node // (NZ * NX), lax.rem(node // NX, NZ), lax.rem(node, NX), feat


def side(s):
    return 0 if s > 0 else 1


def node_of(y, z, x):
    return (y * NZ + z) * NX + x


def across(feat):
    return lax.rem(feat + 2, 4)


def sibling(feat):
    return feat + 1 - 2 * lax.rem(feat, 2)


def meet(peers):
    barrier = pltpu.get_barrier_semaphore()
    for peer in peers:
        pl.semaphore_signal(barrier, inc=1, device_id=peer, device_id_type=MESH)
    pl.semaphore_wait(barrier, len(peers))


def remote(src, dst, send, recv, peer):
    return pltpu.make_async_remote_copy(
        src_ref=src, dst_ref=dst, send_sem=send, recv_sem=recv, device_id=peer, device_id_type=MESH
    )


def exchange(mine, slot, feat, node, sems, send, recv):
    one, two = (node, across(feat)), (node, sibling(feat))
    far, near = across(feat), sibling(feat)
    diag = across(near)
    a = remote(mine, slot(feat), send.at[sems], recv.at[sems], one)
    b = remote(mine, slot(feat), send.at[sems + 1], recv.at[sems + 1], two)
    c = remote(slot(far), slot(far), send.at[sems + 2], recv.at[sems + 2], two)
    a.start()
    b.start()

    def step():
        remote(slot(far), slot(far), send.at[sems], recv.at[sems], one).wait_recv()
        c.start()

    def finish():
        remote(slot(near), slot(near), send.at[sems + 1], recv.at[sems + 1], two).wait_recv()
        remote(slot(diag), slot(diag), send.at[sems + 2], recv.at[sems + 2], two).wait_recv()
        a.wait_send()
        b.wait_send()
        c.wait_send()

    return step, finish


def dot(a, b):
    return jnp.dot(a, b, preferred_element_type=F32)


def nt(a, b):
    return lax.dot_general(a, b, (((1,), (1,)), ((), ())), preferred_element_type=F32)


def iota(shape, dim):
    return lax.broadcasted_iota(jnp.int32, shape, dim)


def order():
    old = iota((TILE, TILE), 1)
    new = jnp.bitwise_and(old, 7) * WORDS + lax.shift_right_logical(old, 3)
    return (iota((TILE, TILE), 0) == new).astype(F32).astype(BF)


ORDER = (
    "s0", "s1", "s2", "s3", "z21", "y", "z01", "e0", "z11", "e1", "z22", "z02", "c",
    "l0", "l1", "l2", "e2", "z12", "l3", "l4", "x", "z23", "e3", "l5", "z03", "h0",
    "l6", "z13", "l7", "i", "z24", "h1", "z04", "z14",
)


def gather_kernel(feats, wself, wneigh, rows, cols, count, words, full, xfull, wfull, edges, listed,
                  raw, ids, codes, marks,
                  zs, zr, es, er, bs, br, cs, cr, ys, yr, fs, fr, ls):
    y, z, x, feat = place()
    node = node_of(y, z, x)
    oy = 1 - y
    HALF = TPN // 2

    def zof(k):
        return lax.rem(z + k + 2 * NZ, NZ)

    def xof(k):
        return lax.rem(x + k + 2 * NX, NX)

    def zdev(s):
        return (node_of(y, zof(s), x), feat)

    def xdev(s):
        return (node_of(y, z, xof(s)), feat)

    ydev = (node_of(oy, z, x), feat)
    beside = (node, sibling(feat))
    peers = [zdev(1), zdev(-1), xdev(1), xdev(-1), xdev(2), ydev, (node, across(feat)), beside]
    barrier = pltpu.get_barrier_semaphore()
    for peer in peers:
        pl.semaphore_signal(barrier, inc=1, device_id=peer, device_id_type=MESH)

    half = lax.rem(feat, 2) * (SLOTS // 2)
    other = SLOTS // 2 - half
    PART = SLOTS // 8

    def load(c):
        base = half + c * PART if c < 4 else other
        span = pl.ds(base, PART if c < 4 else SLOTS // 2)
        return pltpu.make_async_copy(words.at[span], raw.at[span], ls.at[c])

    small = [
        pltpu.make_async_copy(a, b, ls.at[5 + i])
        for i, (a, b) in enumerate((
            (feats, xfull.at[feat]), (wself, wfull.at[feat, 0]), (wneigh, wfull.at[feat, 1]),
            (rows, ids.at[0]), (cols, ids.at[1]),
        ))
    ]
    small[0].start()
    for c in range(5):
        load(c).start()
    for copy in small[1:]:
        copy.start()
    perm = order()
    small[0].wait()
    for t in range(TPN):
        full[y, z, t] = nt(xfull[feat, :, t * TILE:(t + 1) * TILE], perm).astype(BF)
    for i in range(4):
        load(i).wait()
        span = pl.ds(half + i * PART, PART)
        edges[x, span] = raw[span].astype(jnp.int16)
    for copy in small[3:]:
        copy.wait()
    at = iota((2, TILE), 0) * TILE + iota((2, TILE), 1)
    codes[...] = jnp.full_like(codes, -1)
    codes[0:2] = jnp.where(at < count[0], ids[0] * 65536 + ids[1], -1)
    marks[x] = codes[...]
    pl.semaphore_wait(barrier, len(peers))

    def block(u, zr, d, s):
        base = (0, 0, HALF)[u] + (side(s) * (HALF // 2) if d == 4 else 0)
        return full.at[oy if u == 1 else y, zof(zr), pl.ds(base, HALF // 2 if d == 4 else HALF)]

    def zhop(s, u, d, arriving=False):
        i = (side(s), u, d - 1)
        at = block(u, -s * d if arriving else -s * (d - 1), d, s)
        return remote(at, at, zs.at[i], zr.at[i], zdev(s))

    def yhop(s, d, arriving=False):
        i = d if d < 1 else 1 + side(s) * 4 + d - 1
        i = 9 if d < 0 else i
        who = oy if arriving else y
        base = 0 if d < 0 else HALF
        base = base + (side(s) * (HALF // 2) if d == 4 else 0)
        at = full.at[who, zof(-s * max(d, 0)), pl.ds(base, HALF // 2 if d == 4 else HALF)]
        return remote(at, at, ys.at[i], yr.at[i], ydev)

    def ehop(s, c, d, arriving=False):
        i = (side(s), c, d - 1)
        at = edges.at[xof(-s * d if arriving else -s * (d - 1)), pl.ds(half + c * PART, PART)]
        return remote(at, at, es.at[i], er.at[i], xdev(s))

    def ehand(s, c, d, arriving=False):
        i = (side(s), c, d - 1)
        at = edges.at[xof(-s * d), pl.ds((other if arriving else half) + c * PART, PART)]
        return remote(at, at, bs.at[i], br.at[i], beside)

    def nth(s, i):
        return i if s > 0 else (i + 2) % 4

    def chop(k, arriving=False):
        at = marks.at[xof(-k) if arriving else x]
        return remote(codes if not arriving else at, at, cs.at[k - 1], cr.at[k - 1], xdev(k))

    yhop(1, -1).start()
    for s in BOTH:
        zhop(s, 2, 1).start()
        zhop(s, 0, 1).start()
    for k in range(1, NX):
        chop(k).start()
    yhop(1, 0).start()
    xstep, xfinish = exchange(feats, lambda k: xfull.at[k], feat, node, 0, fs, fr)
    wstep, wfinish = exchange(wself, lambda k: wfull.at[k, 0], feat, node, 3, fs, fr)
    vstep, vfinish = exchange(wneigh, lambda k: wfull.at[k, 1], feat, node, 6, fs, fr)
    small[1].wait()
    small[2].wait()

    def zpass(u, d):
        for s in BOTH:
            zhop(s, u, d, True).wait_recv()
            if d < 4:
                zhop(s, u, d + 1).start()
            if u == 2:
                yhop(s, d).start()

    def eround(i):
        for s in BOTH:
            c = nth(s, i)
            ehop(s, c, 1, True).wait_recv()
            if i < 2:
                ehop(s, c, 2).start()
            ehand(s, c, 1).start()

    def efar(i):
        for s in BOTH:
            c = nth(s, i)
            ehop(s, c, 2, True).wait_recv()
            ehand(s, c, 2).start()

    def efirst(i):
        for s in BOTH:
            ehop(s, nth(s, i), 1).start()

    def ycross():
        yhop(1, -1, True).wait_recv()
        for s in BOTH:
            zhop(s, 1, 1).start()

    def passon():
        for step in (xstep, wstep, vstep):
            step()

    state = {}

    def prepare():
        load(4).wait()
        span = pl.ds(other, SLOTS // 2)
        edges[x, span] = raw[span].astype(jnp.int16)
        for k in range(1, NX):
            chop(k, True).wait_recv()
        code = jnp.concatenate([marks[b, 0:2] for b in range(NX)], axis=0)
        col = jnp.bitwise_and(code, 511)
        mine = jnp.where(
            jnp.logical_and(code >= 0, jnp.bitwise_and(lax.shift_right_logical(col, 3), 3) == x), 1.0, 0.0
        )
        slot = iota((8, TILE), 0) * TILE + iota((8, TILE), 1)
        row = lax.shift_right_logical(slot, 8) * TPN + jnp.bitwise_and(lax.shift_right_arithmetic(code, 16), 7)
        near = lax.shift_left(lax.shift_right_logical(col, 5), 3) + jnp.bitwise_and(col, 7)
        upto = jnp.where(iota((TILE, TILE), 0) <= iota((TILE, TILE), 1), 1.0, 0.0).astype(BF)
        prefix = dot(mine.astype(BF), upto)
        pos = jnp.where(mine > 0.0, prefix - 1.0, -1.0e6)
        base = jnp.zeros((1, 1), F32)
        shifted = []
        for r in range(8):
            shifted.append(pos[r:r + 1] + base)
            base = base + prefix[r:r + 1, TILE - 1:TILE]
        pos = jnp.concatenate(shifted + [jnp.zeros((TILE - 8, TILE), F32)], axis=0).T
        wide = iota((TILE, 8 * TILE), 1).astype(F32)
        picked = jnp.zeros((8, 8 * TILE), F32)
        fields = (jnp.bitwise_and(slot, 255), lax.shift_right_logical(slot, 8), row, near)
        state.update(pos=pos, base=base, wide=wide, picked=picked, fields=fields)

    def pick(r):
        pos, wide, fields = state["pos"], state["wide"], state["fields"]
        hot = jnp.where(pos[:, r:r + 1] == wide, 1.0, 0.0).astype(BF)
        stack = jnp.concatenate([f[r:r + 1].astype(F32) for f in fields] + [jnp.zeros((4, TILE), F32)], axis=0)
        state["picked"] += dot(stack.astype(BF), hot)

    def enlist():
        picked, base = state["picked"], state["base"]
        items = (picked[0:1] + 256.0 * picked[1:2] + 1024.0 * picked[2:3] + 32768.0 * picked[3:4]).astype(jnp.int32)
        for r in range(8):
            listed[r:r + 1] = items[:, r * TILE:(r + 1) * TILE]
        listed[8:16] = jnp.broadcast_to(base, (8, TILE)).astype(jnp.int32)

    steps = {"z": zpass, "e": eround, "h": efar, "s": efirst, "y": ycross, "x": passon, "c": prepare, "l": pick, "i": enlist}
    for step in ORDER:
        steps[step[0]](*(int(digit) for digit in step[1:]))
    for s in BOTH:
        for i in range(4):
            c = nth(s, i)
            for d in (1, 2) if i < 2 else (1,):
                ehand(s, c, d, True).wait_recv()
                ehand(s, c, d).wait_send()
                ehop(s, c, d).wait_send()
        for d in range(1, 5):
            for u in range(3):
                zhop(s, u, d).wait_send()
            yhop(s, d, True).wait_recv()
            yhop(s, d).wait_send()
    yhop(1, 0, True).wait_recv()
    yhop(1, 0).wait_send()
    yhop(1, -1).wait_send()
    for k in range(1, NX):
        chop(k).wait_send()
    xfinish()
    wfinish()
    vfinish()


def gather(feats, wself, wneigh, rows, cols, count, words):
    dma = pltpu.SemaphoreType.DMA
    return pl.pallas_call(
        gather_kernel,
        out_shape=(
            OUT((NY, NZ, TPN, FC, TILE), BF),
            OUT((4, FC, ROWS), BF),
            OUT((4, 2, FC, 4 * FC), BF),
            OUT((NX, *words.shape), jnp.int16),
            jax.ShapeDtypeStruct((16, TILE), jnp.int32),
        ),
        in_specs=[HBM] * 5 + [SMEM, HBM],
        out_specs=(VMEM,) * 5,
        scratch_shapes=[
            pltpu.VMEM(words.shape, jnp.int32), pltpu.VMEM((2, 2, TILE), jnp.int32),
            pltpu.VMEM((8, TILE), jnp.int32), pltpu.VMEM((NX, 8, TILE), jnp.int32),
            dma((2, 3, 4)), dma((2, 3, 4)), dma((2, 4, 2)), dma((2, 4, 2)), dma((2, 4, 2)), dma((2, 4, 2)),
            dma((3,)), dma((3,)), dma((10,)), dma((10,)), dma((9,)), dma((9,)), dma((10,)),
        ],
        compiler_params=pltpu.CompilerParams(
            collective_id=0, has_side_effects=True, vmem_limit_bytes=24 * 2**20
        ),
        name="gather",
    )(feats, wself, wneigh, rows, cols, count, words)


def planes_of(words):
    one, zero = jnp.ones(words.shape, BF), jnp.zeros(words.shape, BF)
    return jnp.concatenate(
        [jnp.where(jnp.bitwise_and(words, jnp.int16(1 << b)) != 0, one, zero) for b in range(8)], axis=0
    )


def entry(slots, group, u, count, edges):
    item = slots[lax.shift_right_logical(group, 4), jnp.bitwise_and(group, 15) * UNROLL + u]
    words = edges[jnp.bitwise_and(lax.shift_right_logical(item, 8), 3), jnp.bitwise_and(item, 255)]
    planes = planes_of(jnp.where(group * UNROLL + u < count, words, jnp.zeros_like(words)))
    return jnp.bitwise_and(lax.shift_right_logical(item, 10), 31), lax.shift_right_logical(item, 15), planes


def forward_kernel(slots, edges, full, acc):
    acc[...] = jnp.zeros_like(acc)
    count = slots[8, 0]
    ones = jnp.ones((CNT, TILE), BF)

    def group(g, _):
        for u in range(UNROLL):
            row, col, planes = entry(slots, g, u, count, edges)
            near, t = lax.shift_right_logical(col, 3), jnp.bitwise_and(col, 7)
            block, tile = lax.shift_right_logical(row, 3), jnp.bitwise_and(row, 7)
            source = full[lax.shift_right_logical(near, 3), jnp.bitwise_and(near, 7), t]
            acc[block, tile] += dot(jnp.concatenate([source, ones], axis=0), planes)
        return 0

    lax.fori_loop(0, (count + UNROLL - 1) // UNROLL, group, 0)


def forward(slots, edges, full):
    return pl.pallas_call(
        forward_kernel,
        out_shape=OUT((NX, TPN, FC + CNT, TILE), F32),
        in_specs=[SMEM, VMEM, VMEM],
        out_specs=VMEM,
        compiler_params=pltpu.CompilerParams(vmem_limit_bytes=24 * 2**20),
        name="forward_sums",
    )(slots, edges, full)


DENSE = (
    "a0", "a1", "b0", "a2", "b1", "g0", "a3", "b2", "g1", "h0",
    "b3", "g2", "h1", "s0", "g3", "h2", "s1", "h3", "s2", "s3",
)


def dense_kernel(part, xfull, wfull, wself, wneigh, cot, act, direct, scaled, wgrad,
                 pq, pm, rq, rm, av, gr, send, recv, rs, rr, ss, sr):
    y, z, x, feat = place()
    node = node_of(y, z, x)
    CT = TPN // PARTS
    SPAN = ROWS // PARTS

    def xof(k):
        return lax.rem(x + k + 2 * NX, NX)

    def xdev(s):
        return (node_of(y, z, xof(s)), feat)

    peers = [xdev(1), xdev(-1), xdev(2), (node, across(feat)), (node, sibling(feat))]
    barrier = pltpu.get_barrier_semaphore()
    for peer in peers:
        pl.semaphore_signal(barrier, inc=1, device_id=peer, device_id_type=MESH)

    def pack(c, k):
        block = xof(k)
        for q in range(CT):
            r = c * CT + q
            sums = part[block, r, 0:FC]
            most = jnp.maximum(jnp.max(jnp.abs(sums), axis=0, keepdims=True), 1e-30)
            pq[c, k - 1, q] = jnp.round(sums * (32766.0 / most)).astype(jnp.int32).astype(jnp.int16)
            pm[c, k - 1, q:q + 1] = most * (1.0 / 32766.0)
            pm[c, k - 1, CT + q:CT + q + 1] = part[block, r, FC:FC + 1]

    def hop(c, k, what):
        i = (c, k - 1, what)
        src, dst = ((pq, rq), (pm, rm))[what]
        return remote(src.at[c, k - 1], dst.at[c, k - 1], rs.at[i], rr.at[i], xdev(k))

    ORDER = (2, 1, 3)
    for k in ORDER:
        pack(0, k)
    pl.semaphore_wait(barrier, len(peers))
    for c in range(PARTS):
        for k in ORDER:
            if c > 0:
                pack(c, k)
            hop(c, k, 1).start()
            hop(c, k, 0).start()

    choose = (iota((FC, 4 * FC), 1) == iota((FC, 4 * FC), 0) + feat * FC).astype(F32).astype(BF)

    def cols_of(k, which):
        return nt(choose, wfull[k, which]).astype(BF)

    pre = dot(cols_of(0, 0), xfull[0])
    for k in range(1, 4):
        pre += dot(cols_of(k, 0), xfull[k])
    neigh = [cols_of(k, 1) for k in range(4)]

    def share(ref, stage, c):
        return exchange(
            ref.at[feat, c], lambda k: ref.at[k, c], feat, node, 3 * (stage * PARTS + c), send, recv
        )

    degrees, first, second = {}, {}, {}

    def average(c):
        for k in ORDER:
            for what in (1, 0):
                hop(c, k, what).wait_recv()
        for q in range(CT):
            r = c * CT + q
            total = part[x, r, 0:FC]
            degree = part[x, r, FC:FC + 1]
            for k in range(3):
                total += rq[c, k, q].astype(jnp.int32).astype(F32) * rm[c, k, q:q + 1]
                degree += rm[c, k, CT + q:CT + q + 1]
            degrees[r] = jnp.maximum(degree, 1.0)
            av[feat, c, :, q * TILE:(q + 1) * TILE] = (total / degrees[r]).astype(BF)
        first[c] = share(av, 0, c)

    def gradient(c):
        first[c][1]()
        span = slice(c * SPAN, (c + 1) * SPAN)
        own = pre[:, span]
        for k in range(4):
            own += dot(neigh[k], av[k, c])
        sig = jax.nn.sigmoid(own)
        grad = cot[:, span] * sig * (1.0 + own * (1.0 - sig))
        gr[feat, c] = grad.astype(BF)
        second[c] = share(gr, 1, c)
        act[:, span] = own * sig

    def shop(c, k, arriving=False):
        at = scaled.at[xof(-k) if arriving else x, pl.ds(c * CT, CT)]
        return remote(at, at, ss.at[c, k - 1], sr.at[c, k - 1], xdev(k))

    def scale(c):
        second[c][1]()
        sums = dot(wneigh[:, 0:FC], gr[0, c])
        for k in range(1, 4):
            sums += dot(wneigh[:, k * FC:(k + 1) * FC], gr[k, c])
        for q in range(CT):
            r = c * CT + q
            scaled[x, r] = (sums[:, q * TILE:(q + 1) * TILE] / degrees[r]).astype(BF)
        for k in ORDER:
            shop(c, k).start()

    steps = {
        "a": average, "b": lambda c: first[c][0](), "g": gradient, "h": lambda c: second[c][0](), "s": scale
    }
    for step in DENSE:
        steps[step[0]](int(step[1]))
    for c in range(PARTS):
        total = dot(wself[:, 0:FC], gr[0, c])
        for k in range(1, 4):
            total += dot(wself[:, k * FC:(k + 1) * FC], gr[k, c])
        direct[:, c * SPAN:(c + 1) * SPAN] = total
    for k in range(4):
        lanes = slice(k * FC, (k + 1) * FC)
        mine, near = jnp.zeros((FC, FC), F32), jnp.zeros((FC, FC), F32)
        for c in range(PARTS):
            mine += nt(xfull[feat, :, c * SPAN:(c + 1) * SPAN], gr[k, c])
            near += nt(av[feat, c], gr[k, c])
        wgrad[0:FC, lanes] = mine
        wgrad[FC:2 * FC, lanes] = near
    for c in range(PARTS):
        for k in ORDER:
            shop(c, k, True).wait_recv()
            shop(c, k).wait_send()
            for what in range(2):
                hop(c, k, what).wait_send()


def dense(part, xfull, wfull, wself, wneigh, cot):
    dma = pltpu.SemaphoreType.DMA
    return pl.pallas_call(
        dense_kernel,
        out_shape=(
            jax.ShapeDtypeStruct((FC, ROWS), F32),
            OUT((FC, ROWS), F32),
            OUT((NX, TPN, FC, TILE), BF),
            OUT((2 * FC, 4 * FC), F32),
        ),
        in_specs=[VMEM] * 6,
        out_specs=(VMEM,) * 4,
        scratch_shapes=[
            pltpu.VMEM((PARTS, 3, TPN // PARTS, FC, TILE), jnp.int16), pltpu.VMEM((PARTS, 3, 8, TILE), F32),
            pltpu.VMEM((PARTS, 3, TPN // PARTS, FC, TILE), jnp.int16), pltpu.VMEM((PARTS, 3, 8, TILE), F32),
            pltpu.VMEM((4, PARTS, FC, ROWS // PARTS), BF), pltpu.VMEM((4, PARTS, FC, ROWS // PARTS), BF),
            dma((6 * PARTS,)), dma((6 * PARTS,)), dma((PARTS, 3, 2)), dma((PARTS, 3, 2)),
            dma((PARTS, 3)), dma((PARTS, 3)),
        ],
        compiler_params=pltpu.CompilerParams(
            collective_id=1, has_side_effects=True, vmem_limit_bytes=24 * 2**20
        ),
        name="dense",
    )(part, xfull, wfull, wself, wneigh, cot)


def backward_kernel(slots, edges, source, act, out, acted, acc):
    acted[...] = act[...]
    acc[...] = jnp.zeros_like(acc)
    count = slots[8, 0]

    def group(g, _):
        for u in range(UNROLL):
            row, col, planes = entry(slots, g, u, count, edges)
            block, tile = lax.shift_right_logical(row, 3), jnp.bitwise_and(row, 7)
            acc[col] += nt(source[block, tile], planes)
        return 0

    lax.fori_loop(0, (count + UNROLL - 1) // UNROLL, group, 0)
    for y in range(NY):
        for z in range(NZ):
            base = (y * NZ + z) * TPN
            out[y, z] = acc[base:base + TPN].astype(BF)


def backward(slots, edges, source, act):
    return pl.pallas_call(
        backward_kernel,
        out_shape=(OUT((NY, NZ, TPN, FC, TILE), BF), jax.ShapeDtypeStruct((FC, ROWS), F32)),
        in_specs=[SMEM, VMEM, VMEM, VMEM],
        out_specs=(VMEM, VMEM),
        scratch_shapes=[pltpu.VMEM((NY * NZ * TPN, FC, TILE), F32)],
        compiler_params=pltpu.CompilerParams(vmem_limit_bytes=24 * 2**20),
        name="backward_sums",
    )(slots, edges, source, act)


W_AT = ((4, 0), (3, 0), (2, 0))
NEAR = 3


def scatter_kernel(part, wgrad, direct, out, wout, rz, ry, rl, w1, w2, w3, w4, zs, zr, ys, yr, ws, wr):
    y, z, x, feat = place()
    oy = 1 - y
    FAR = TPN - NEAR

    def zof(k):
        return lax.rem(z + k + 2 * NZ, NZ)

    def zdev(s):
        return (node_of(y, zof(s), x), feat)

    plane = y * NX + x

    def pdev(k):
        p = lax.rem(plane + k, NY * NX)
        return (node_of(p // NX, z, lax.rem(p, NX)), feat)

    meet([zdev(k) for k in range(1, NZ)] + [pdev(k) for k in range(1, NY * NX)])
    ydev = (node_of(oy, z, x), feat)

    def term(u, k):
        if u == 2:
            return ry.at[(k + NZ) % NZ]
        return part.at[oy if u == 1 else y, zof(k), pl.ds(0, NEAR)]

    def size(u):
        return FAR if u == 2 else NEAR

    def cut(u, k):
        return pl.ds(0, 2) if k == 0 else pl.ds(2, size(u) - 2)

    def slot(s, u, d):
        return rz.at[side(s), u, d - 1, pl.ds(0, size(u))]

    def hop(s, u, d):
        i = (side(s), u, d - 1)
        src, dst = term(u, 4) if d == 4 else slot(s, u, d + 1), slot(s, u, d)
        if d == 4:
            src, dst = src.at[cut(u, side(s))], dst.at[cut(u, side(s))]
        return remote(src, dst, zs.at[i], zr.at[i], zdev(s))

    def yhop(k):
        return remote(part.at[oy, zof(k), pl.ds(NEAR, FAR)], ry.at[(k + NZ) % NZ],
                      ys.at[(k + NZ) % NZ], yr.at[(k + NZ) % NZ], ydev)

    def join(k):
        yhop(k).wait_recv()
        at = (k + NZ) % NZ
        ry[at] = (ry[at].astype(F32) + part[y, zof(k), NEAR:TPN].astype(F32)).astype(BF)

    last = remote(slot(1, 1, 1), rl, ys.at[NZ], yr.at[NZ], ydev)

    def rows(p):
        return pl.ds(pl.multiple_of(p * 16, 16), 16)

    def pof(k):
        return lax.rem(plane + k + NY * NX, NY * NX)

    def wcopy(phase, k):
        i = phase * 7 + k - 1
        peer = pdev(k) if phase in (0, 3) else zdev(k)
        src, dst = (
            (wgrad.at[rows(pof(k))], w1.at[k - 1]), (w2.at[zof(k)], w3.at[k - 1]), (w4.at[z], w4.at[z]),
            (wout.at[rows(plane)], wout.at[rows(plane)]),
        )[phase]
        return remote(src, dst, ws.at[i], wr.at[i], peer)

    def wexpect(phase, k):
        i = phase * 7 + k - 1
        dst = (w1.at[k - 1], w3.at[k - 1], w4.at[zof(-k)], wout.at[rows(pof(-k))])[phase]
        return remote(dst, dst, ws.at[i], wr.at[i], zdev(k))

    def wturn(phase):
        for k in range(1, 8):
            wexpect(phase, k).wait_recv()
        if phase == 0:
            acc = wgrad[rows(plane)]
            for k in range(1, 8):
                acc += w1[k - 1]
            for q in range(NZ):
                w2[q] = acc[2 * q:2 * q + 2]
        elif phase == 1:
            acc = w2[z]
            for k in range(1, 8):
                acc += w3[k - 1]
            w4[z] = acc
        else:
            wout[rows(plane)] = jnp.concatenate([w4[q] for q in range(NZ)], axis=0)
        for k in range(1, 8):
            wcopy(phase + 1, k).start()

    for k in range(1, 8):
        wcopy(0, k).start()
    for k in (4, 3, -3):
        yhop(k).start()
    for u in (1, 0):
        for s in BOTH:
            hop(s, u, 4).start()
    for k in (2, -2, 1, -1, 0):
        yhop(k).start()
    join(4)
    for s in BOTH:
        hop(s, 2, 4).start()
    for d in (4, 3, 2):
        for u in (1, 0, 2):
            if u == 2:
                join(d - 1)
                join(1 - d)
            for s in BOTH:
                hop(s, u, d).wait_recv()
                i = (side(s), u, d - 1)
                more = term(u, s * (d - 1))
                if d == 4:
                    a, b = cut(u, side(s)), cut(u, 1 - side(s))
                    rz[(*i, a)] = (rz[(*i, a)].astype(F32) + more[a].astype(F32)).astype(BF)
                    rz[(*i, b)] = more[b]
                else:
                    i = (*i, slice(0, size(u)))
                    rz[i] = (rz[i].astype(F32) + more[...].astype(F32)).astype(BF)
                hop(s, u, d - 1).start()
            if (d, u) in W_AT:
                wturn(W_AT.index((d, u)))

    def total(u):
        for s in BOTH:
            hop(s, u, 1).wait_recv()
        one, two = rz[0, u, 0, 0:size(u)].astype(F32), rz[1, u, 0, 0:size(u)].astype(F32)
        return term(u, 0)[...].astype(F32) + one + two

    perm = order()

    def finish(base, sums):
        flat = sums.reshape(-1, TILE)
        high = flat.astype(BF)
        back = dot(high, perm) + dot((flat - high.astype(F32)).astype(BF), perm)
        for t in range(sums.shape[0]):
            lanes = slice((base + t) * TILE, (base + t + 1) * TILE)
            out[:, lanes] = direct[:, lanes] + back[t * FC:(t + 1) * FC]

    rz[0, 1, 0, 0:NEAR] = total(1).astype(BF)
    last.start()
    join(0)
    finish(NEAR, total(2))
    sums = total(0)
    last.wait_recv()
    finish(0, sums + rl[...].astype(F32))
    for k in range(1, NZ):
        wexpect(3, k).wait_recv()
    for s in BOTH:
        for u in range(3):
            for d in range(1, 5):
                hop(s, u, d).wait_send()
    for k in range(NZ):
        yhop(k).wait_send()
    last.wait_send()
    for phase in range(4):
        for k in range(1, 8):
            wcopy(phase, k).wait_send()


def scatter(part, wgrad, direct):
    dma = pltpu.SemaphoreType.DMA
    return pl.pallas_call(
        scatter_kernel,
        out_shape=(
            jax.ShapeDtypeStruct((FC, ROWS), F32),
            jax.ShapeDtypeStruct((2 * FC, 4 * FC), F32),
        ),
        in_specs=[VMEM, VMEM, VMEM],
        out_specs=(VMEM, VMEM),
        scratch_shapes=[
            pltpu.VMEM((2, 3, 4, TPN - NEAR, FC, TILE), BF),
            pltpu.VMEM((NZ, TPN - NEAR, FC, TILE), BF),
            pltpu.VMEM((NEAR, FC, TILE), BF),
            pltpu.VMEM((NZ - 1, 16, 256), F32),
            pltpu.VMEM((NZ, 2, 256), F32), pltpu.VMEM((NZ - 1, 2, 256), F32), pltpu.VMEM((NZ, 2, 256), F32),
            dma((2, 3, 4)), dma((2, 3, 4)), dma((NZ + 1,)), dma((NZ + 1,)), dma((28,)), dma((28,)),
        ],
        compiler_params=pltpu.CompilerParams(
            collective_id=2, has_side_effects=True, vmem_limit_bytes=24 * 2**20
        ),
        name="scatter",
    )(part, wgrad, direct)


def local(features, w_self, w_neigh, tile_rows, tile_cols, tile_count, edge_bits, cotangent):
    rows, cols = tile_rows.reshape(2, TILE), tile_cols.reshape(2, TILE)
    given = [
        pltpu.with_memory_space_constraint(a, pltpu.HBM)
        for a in (features.T, w_self, w_neigh, rows, cols, edge_bits)
    ]
    full, xfull, wfull, edges, slots = gather(*given[:5], tile_count, given[5])
    part = forward(slots, edges, full)
    act, direct, scaled, wgrad = dense(part, xfull, wfull, w_self, w_neigh, cotangent.T)
    part, act = backward(slots, edges, scaled, act)
    grad, wsum = scatter(part, wgrad, direct)
    return act.T, grad.T, wsum[:FC], wsum[FC:]


def solution(mesh):
    placed = (
        P("node", "feat"),
        P("feat", None),
        P("feat", None),
        P("node"),
        P("node"),
        P("node"),
        P("node", None, None),
        P("node", "feat"),
    )
    return jax.shard_map(
        local,
        mesh=mesh,
        in_specs=placed,
        out_specs=(P("node", "feat"), P("node", "feat"), P("feat", None), P("feat", None)),
        check_vma=False,
    )
```

```python
import jax
import jax.numpy as jnp
from jax import lax
from jax.experimental import pallas as pl
from jax.experimental.pallas import tpu as pltpu
from jax.sharding import PartitionSpec as P

MESH = pl.DeviceIdType.MESH
BF = jnp.bfloat16
F32 = jnp.float32
NY, NZ, NX = 2, 8, 4
TPN = 8
FC = 64
TILE = 128
ROWS = TPN * TILE
SLOTS = 256
WORDS = 16
LISTED = 9
CNT = 16
BOTH = (1, -1)
PARTS = 4
UNROLL = 8
HBM = pl.BlockSpec(memory_space=pltpu.HBM)
VMEM = pl.BlockSpec(memory_space=pltpu.VMEM)
SMEM = pl.BlockSpec(memory_space=pltpu.SMEM)
OUT = pltpu.VMEM


def place():
    node, feat = lax.axis_index("node"), lax.axis_index("feat")
    return node // (NZ * NX), lax.rem(node // NX, NZ), lax.rem(node, NX), feat


def side(s):
    return 0 if s > 0 else 1


def node_of(y, z, x):
    return (y * NZ + z) * NX + x


def across(feat):
    return lax.rem(feat + 2, 4)


def sibling(feat):
    return feat + 1 - 2 * lax.rem(feat, 2)


def meet(peers):
    barrier = pltpu.get_barrier_semaphore()
    for peer in peers:
        pl.semaphore_signal(barrier, inc=1, device_id=peer, device_id_type=MESH)
    pl.semaphore_wait(barrier, len(peers))


def remote(src, dst, send, recv, peer):
    return pltpu.make_async_remote_copy(
        src_ref=src, dst_ref=dst, send_sem=send, recv_sem=recv, device_id=peer, device_id_type=MESH
    )


def exchange(mine, slot, feat, node, sems, send, recv):
    one, two = (node, across(feat)), (node, sibling(feat))
    far, near = across(feat), sibling(feat)
    diag = across(near)
    a = remote(mine, slot(feat), send.at[sems], recv.at[sems], one)
    b = remote(mine, slot(feat), send.at[sems + 1], recv.at[sems + 1], two)
    c = remote(slot(far), slot(far), send.at[sems + 2], recv.at[sems + 2], two)
    a.start()
    b.start()

    def step():
        remote(slot(far), slot(far), send.at[sems], recv.at[sems], one).wait_recv()
        c.start()

    def finish():
        remote(slot(near), slot(near), send.at[sems + 1], recv.at[sems + 1], two).wait_recv()
        remote(slot(diag), slot(diag), send.at[sems + 2], recv.at[sems + 2], two).wait_recv()
        a.wait_send()
        b.wait_send()
        c.wait_send()

    return step, finish


def dot(a, b):
    return jnp.dot(a, b, preferred_element_type=F32)


def nt(a, b):
    return lax.dot_general(a, b, (((1,), (1,)), ((), ())), preferred_element_type=F32)


def iota(shape, dim):
    return lax.broadcasted_iota(jnp.int32, shape, dim)


def order():
    old = iota((TILE, TILE), 1)
    new = jnp.bitwise_and(old, 7) * WORDS + lax.shift_right_logical(old, 3)
    return (iota((TILE, TILE), 0) == new).astype(F32).astype(BF)


ORDER = (
    "s0", "s1", "s2", "s3", "z21", "y", "z01", "e0", "z11", "e1", "z22", "z02", "c",
    "l0", "l1", "l2", "e2", "z12", "l3", "l4", "x", "z23", "e3", "l5", "z03", "h0",
    "l6", "z13", "l7", "i", "z24", "h1", "z04", "z14",
)


def gather_kernel(feats, wself, wneigh, rows, cols, count, words, full, xfull, wfull, edges, listed,
                  raw, ids, codes, marks,
                  zs, zr, es, er, bs, br, cs, cr, ys, yr, fs, fr, ls):
    y, z, x, feat = place()
    node = node_of(y, z, x)
    oy = 1 - y
    HALF = TPN // 2

    def zof(k):
        return lax.rem(z + k + 2 * NZ, NZ)

    def xof(k):
        return lax.rem(x + k + 2 * NX, NX)

    def zdev(s):
        return (node_of(y, zof(s), x), feat)

    def xdev(s):
        return (node_of(y, z, xof(s)), feat)

    ydev = (node_of(oy, z, x), feat)
    beside = (node, sibling(feat))
    peers = [zdev(1), zdev(-1), xdev(1), xdev(-1), xdev(2), ydev, (node, across(feat)), beside]
    barrier = pltpu.get_barrier_semaphore()
    for peer in peers:
        pl.semaphore_signal(barrier, inc=1, device_id=peer, device_id_type=MESH)

    half = lax.rem(feat, 2) * (SLOTS // 2)
    other = SLOTS // 2 - half
    PART = SLOTS // 8

    def load(c):
        base = half + c * PART if c < 4 else other
        span = pl.ds(base, PART if c < 4 else SLOTS // 2)
        return pltpu.make_async_copy(words.at[span], raw.at[span], ls.at[c])

    small = [
        pltpu.make_async_copy(a, b, ls.at[5 + i])
        for i, (a, b) in enumerate((
            (feats, xfull.at[feat]), (wself, wfull.at[feat, 0]), (wneigh, wfull.at[feat, 1]),
            (rows, ids.at[0]), (cols, ids.at[1]),
        ))
    ]
    small[0].start()
    for c in range(5):
        load(c).start()
    for copy in small[1:]:
        copy.start()
    perm = order()
    small[0].wait()
    for t in range(TPN):
        full[y, z, t] = nt(xfull[feat, :, t * TILE:(t + 1) * TILE], perm).astype(BF)
    for i in range(4):
        load(i).wait()
        span = pl.ds(half + i * PART, PART)
        edges[x, span] = raw[span].astype(jnp.int16)
    for copy in small[3:]:
        copy.wait()
    at = iota((2, TILE), 0) * TILE + iota((2, TILE), 1)
    codes[...] = jnp.full_like(codes, -1)
    codes[0:2] = jnp.where(at < count[0], ids[0] * 65536 + ids[1], -1)
    marks[x] = codes[...]
    pl.semaphore_wait(barrier, len(peers))

    def block(u, zr, d, s):
        base = (0, 0, HALF)[u] + (side(s) * (HALF // 2) if d == 4 else 0)
        return full.at[oy if u == 1 else y, zof(zr), pl.ds(base, HALF // 2 if d == 4 else HALF)]

    def zhop(s, u, d, arriving=False):
        i = (side(s), u, d - 1)
        at = block(u, -s * d if arriving else -s * (d - 1), d, s)
        return remote(at, at, zs.at[i], zr.at[i], zdev(s))

    def yhop(s, d, arriving=False):
        i = d if d < 1 else 1 + side(s) * 4 + d - 1
        i = 9 if d < 0 else i
        who = oy if arriving else y
        base = 0 if d < 0 else HALF
        base = base + (side(s) * (HALF // 2) if d == 4 else 0)
        at = full.at[who, zof(-s * max(d, 0)), pl.ds(base, HALF // 2 if d == 4 else HALF)]
        return remote(at, at, ys.at[i], yr.at[i], ydev)

    def ehop(s, c, d, arriving=False):
        i = (side(s), c, d - 1)
        at = edges.at[xof(-s * d if arriving else -s * (d - 1)), pl.ds(half + c * PART, PART)]
        return remote(at, at, es.at[i], er.at[i], xdev(s))

    def ehand(s, c, d, arriving=False):
        i = (side(s), c, d - 1)
        at = edges.at[xof(-s * d), pl.ds((other if arriving else half) + c * PART, PART)]
        return remote(at, at, bs.at[i], br.at[i], beside)

    def nth(s, i):
        return i if s > 0 else (i + 2) % 4

    def chop(k, arriving=False):
        at = marks.at[xof(-k) if arriving else x]
        return remote(codes if not arriving else at, at, cs.at[k - 1], cr.at[k - 1], xdev(k))

    yhop(1, -1).start()
    for s in BOTH:
        zhop(s, 2, 1).start()
        zhop(s, 0, 1).start()
    for k in range(1, NX):
        chop(k).start()
    yhop(1, 0).start()
    xstep, xfinish = exchange(feats, lambda k: xfull.at[k], feat, node, 0, fs, fr)
    wstep, wfinish = exchange(wself, lambda k: wfull.at[k, 0], feat, node, 3, fs, fr)
    vstep, vfinish = exchange(wneigh, lambda k: wfull.at[k, 1], feat, node, 6, fs, fr)
    small[1].wait()
    small[2].wait()

    def zpass(u, d):
        for s in BOTH:
            zhop(s, u, d, True).wait_recv()
            if d < 4:
                zhop(s, u, d + 1).start()
            if u == 2:
                yhop(s, d).start()

    def eround(i):
        for s in BOTH:
            c = nth(s, i)
            ehop(s, c, 1, True).wait_recv()
            if i < 2:
                ehop(s, c, 2).start()
            ehand(s, c, 1).start()

    def efar(i):
        for s in BOTH:
            c = nth(s, i)
            ehop(s, c, 2, True).wait_recv()
            ehand(s, c, 2).start()

    def efirst(i):
        for s in BOTH:
            ehop(s, nth(s, i), 1).start()

    def ycross():
        yhop(1, -1, True).wait_recv()
        for s in BOTH:
            zhop(s, 1, 1).start()

    def passon():
        for step in (xstep, wstep, vstep):
            step()

    state = {}

    def prepare():
        load(4).wait()
        span = pl.ds(other, SLOTS // 2)
        edges[x, span] = raw[span].astype(jnp.int16)
        for k in range(1, NX):
            chop(k, True).wait_recv()
        code = jnp.concatenate([marks[b, 0:2] for b in range(NX)], axis=0)
        col = jnp.bitwise_and(code, 511)
        mine = jnp.where(
            jnp.logical_and(code >= 0, jnp.bitwise_and(lax.shift_right_logical(col, 3), 3) == x), 1.0, 0.0
        )
        slot = iota((8, TILE), 0) * TILE + iota((8, TILE), 1)
        row = lax.shift_right_logical(slot, 8) * TPN + jnp.bitwise_and(lax.shift_right_arithmetic(code, 16), 7)
        near = lax.shift_left(lax.shift_right_logical(col, 5), 3) + jnp.bitwise_and(col, 7)
        upto = jnp.where(iota((TILE, TILE), 0) <= iota((TILE, TILE), 1), 1.0, 0.0).astype(BF)
        tile = jnp.bitwise_and(row, 7)
        runs, begin, places = [], jnp.zeros((1, TILE), F32), []
        for b in range(NX):
            seen = jnp.zeros((TPN, 1), F32)
            for r in (2 * b, 2 * b + 1):
                hot = jnp.where(iota((TPN, TILE), 0) == tile[r:r + 1], mine[r:r + 1], 0.0)
                rank = dot(hot.astype(BF), upto) + seen
                runs.append((hot, rank))
                seen = rank[:, TILE - 1:TILE]
            even = jnp.broadcast_to(2.0 * jnp.floor((seen + 1.0) * 0.5), (TPN, TILE))
            starts = []
            for j in range(TPN):
                starts.append(begin)
                begin = begin + even[j:j + 1]
            start = jnp.concatenate(starts, axis=0) - 1.0
            for r in (2 * b, 2 * b + 1):
                hot, rank = runs[r]
                place = jnp.sum(hot * (start + rank), axis=0, keepdims=True)
                places.append(jnp.where(mine[r:r + 1] > 0.0, place, -1.0e6))
        base = begin
        pos = jnp.concatenate(places + [jnp.zeros((TILE - 8, TILE), F32)], axis=0).T
        wide = iota((TILE, LISTED * TILE), 1).astype(F32)
        picked = jnp.zeros((8, LISTED * TILE), F32)
        fields = (jnp.bitwise_and(slot, 255), lax.shift_right_logical(slot, 8), row, near + 128)
        state.update(pos=pos, base=base, wide=wide, picked=picked, fields=fields)

    def pick(r):
        pos, wide, fields = state["pos"], state["wide"], state["fields"]
        hot = jnp.where(pos[:, r:r + 1] == wide, 1.0, 0.0).astype(BF)
        stack = jnp.concatenate([f[r:r + 1].astype(F32) for f in fields] + [jnp.zeros((4, TILE), F32)], axis=0)
        state["picked"] += dot(stack.astype(BF), hot)

    def enlist():
        picked, base = state["picked"], state["base"]
        items = (picked[0:1] + 256.0 * picked[1:2] + 1024.0 * picked[2:3] + 32768.0 * picked[3:4]).astype(jnp.int32)
        for r in range(LISTED):
            listed[r:r + 1] = items[:, r * TILE:(r + 1) * TILE]
        listed[LISTED:16] = jnp.broadcast_to(base, (16 - LISTED, TILE)).astype(jnp.int32)

    steps = {"z": zpass, "e": eround, "h": efar, "s": efirst, "y": ycross, "x": passon, "c": prepare, "l": pick, "i": enlist}
    for step in ORDER:
        steps[step[0]](*(int(digit) for digit in step[1:]))
    for s in BOTH:
        for i in range(4):
            c = nth(s, i)
            for d in (1, 2) if i < 2 else (1,):
                ehand(s, c, d, True).wait_recv()
                ehand(s, c, d).wait_send()
                ehop(s, c, d).wait_send()
        for d in range(1, 5):
            for u in range(3):
                zhop(s, u, d).wait_send()
            yhop(s, d, True).wait_recv()
            yhop(s, d).wait_send()
    yhop(1, 0, True).wait_recv()
    yhop(1, 0).wait_send()
    yhop(1, -1).wait_send()
    for k in range(1, NX):
        chop(k).wait_send()
    xfinish()
    wfinish()
    vfinish()


def gather(feats, wself, wneigh, rows, cols, count, words):
    dma = pltpu.SemaphoreType.DMA
    return pl.pallas_call(
        gather_kernel,
        out_shape=(
            OUT((NY, NZ, TPN, FC, TILE), BF),
            OUT((4, FC, ROWS), BF),
            OUT((4, 2, FC, 4 * FC), BF),
            OUT((NX, *words.shape), jnp.int16),
            jax.ShapeDtypeStruct((16, TILE), jnp.int32),
        ),
        in_specs=[HBM] * 5 + [SMEM, HBM],
        out_specs=(VMEM,) * 5,
        scratch_shapes=[
            pltpu.VMEM(words.shape, jnp.int32), pltpu.VMEM((2, 2, TILE), jnp.int32),
            pltpu.VMEM((8, TILE), jnp.int32), pltpu.VMEM((NX, 8, TILE), jnp.int32),
            dma((2, 3, 4)), dma((2, 3, 4)), dma((2, 4, 2)), dma((2, 4, 2)), dma((2, 4, 2)), dma((2, 4, 2)),
            dma((3,)), dma((3,)), dma((10,)), dma((10,)), dma((9,)), dma((9,)), dma((10,)),
        ],
        compiler_params=pltpu.CompilerParams(
            collective_id=0, has_side_effects=True, vmem_limit_bytes=24 * 2**20
        ),
        name="gather",
    )(feats, wself, wneigh, rows, cols, count, words)


def planes_of(words):
    one, zero = jnp.ones(words.shape, BF), jnp.zeros(words.shape, BF)
    return jnp.concatenate(
        [jnp.where(jnp.bitwise_and(words, jnp.int16(1 << b)) != 0, one, zero) for b in range(8)], axis=0
    )


def entry(slots, group, u, edges):
    item = slots[lax.shift_right_logical(group, 4), jnp.bitwise_and(group, 15) * UNROLL + u]
    words = edges[jnp.bitwise_and(lax.shift_right_logical(item, 8), 3), jnp.bitwise_and(item, 255)]
    planes = planes_of(jnp.where(item > 0, words, jnp.zeros_like(words)))
    row, col = lax.shift_right_logical(item, 10), lax.shift_right_logical(item, 15)
    return jnp.bitwise_and(row, 31), jnp.bitwise_and(col, 127), planes


def forward_kernel(slots, edges, full, acc):
    acc[...] = jnp.zeros_like(acc)
    count = slots[LISTED, 0]
    ones = jnp.ones((CNT, TILE), BF)

    def source(col):
        near, t = lax.shift_right_logical(col, 3), jnp.bitwise_and(col, 7)
        return jnp.concatenate([full[lax.shift_right_logical(near, 3), jnp.bitwise_and(near, 7), t], ones], axis=0)

    def group(g, _):
        for u in range(0, UNROLL, 2):
            row, one, first = entry(slots, g, u, edges)
            _, two, second = entry(slots, g, u + 1, edges)
            acc[lax.shift_right_logical(row, 3), jnp.bitwise_and(row, 7)] += dot(
                jnp.concatenate([source(one), source(two)], axis=1), jnp.concatenate([first, second], axis=0)
            )
        return 0

    lax.fori_loop(0, (count + UNROLL - 1) // UNROLL, group, 0)


def forward(slots, edges, full):
    return pl.pallas_call(
        forward_kernel,
        out_shape=OUT((NX, TPN, FC + CNT, TILE), F32),
        in_specs=[SMEM, VMEM, VMEM],
        out_specs=VMEM,
        compiler_params=pltpu.CompilerParams(vmem_limit_bytes=24 * 2**20),
        name="forward_sums",
    )(slots, edges, full)


DENSE = (
    "a0", "a1", "b0", "a2", "b1", "g0", "a3", "b2", "g1", "h0",
    "b3", "g2", "h1", "s0", "g3", "h2", "s1", "h3", "s2", "s3",
)


def dense_kernel(part, xfull, wfull, wself, wneigh, cot, act, direct, scaled, wgrad,
                 pq, pm, rq, rm, av, gr, send, recv, rs, rr, ss, sr):
    y, z, x, feat = place()
    node = node_of(y, z, x)
    CT = TPN // PARTS
    SPAN = ROWS // PARTS

    def xof(k):
        return lax.rem(x + k + 2 * NX, NX)

    def xdev(s):
        return (node_of(y, z, xof(s)), feat)

    peers = [xdev(1), xdev(-1), xdev(2), (node, across(feat)), (node, sibling(feat))]
    barrier = pltpu.get_barrier_semaphore()
    for peer in peers:
        pl.semaphore_signal(barrier, inc=1, device_id=peer, device_id_type=MESH)

    def pack(c, k):
        block = xof(k)
        for q in range(CT):
            r = c * CT + q
            sums = part[block, r, 0:FC]
            most = jnp.maximum(jnp.max(jnp.abs(sums), axis=0, keepdims=True), 1e-30)
            pq[c, k - 1, q] = jnp.round(sums * (32766.0 / most)).astype(jnp.int32).astype(jnp.int16)
            pm[c, k - 1, q:q + 1] = most * (1.0 / 32766.0)
            pm[c, k - 1, CT + q:CT + q + 1] = part[block, r, FC:FC + 1]

    def hop(c, k, what):
        i = (c, k - 1, what)
        src, dst = ((pq, rq), (pm, rm))[what]
        return remote(src.at[c, k - 1], dst.at[c, k - 1], rs.at[i], rr.at[i], xdev(k))

    ORDER = (2, 1, 3)
    for k in ORDER:
        pack(0, k)
    pl.semaphore_wait(barrier, len(peers))
    for c in range(PARTS):
        for k in ORDER:
            if c > 0:
                pack(c, k)
            hop(c, k, 1).start()
            hop(c, k, 0).start()

    choose = (iota((FC, 4 * FC), 1) == iota((FC, 4 * FC), 0) + feat * FC).astype(F32).astype(BF)

    def cols_of(k, which):
        return nt(choose, wfull[k, which]).astype(BF)

    pre = dot(cols_of(0, 0), xfull[0])
    for k in range(1, 4):
        pre += dot(cols_of(k, 0), xfull[k])
    neigh = [cols_of(k, 1) for k in range(4)]

    def share(ref, stage, c):
        return exchange(
            ref.at[feat, c], lambda k: ref.at[k, c], feat, node, 3 * (stage * PARTS + c), send, recv
        )

    degrees, first, second = {}, {}, {}

    def average(c):
        for k in ORDER:
            for what in (1, 0):
                hop(c, k, what).wait_recv()
        for q in range(CT):
            r = c * CT + q
            total = part[x, r, 0:FC]
            degree = part[x, r, FC:FC + 1]
            for k in range(3):
                total += rq[c, k, q].astype(jnp.int32).astype(F32) * rm[c, k, q:q + 1]
                degree += rm[c, k, CT + q:CT + q + 1]
            degrees[r] = jnp.maximum(degree, 1.0)
            av[feat, c, :, q * TILE:(q + 1) * TILE] = (total / degrees[r]).astype(BF)
        first[c] = share(av, 0, c)

    def gradient(c):
        first[c][1]()
        span = slice(c * SPAN, (c + 1) * SPAN)
        own = pre[:, span]
        for k in range(4):
            own += dot(neigh[k], av[k, c])
        sig = jax.nn.sigmoid(own)
        grad = cot[:, span] * sig * (1.0 + own * (1.0 - sig))
        gr[feat, c] = grad.astype(BF)
        second[c] = share(gr, 1, c)
        act[:, span] = own * sig

    def shop(c, k, arriving=False):
        at = scaled.at[xof(-k) if arriving else x, pl.ds(c * CT, CT)]
        return remote(at, at, ss.at[c, k - 1], sr.at[c, k - 1], xdev(k))

    def scale(c):
        second[c][1]()
        sums = dot(wneigh[:, 0:FC], gr[0, c])
        for k in range(1, 4):
            sums += dot(wneigh[:, k * FC:(k + 1) * FC], gr[k, c])
        for q in range(CT):
            r = c * CT + q
            scaled[x, r] = (sums[:, q * TILE:(q + 1) * TILE] / degrees[r]).astype(BF)
        for k in ORDER:
            shop(c, k).start()

    steps = {
        "a": average, "b": lambda c: first[c][0](), "g": gradient, "h": lambda c: second[c][0](), "s": scale
    }
    for step in DENSE:
        steps[step[0]](int(step[1]))
    for c in range(PARTS):
        total = dot(wself[:, 0:FC], gr[0, c])
        for k in range(1, 4):
            total += dot(wself[:, k * FC:(k + 1) * FC], gr[k, c])
        direct[:, c * SPAN:(c + 1) * SPAN] = total
    for k in range(4):
        lanes = slice(k * FC, (k + 1) * FC)
        mine, near = jnp.zeros((FC, FC), F32), jnp.zeros((FC, FC), F32)
        for c in range(PARTS):
            mine += nt(xfull[feat, :, c * SPAN:(c + 1) * SPAN], gr[k, c])
            near += nt(av[feat, c], gr[k, c])
        wgrad[0:FC, lanes] = mine
        wgrad[FC:2 * FC, lanes] = near
    for c in range(PARTS):
        for k in ORDER:
            shop(c, k, True).wait_recv()
            shop(c, k).wait_send()
            for what in range(2):
                hop(c, k, what).wait_send()


def dense(part, xfull, wfull, wself, wneigh, cot):
    dma = pltpu.SemaphoreType.DMA
    return pl.pallas_call(
        dense_kernel,
        out_shape=(
            jax.ShapeDtypeStruct((FC, ROWS), F32),
            OUT((FC, ROWS), F32),
            OUT((NX, TPN, FC, TILE), BF),
            OUT((2 * FC, 4 * FC), F32),
        ),
        in_specs=[VMEM] * 6,
        out_specs=(VMEM,) * 4,
        scratch_shapes=[
            pltpu.VMEM((PARTS, 3, TPN // PARTS, FC, TILE), jnp.int16), pltpu.VMEM((PARTS, 3, 8, TILE), F32),
            pltpu.VMEM((PARTS, 3, TPN // PARTS, FC, TILE), jnp.int16), pltpu.VMEM((PARTS, 3, 8, TILE), F32),
            pltpu.VMEM((4, PARTS, FC, ROWS // PARTS), BF), pltpu.VMEM((4, PARTS, FC, ROWS // PARTS), BF),
            dma((6 * PARTS,)), dma((6 * PARTS,)), dma((PARTS, 3, 2)), dma((PARTS, 3, 2)),
            dma((PARTS, 3)), dma((PARTS, 3)),
        ],
        compiler_params=pltpu.CompilerParams(
            collective_id=1, has_side_effects=True, vmem_limit_bytes=24 * 2**20
        ),
        name="dense",
    )(part, xfull, wfull, wself, wneigh, cot)


def backward_kernel(slots, edges, source, act, out, acted, acc):
    acted[...] = act[...]
    acc[...] = jnp.zeros_like(acc)
    count = slots[LISTED, 0]

    def group(g, _):
        for u in range(0, UNROLL, 2):
            row, one, first = entry(slots, g, u, edges)
            _, two, second = entry(slots, g, u + 1, edges)
            sums = nt(
                source[lax.shift_right_logical(row, 3), jnp.bitwise_and(row, 7)],
                jnp.concatenate([first, second], axis=0),
            )
            acc[one] += sums[:, 0:TILE]
            acc[two] += sums[:, TILE:2 * TILE]
        return 0

    lax.fori_loop(0, (count + UNROLL - 1) // UNROLL, group, 0)
    for y in range(NY):
        for z in range(NZ):
            base = (y * NZ + z) * TPN
            out[y, z] = acc[base:base + TPN].astype(BF)


def backward(slots, edges, source, act):
    return pl.pallas_call(
        backward_kernel,
        out_shape=(OUT((NY, NZ, TPN, FC, TILE), BF), jax.ShapeDtypeStruct((FC, ROWS), F32)),
        in_specs=[SMEM, VMEM, VMEM, VMEM],
        out_specs=(VMEM, VMEM),
        scratch_shapes=[pltpu.VMEM((NY * NZ * TPN, FC, TILE), F32)],
        compiler_params=pltpu.CompilerParams(vmem_limit_bytes=24 * 2**20),
        name="backward_sums",
    )(slots, edges, source, act)


W_AT = ((4, 0), (3, 0), (2, 0))
NEAR = 3


def scatter_kernel(part, wgrad, direct, out, wout, rz, ry, rl, w1, w2, w3, w4, zs, zr, ys, yr, ws, wr):
    y, z, x, feat = place()
    oy = 1 - y
    FAR = TPN - NEAR

    def zof(k):
        return lax.rem(z + k + 2 * NZ, NZ)

    def zdev(s):
        return (node_of(y, zof(s), x), feat)

    plane = y * NX + x

    def pdev(k):
        p = lax.rem(plane + k, NY * NX)
        return (node_of(p // NX, z, lax.rem(p, NX)), feat)

    meet([zdev(k) for k in range(1, NZ)] + [pdev(k) for k in range(1, NY * NX)])
    ydev = (node_of(oy, z, x), feat)

    def term(u, k):
        if u == 2:
            return ry.at[(k + NZ) % NZ]
        return part.at[oy if u == 1 else y, zof(k), pl.ds(0, NEAR)]

    def size(u):
        return FAR if u == 2 else NEAR

    def cut(u, k):
        return pl.ds(0, 2) if k == 0 else pl.ds(2, size(u) - 2)

    def slot(s, u, d):
        return rz.at[side(s), u, d - 1, pl.ds(0, size(u))]

    def hop(s, u, d):
        i = (side(s), u, d - 1)
        src, dst = term(u, 4) if d == 4 else slot(s, u, d + 1), slot(s, u, d)
        if d == 4:
            src, dst = src.at[cut(u, side(s))], dst.at[cut(u, side(s))]
        return remote(src, dst, zs.at[i], zr.at[i], zdev(s))

    def yhop(k):
        return remote(part.at[oy, zof(k), pl.ds(NEAR, FAR)], ry.at[(k + NZ) % NZ],
                      ys.at[(k + NZ) % NZ], yr.at[(k + NZ) % NZ], ydev)

    def join(k):
        yhop(k).wait_recv()
        at = (k + NZ) % NZ
        ry[at] = (ry[at].astype(F32) + part[y, zof(k), NEAR:TPN].astype(F32)).astype(BF)

    last = remote(slot(1, 1, 1), rl, ys.at[NZ], yr.at[NZ], ydev)

    def rows(p):
        return pl.ds(pl.multiple_of(p * 16, 16), 16)

    def pof(k):
        return lax.rem(plane + k + NY * NX, NY * NX)

    def wcopy(phase, k):
        i = phase * 7 + k - 1
        peer = pdev(k) if phase in (0, 3) else zdev(k)
        src, dst = (
            (wgrad.at[rows(pof(k))], w1.at[k - 1]), (w2.at[zof(k)], w3.at[k - 1]), (w4.at[z], w4.at[z]),
            (wout.at[rows(plane)], wout.at[rows(plane)]),
        )[phase]
        return remote(src, dst, ws.at[i], wr.at[i], peer)

    def wexpect(phase, k):
        i = phase * 7 + k - 1
        dst = (w1.at[k - 1], w3.at[k - 1], w4.at[zof(-k)], wout.at[rows(pof(-k))])[phase]
        return remote(dst, dst, ws.at[i], wr.at[i], zdev(k))

    def wturn(phase):
        for k in range(1, 8):
            wexpect(phase, k).wait_recv()
        if phase == 0:
            acc = wgrad[rows(plane)]
            for k in range(1, 8):
                acc += w1[k - 1]
            for q in range(NZ):
                w2[q] = acc[2 * q:2 * q + 2]
        elif phase == 1:
            acc = w2[z]
            for k in range(1, 8):
                acc += w3[k - 1]
            w4[z] = acc
        else:
            wout[rows(plane)] = jnp.concatenate([w4[q] for q in range(NZ)], axis=0)
        for k in range(1, 8):
            wcopy(phase + 1, k).start()

    for k in range(1, 8):
        wcopy(0, k).start()
    for k in (4, 3, -3):
        yhop(k).start()
    for u in (1, 0):
        for s in BOTH:
            hop(s, u, 4).start()
    for k in (2, -2, 1, -1, 0):
        yhop(k).start()
    join(4)
    for s in BOTH:
        hop(s, 2, 4).start()
    for d in (4, 3, 2):
        for u in (1, 0, 2):
            if u == 2:
                join(d - 1)
                join(1 - d)
            for s in BOTH:
                hop(s, u, d).wait_recv()
                i = (side(s), u, d - 1)
                more = term(u, s * (d - 1))
                if d == 4:
                    a, b = cut(u, side(s)), cut(u, 1 - side(s))
                    rz[(*i, a)] = (rz[(*i, a)].astype(F32) + more[a].astype(F32)).astype(BF)
                    rz[(*i, b)] = more[b]
                else:
                    i = (*i, slice(0, size(u)))
                    rz[i] = (rz[i].astype(F32) + more[...].astype(F32)).astype(BF)
                hop(s, u, d - 1).start()
            if (d, u) in W_AT:
                wturn(W_AT.index((d, u)))

    def total(u):
        for s in BOTH:
            hop(s, u, 1).wait_recv()
        one, two = rz[0, u, 0, 0:size(u)].astype(F32), rz[1, u, 0, 0:size(u)].astype(F32)
        return term(u, 0)[...].astype(F32) + one + two

    perm = order()

    def finish(base, sums):
        flat = sums.reshape(-1, TILE)
        high = flat.astype(BF)
        back = dot(high, perm) + dot((flat - high.astype(F32)).astype(BF), perm)
        for t in range(sums.shape[0]):
            lanes = slice((base + t) * TILE, (base + t + 1) * TILE)
            out[:, lanes] = direct[:, lanes] + back[t * FC:(t + 1) * FC]

    rz[0, 1, 0, 0:NEAR] = total(1).astype(BF)
    last.start()
    join(0)
    finish(NEAR, total(2))
    sums = total(0)
    last.wait_recv()
    finish(0, sums + rl[...].astype(F32))
    for k in range(1, NZ):
        wexpect(3, k).wait_recv()
    for s in BOTH:
        for u in range(3):
            for d in range(1, 5):
                hop(s, u, d).wait_send()
    for k in range(NZ):
        yhop(k).wait_send()
    last.wait_send()
    for phase in range(4):
        for k in range(1, 8):
            wcopy(phase, k).wait_send()


def scatter(part, wgrad, direct):
    dma = pltpu.SemaphoreType.DMA
    return pl.pallas_call(
        scatter_kernel,
        out_shape=(
            jax.ShapeDtypeStruct((FC, ROWS), F32),
            jax.ShapeDtypeStruct((2 * FC, 4 * FC), F32),
        ),
        in_specs=[VMEM, VMEM, VMEM],
        out_specs=(VMEM, VMEM),
        scratch_shapes=[
            pltpu.VMEM((2, 3, 4, TPN - NEAR, FC, TILE), BF),
            pltpu.VMEM((NZ, TPN - NEAR, FC, TILE), BF),
            pltpu.VMEM((NEAR, FC, TILE), BF),
            pltpu.VMEM((NZ - 1, 16, 256), F32),
            pltpu.VMEM((NZ, 2, 256), F32), pltpu.VMEM((NZ - 1, 2, 256), F32), pltpu.VMEM((NZ, 2, 256), F32),
            dma((2, 3, 4)), dma((2, 3, 4)), dma((NZ + 1,)), dma((NZ + 1,)), dma((28,)), dma((28,)),
        ],
        compiler_params=pltpu.CompilerParams(
            collective_id=2, has_side_effects=True, vmem_limit_bytes=24 * 2**20
        ),
        name="scatter",
    )(part, wgrad, direct)


def local(features, w_self, w_neigh, tile_rows, tile_cols, tile_count, edge_bits, cotangent):
    rows, cols = tile_rows.reshape(2, TILE), tile_cols.reshape(2, TILE)
    given = [
        pltpu.with_memory_space_constraint(a, pltpu.HBM)
        for a in (features.T, w_self, w_neigh, rows, cols, edge_bits)
    ]
    full, xfull, wfull, edges, slots = gather(*given[:5], tile_count, given[5])
    part = forward(slots, edges, full)
    act, direct, scaled, wgrad = dense(part, xfull, wfull, w_self, w_neigh, cotangent.T)
    part, act = backward(slots, edges, scaled, act)
    grad, wsum = scatter(part, wgrad, direct)
    return act.T, grad.T, wsum[:FC], wsum[FC:]


def solution(mesh):
    placed = (
        P("node", "feat"),
        P("feat", None),
        P("feat", None),
        P("node"),
        P("node"),
        P("node"),
        P("node", None, None),
        P("node", "feat"),
    )
    return jax.shard_map(
        local,
        mesh=mesh,
        in_specs=placed,
        out_specs=(P("node", "feat"), P("node", "feat"), P("feat", None), P("feat", None)),
        check_vma=False,
    )
```

```python
import jax
import jax.numpy as jnp
from jax import lax
from jax.experimental import pallas as pl
from jax.experimental.pallas import tpu as pltpu
from jax.sharding import PartitionSpec as P

MESH = pl.DeviceIdType.MESH
BF = jnp.bfloat16
F32 = jnp.float32
NY, NZ, NX = 2, 8, 4
TPN = 8
FC = 64
TILE = 128
ROWS = TPN * TILE
SLOTS = 256
WORDS = 16
LISTED = 9
CNT = 16
BOTH = (1, -1)
PARTS = 4
UNROLL = 32
TURNS = TILE // UNROLL
HBM = pl.BlockSpec(memory_space=pltpu.HBM)
VMEM = pl.BlockSpec(memory_space=pltpu.VMEM)
SMEM = pl.BlockSpec(memory_space=pltpu.SMEM)
OUT = pltpu.VMEM


def place():
    node, feat = lax.axis_index("node"), lax.axis_index("feat")
    return node // (NZ * NX), lax.rem(node // NX, NZ), lax.rem(node, NX), feat


def side(s):
    return 0 if s > 0 else 1


def node_of(y, z, x):
    return (y * NZ + z) * NX + x


def across(feat):
    return lax.rem(feat + 2, 4)


def sibling(feat):
    return feat + 1 - 2 * lax.rem(feat, 2)


def meet(peers):
    barrier = pltpu.get_barrier_semaphore()
    for peer in peers:
        pl.semaphore_signal(barrier, inc=1, device_id=peer, device_id_type=MESH)
    pl.semaphore_wait(barrier, len(peers))


def remote(src, dst, send, recv, peer):
    return pltpu.make_async_remote_copy(
        src_ref=src, dst_ref=dst, send_sem=send, recv_sem=recv, device_id=peer, device_id_type=MESH
    )


def exchange(mine, slot, feat, node, sems, send, recv):
    one, two = (node, across(feat)), (node, sibling(feat))
    far, near = across(feat), sibling(feat)
    diag = across(near)
    a = remote(mine, slot(feat), send.at[sems], recv.at[sems], one)
    b = remote(mine, slot(feat), send.at[sems + 1], recv.at[sems + 1], two)
    c = remote(slot(far), slot(far), send.at[sems + 2], recv.at[sems + 2], two)
    a.start()
    b.start()

    def step():
        remote(slot(far), slot(far), send.at[sems], recv.at[sems], one).wait_recv()
        c.start()

    def finish():
        remote(slot(near), slot(near), send.at[sems + 1], recv.at[sems + 1], two).wait_recv()
        remote(slot(diag), slot(diag), send.at[sems + 2], recv.at[sems + 2], two).wait_recv()
        a.wait_send()
        b.wait_send()
        c.wait_send()

    return step, finish


def dot(a, b):
    return jnp.dot(a, b, preferred_element_type=F32)


def nt(a, b):
    return lax.dot_general(a, b, (((1,), (1,)), ((), ())), preferred_element_type=F32)


def iota(shape, dim):
    return lax.broadcasted_iota(jnp.int32, shape, dim)


def order():
    old = iota((TILE, TILE), 1)
    new = jnp.bitwise_and(old, 7) * WORDS + lax.shift_right_logical(old, 3)
    return (iota((TILE, TILE), 0) == new).astype(F32).astype(BF)


ORDER = (
    "s0", "s1", "s2", "s3", "z21", "y", "z01", "e0", "z11", "e1", "z22", "z02", "c",
    "l0", "l1", "l2", "e2", "z12", "l3", "l4", "x", "z23", "e3", "l5", "z03", "h0",
    "l6", "z13", "l7", "i", "z24", "h1", "z04", "z14",
)


def gather_kernel(feats, wself, wneigh, rows, cols, count, words, full, xfull, wfull, edges, listed,
                  raw, ids, codes, marks,
                  zs, zr, es, er, bs, br, cs, cr, ys, yr, fs, fr, ls):
    y, z, x, feat = place()
    node = node_of(y, z, x)
    oy = 1 - y
    HALF = TPN // 2

    def zof(k):
        return lax.rem(z + k + 2 * NZ, NZ)

    def xof(k):
        return lax.rem(x + k + 2 * NX, NX)

    def zdev(s):
        return (node_of(y, zof(s), x), feat)

    def xdev(s):
        return (node_of(y, z, xof(s)), feat)

    ydev = (node_of(oy, z, x), feat)
    beside = (node, sibling(feat))
    peers = [zdev(1), zdev(-1), xdev(1), xdev(-1), xdev(2), ydev, (node, across(feat)), beside]
    barrier = pltpu.get_barrier_semaphore()
    for peer in peers:
        pl.semaphore_signal(barrier, inc=1, device_id=peer, device_id_type=MESH)

    half = lax.rem(feat, 2) * (SLOTS // 2)
    other = SLOTS // 2 - half
    PART = SLOTS // 8

    def load(c):
        base = half + c * PART if c < 4 else other
        span = pl.ds(base, PART if c < 4 else SLOTS // 2)
        return pltpu.make_async_copy(words.at[span], raw.at[span], ls.at[c])

    small = [
        pltpu.make_async_copy(a, b, ls.at[5 + i])
        for i, (a, b) in enumerate((
            (feats, xfull.at[feat]), (wself, wfull.at[feat, 0]), (wneigh, wfull.at[feat, 1]),
            (rows, ids.at[0]), (cols, ids.at[1]),
        ))
    ]
    small[0].start()
    for c in range(5):
        load(c).start()
    for copy in small[1:]:
        copy.start()
    perm = order()
    small[0].wait()
    for t in range(TPN):
        full[y, z, t] = nt(xfull[feat, :, t * TILE:(t + 1) * TILE], perm).astype(BF)
    for i in range(4):
        load(i).wait()
        span = pl.ds(half + i * PART, PART)
        edges[x, span] = raw[span].astype(jnp.int16)
    for copy in small[3:]:
        copy.wait()
    at = iota((2, TILE), 0) * TILE + iota((2, TILE), 1)
    codes[...] = jnp.full_like(codes, -1)
    codes[0:2] = jnp.where(at < count[0], ids[0] * 65536 + ids[1], -1)
    marks[x] = codes[...]
    pl.semaphore_wait(barrier, len(peers))

    def block(u, zr, d, s):
        base = (0, 0, HALF)[u] + (side(s) * (HALF // 2) if d == 4 else 0)
        return full.at[oy if u == 1 else y, zof(zr), pl.ds(base, HALF // 2 if d == 4 else HALF)]

    def zhop(s, u, d, arriving=False):
        i = (side(s), u, d - 1)
        at = block(u, -s * d if arriving else -s * (d - 1), d, s)
        return remote(at, at, zs.at[i], zr.at[i], zdev(s))

    def yhop(s, d, arriving=False):
        i = d if d < 1 else 1 + side(s) * 4 + d - 1
        i = 9 if d < 0 else i
        who = oy if arriving else y
        base = 0 if d < 0 else HALF
        base = base + (side(s) * (HALF // 2) if d == 4 else 0)
        at = full.at[who, zof(-s * max(d, 0)), pl.ds(base, HALF // 2 if d == 4 else HALF)]
        return remote(at, at, ys.at[i], yr.at[i], ydev)

    def ehop(s, c, d, arriving=False):
        i = (side(s), c, d - 1)
        at = edges.at[xof(-s * d if arriving else -s * (d - 1)), pl.ds(half + c * PART, PART)]
        return remote(at, at, es.at[i], er.at[i], xdev(s))

    def ehand(s, c, d, arriving=False):
        i = (side(s), c, d - 1)
        at = edges.at[xof(-s * d), pl.ds((other if arriving else half) + c * PART, PART)]
        return remote(at, at, bs.at[i], br.at[i], beside)

    def nth(s, i):
        return i if s > 0 else (i + 2) % 4

    def chop(k, arriving=False):
        at = marks.at[xof(-k) if arriving else x]
        return remote(codes if not arriving else at, at, cs.at[k - 1], cr.at[k - 1], xdev(k))

    yhop(1, -1).start()
    for s in BOTH:
        zhop(s, 2, 1).start()
        zhop(s, 0, 1).start()
    for k in range(1, NX):
        chop(k).start()
    yhop(1, 0).start()
    xstep, xfinish = exchange(feats, lambda k: xfull.at[k], feat, node, 0, fs, fr)
    wstep, wfinish = exchange(wself, lambda k: wfull.at[k, 0], feat, node, 3, fs, fr)
    vstep, vfinish = exchange(wneigh, lambda k: wfull.at[k, 1], feat, node, 6, fs, fr)
    small[1].wait()
    small[2].wait()

    def zpass(u, d):
        for s in BOTH:
            zhop(s, u, d, True).wait_recv()
            if d < 4:
                zhop(s, u, d + 1).start()
            if u == 2:
                yhop(s, d).start()

    def eround(i):
        for s in BOTH:
            c = nth(s, i)
            ehop(s, c, 1, True).wait_recv()
            if i < 2:
                ehop(s, c, 2).start()
            ehand(s, c, 1).start()

    def efar(i):
        for s in BOTH:
            c = nth(s, i)
            ehop(s, c, 2, True).wait_recv()
            ehand(s, c, 2).start()

    def efirst(i):
        for s in BOTH:
            ehop(s, nth(s, i), 1).start()

    def ycross():
        yhop(1, -1, True).wait_recv()
        for s in BOTH:
            zhop(s, 1, 1).start()

    def passon():
        for step in (xstep, wstep, vstep):
            step()

    state = {}

    def prepare():
        load(4).wait()
        span = pl.ds(other, SLOTS // 2)
        edges[x, span] = raw[span].astype(jnp.int16)
        for k in range(1, NX):
            chop(k, True).wait_recv()
        code = jnp.concatenate([marks[b, 0:2] for b in range(NX)], axis=0)
        col = jnp.bitwise_and(code, 511)
        mine = jnp.where(
            jnp.logical_and(code >= 0, jnp.bitwise_and(lax.shift_right_logical(col, 3), 3) == x), 1.0, 0.0
        )
        slot = iota((8, TILE), 0) * TILE + iota((8, TILE), 1)
        row = lax.shift_right_logical(slot, 8) * TPN + jnp.bitwise_and(lax.shift_right_arithmetic(code, 16), 7)
        near = lax.shift_left(lax.shift_right_logical(col, 5), 3) + jnp.bitwise_and(col, 7)
        upto = jnp.where(iota((TILE, TILE), 0) <= iota((TILE, TILE), 1), 1.0, 0.0).astype(BF)
        tile = jnp.bitwise_and(row, 7)
        runs, begin, places = [], jnp.zeros((1, TILE), F32), []
        for b in range(NX):
            seen = jnp.zeros((TPN, 1), F32)
            for r in (2 * b, 2 * b + 1):
                hot = jnp.where(iota((TPN, TILE), 0) == tile[r:r + 1], mine[r:r + 1], 0.0)
                rank = dot(hot.astype(BF), upto) + seen
                runs.append((hot, rank))
                seen = rank[:, TILE - 1:TILE]
            even = jnp.broadcast_to(2.0 * jnp.floor((seen + 1.0) * 0.5), (TPN, TILE))
            starts = []
            for j in range(TPN):
                starts.append(begin)
                begin = begin + even[j:j + 1]
            start = jnp.concatenate(starts, axis=0) - 1.0
            for r in (2 * b, 2 * b + 1):
                hot, rank = runs[r]
                place = jnp.sum(hot * (start + rank), axis=0, keepdims=True)
                places.append(jnp.where(mine[r:r + 1] > 0.0, place, -1.0e6))
        base = begin
        pos = jnp.concatenate(places + [jnp.zeros((TILE - 8, TILE), F32)], axis=0).T
        wide = iota((TILE, LISTED * TILE), 1).astype(F32)
        picked = jnp.zeros((8, LISTED * TILE), F32)
        fields = (jnp.bitwise_and(slot, 255), lax.shift_right_logical(slot, 8), row, near + 128)
        state.update(pos=pos, base=base, wide=wide, picked=picked, fields=fields)

    def pick(r):
        pos, wide, fields = state["pos"], state["wide"], state["fields"]
        hot = jnp.where(pos[:, r:r + 1] == wide, 1.0, 0.0).astype(BF)
        stack = jnp.concatenate([f[r:r + 1].astype(F32) for f in fields] + [jnp.zeros((4, TILE), F32)], axis=0)
        state["picked"] += dot(stack.astype(BF), hot)

    def enlist():
        picked, base = state["picked"], state["base"]
        items = (picked[0:1] + 256.0 * picked[1:2] + 1024.0 * picked[2:3] + 32768.0 * picked[3:4]).astype(jnp.int32)
        for r in range(LISTED):
            listed[r:r + 1] = items[:, r * TILE:(r + 1) * TILE]
        listed[LISTED:16] = jnp.broadcast_to(base, (16 - LISTED, TILE)).astype(jnp.int32)

    steps = {"z": zpass, "e": eround, "h": efar, "s": efirst, "y": ycross, "x": passon, "c": prepare, "l": pick, "i": enlist}
    for step in ORDER:
        steps[step[0]](*(int(digit) for digit in step[1:]))
    for s in BOTH:
        for i in range(4):
            c = nth(s, i)
            for d in (1, 2) if i < 2 else (1,):
                ehand(s, c, d, True).wait_recv()
                ehand(s, c, d).wait_send()
                ehop(s, c, d).wait_send()
        for d in range(1, 5):
            for u in range(3):
                zhop(s, u, d).wait_send()
            yhop(s, d, True).wait_recv()
            yhop(s, d).wait_send()
    yhop(1, 0, True).wait_recv()
    yhop(1, 0).wait_send()
    yhop(1, -1).wait_send()
    for k in range(1, NX):
        chop(k).wait_send()
    xfinish()
    wfinish()
    vfinish()


def gather(feats, wself, wneigh, rows, cols, count, words):
    dma = pltpu.SemaphoreType.DMA
    return pl.pallas_call(
        gather_kernel,
        out_shape=(
            OUT((NY, NZ, TPN, FC, TILE), BF),
            OUT((4, FC, ROWS), BF),
            OUT((4, 2, FC, 4 * FC), BF),
            OUT((NX, *words.shape), jnp.int16),
            jax.ShapeDtypeStruct((16, TILE), jnp.int32),
        ),
        in_specs=[HBM] * 5 + [SMEM, HBM],
        out_specs=(VMEM,) * 5,
        scratch_shapes=[
            pltpu.VMEM(words.shape, jnp.int32), pltpu.VMEM((2, 2, TILE), jnp.int32),
            pltpu.VMEM((8, TILE), jnp.int32), pltpu.VMEM((NX, 8, TILE), jnp.int32),
            dma((2, 3, 4)), dma((2, 3, 4)), dma((2, 4, 2)), dma((2, 4, 2)), dma((2, 4, 2)), dma((2, 4, 2)),
            dma((3,)), dma((3,)), dma((10,)), dma((10,)), dma((9,)), dma((9,)), dma((10,)),
        ],
        compiler_params=pltpu.CompilerParams(
            collective_id=0, has_side_effects=True, vmem_limit_bytes=24 * 2**20
        ),
        name="gather",
    )(feats, wself, wneigh, rows, cols, count, words)


def planes_of(words):
    one, zero = jnp.ones(words.shape, BF), jnp.zeros(words.shape, BF)
    return jnp.concatenate(
        [jnp.where(jnp.bitwise_and(words, jnp.int16(1 << b)) != 0, one, zero) for b in range(8)], axis=0
    )


def entry(slots, group, u, edges):
    item = slots[group // TURNS, lax.rem(group, TURNS) * UNROLL + u]
    words = edges[jnp.bitwise_and(lax.shift_right_logical(item, 8), 3), jnp.bitwise_and(item, 255)]
    planes = planes_of(jnp.where(item > 0, words, jnp.zeros_like(words)))
    row, col = lax.shift_right_logical(item, 10), lax.shift_right_logical(item, 15)
    return jnp.bitwise_and(row, 31), jnp.bitwise_and(col, 127), planes


def forward_kernel(slots, edges, full, acc):
    acc[...] = jnp.zeros_like(acc)
    count = slots[LISTED, 0]
    ones = jnp.ones((CNT, TILE), BF)

    def source(col):
        near, t = lax.shift_right_logical(col, 3), jnp.bitwise_and(col, 7)
        return jnp.concatenate([full[lax.shift_right_logical(near, 3), jnp.bitwise_and(near, 7), t], ones], axis=0)

    def group(g, _):
        for u in range(0, UNROLL, 2):
            row, one, first = entry(slots, g, u, edges)
            _, two, second = entry(slots, g, u + 1, edges)
            acc[lax.shift_right_logical(row, 3), jnp.bitwise_and(row, 7)] += dot(
                jnp.concatenate([source(one), source(two)], axis=1), jnp.concatenate([first, second], axis=0)
            )
        return 0

    lax.fori_loop(0, (count + UNROLL - 1) // UNROLL, group, 0)


def forward(slots, edges, full):
    return pl.pallas_call(
        forward_kernel,
        out_shape=OUT((NX, TPN, FC + CNT, TILE), F32),
        in_specs=[SMEM, VMEM, VMEM],
        out_specs=VMEM,
        compiler_params=pltpu.CompilerParams(vmem_limit_bytes=24 * 2**20),
        name="forward_sums",
    )(slots, edges, full)


DENSE = (
    "a0", "a1", "b0", "a2", "b1", "g0", "a3", "b2", "g1", "h0",
    "b3", "g2", "h1", "s0", "g3", "h2", "s1", "h3", "s2", "s3",
)


def dense_kernel(part, xfull, wfull, wself, wneigh, cot, act, direct, scaled, wgrad,
                 pq, pm, rq, rm, av, gr, send, recv, rs, rr, ss, sr):
    y, z, x, feat = place()
    node = node_of(y, z, x)
    CT = TPN // PARTS
    SPAN = ROWS // PARTS

    def xof(k):
        return lax.rem(x + k + 2 * NX, NX)

    def xdev(s):
        return (node_of(y, z, xof(s)), feat)

    peers = [xdev(1), xdev(-1), xdev(2), (node, across(feat)), (node, sibling(feat))]
    barrier = pltpu.get_barrier_semaphore()
    for peer in peers:
        pl.semaphore_signal(barrier, inc=1, device_id=peer, device_id_type=MESH)

    def pack(c, k):
        block = xof(k)
        for q in range(CT):
            r = c * CT + q
            sums = part[block, r, 0:FC]
            most = jnp.maximum(jnp.max(jnp.abs(sums), axis=0, keepdims=True), 1e-30)
            pq[c, k - 1, q] = jnp.round(sums * (32766.0 / most)).astype(jnp.int32).astype(jnp.int16)
            pm[c, k - 1, q:q + 1] = most * (1.0 / 32766.0)
            pm[c, k - 1, CT + q:CT + q + 1] = part[block, r, FC:FC + 1]

    def hop(c, k, what):
        i = (c, k - 1, what)
        src, dst = ((pq, rq), (pm, rm))[what]
        return remote(src.at[c, k - 1], dst.at[c, k - 1], rs.at[i], rr.at[i], xdev(k))

    ORDER = (2, 1, 3)
    for k in ORDER:
        pack(0, k)
    pl.semaphore_wait(barrier, len(peers))
    for c in range(PARTS):
        for k in ORDER:
            if c > 0:
                pack(c, k)
            hop(c, k, 1).start()
            hop(c, k, 0).start()

    choose = (iota((FC, 4 * FC), 1) == iota((FC, 4 * FC), 0) + feat * FC).astype(F32).astype(BF)

    def cols_of(k, which):
        return nt(choose, wfull[k, which]).astype(BF)

    pre = dot(cols_of(0, 0), xfull[0])
    for k in range(1, 4):
        pre += dot(cols_of(k, 0), xfull[k])
    neigh = [cols_of(k, 1) for k in range(4)]

    def share(ref, stage, c):
        return exchange(
            ref.at[feat, c], lambda k: ref.at[k, c], feat, node, 3 * (stage * PARTS + c), send, recv
        )

    degrees, first, second = {}, {}, {}

    def average(c):
        for k in ORDER:
            for what in (1, 0):
                hop(c, k, what).wait_recv()
        for q in range(CT):
            r = c * CT + q
            total = part[x, r, 0:FC]
            degree = part[x, r, FC:FC + 1]
            for k in range(3):
                total += rq[c, k, q].astype(jnp.int32).astype(F32) * rm[c, k, q:q + 1]
                degree += rm[c, k, CT + q:CT + q + 1]
            degrees[r] = jnp.maximum(degree, 1.0)
            av[feat, c, :, q * TILE:(q + 1) * TILE] = (total / degrees[r]).astype(BF)
        first[c] = share(av, 0, c)

    def gradient(c):
        first[c][1]()
        span = slice(c * SPAN, (c + 1) * SPAN)
        own = pre[:, span]
        for k in range(4):
            own += dot(neigh[k], av[k, c])
        sig = jax.nn.sigmoid(own)
        grad = cot[:, span] * sig * (1.0 + own * (1.0 - sig))
        gr[feat, c] = grad.astype(BF)
        second[c] = share(gr, 1, c)
        act[:, span] = own * sig

    def shop(c, k, arriving=False):
        at = scaled.at[xof(-k) if arriving else x, pl.ds(c * CT, CT)]
        return remote(at, at, ss.at[c, k - 1], sr.at[c, k - 1], xdev(k))

    def scale(c):
        second[c][1]()
        sums = dot(wneigh[:, 0:FC], gr[0, c])
        for k in range(1, 4):
            sums += dot(wneigh[:, k * FC:(k + 1) * FC], gr[k, c])
        for q in range(CT):
            r = c * CT + q
            scaled[x, r] = (sums[:, q * TILE:(q + 1) * TILE] / degrees[r]).astype(BF)
        for k in ORDER:
            shop(c, k).start()

    steps = {
        "a": average, "b": lambda c: first[c][0](), "g": gradient, "h": lambda c: second[c][0](), "s": scale
    }
    for step in DENSE:
        steps[step[0]](int(step[1]))
    for c in range(PARTS):
        total = dot(wself[:, 0:FC], gr[0, c])
        for k in range(1, 4):
            total += dot(wself[:, k * FC:(k + 1) * FC], gr[k, c])
        direct[:, c * SPAN:(c + 1) * SPAN] = total
    for k in range(4):
        lanes = slice(k * FC, (k + 1) * FC)
        mine, near = jnp.zeros((FC, FC), F32), jnp.zeros((FC, FC), F32)
        for c in range(PARTS):
            mine += nt(xfull[feat, :, c * SPAN:(c + 1) * SPAN], gr[k, c])
            near += nt(av[feat, c], gr[k, c])
        wgrad[0:FC, lanes] = mine
        wgrad[FC:2 * FC, lanes] = near
    for c in range(PARTS):
        for k in ORDER:
            shop(c, k, True).wait_recv()
            shop(c, k).wait_send()
            for what in range(2):
                hop(c, k, what).wait_send()


def dense(part, xfull, wfull, wself, wneigh, cot):
    dma = pltpu.SemaphoreType.DMA
    return pl.pallas_call(
        dense_kernel,
        out_shape=(
            jax.ShapeDtypeStruct((FC, ROWS), F32),
            OUT((FC, ROWS), F32),
            OUT((NX, TPN, FC, TILE), BF),
            OUT((2 * FC, 4 * FC), F32),
        ),
        in_specs=[VMEM] * 6,
        out_specs=(VMEM,) * 4,
        scratch_shapes=[
            pltpu.VMEM((PARTS, 3, TPN // PARTS, FC, TILE), jnp.int16), pltpu.VMEM((PARTS, 3, 8, TILE), F32),
            pltpu.VMEM((PARTS, 3, TPN // PARTS, FC, TILE), jnp.int16), pltpu.VMEM((PARTS, 3, 8, TILE), F32),
            pltpu.VMEM((4, PARTS, FC, ROWS // PARTS), BF), pltpu.VMEM((4, PARTS, FC, ROWS // PARTS), BF),
            dma((6 * PARTS,)), dma((6 * PARTS,)), dma((PARTS, 3, 2)), dma((PARTS, 3, 2)),
            dma((PARTS, 3)), dma((PARTS, 3)),
        ],
        compiler_params=pltpu.CompilerParams(
            collective_id=1, has_side_effects=True, vmem_limit_bytes=24 * 2**20
        ),
        name="dense",
    )(part, xfull, wfull, wself, wneigh, cot)


def backward_kernel(slots, edges, source, act, out, acted, acc):
    acted[...] = act[...]
    acc[...] = jnp.zeros_like(acc)
    count = slots[LISTED, 0]

    def group(g, _):
        for u in range(0, UNROLL, 2):
            row, one, first = entry(slots, g, u, edges)
            _, two, second = entry(slots, g, u + 1, edges)
            sums = nt(
                source[lax.shift_right_logical(row, 3), jnp.bitwise_and(row, 7)],
                jnp.concatenate([first, second], axis=0),
            )
            acc[one] += sums[:, 0:TILE]
            acc[two] += sums[:, TILE:2 * TILE]
        return 0

    lax.fori_loop(0, (count + UNROLL - 1) // UNROLL, group, 0)
    for y in range(NY):
        for z in range(NZ):
            base = (y * NZ + z) * TPN
            out[y, z] = acc[base:base + TPN].astype(BF)


def backward(slots, edges, source, act):
    return pl.pallas_call(
        backward_kernel,
        out_shape=(OUT((NY, NZ, TPN, FC, TILE), BF), jax.ShapeDtypeStruct((FC, ROWS), F32)),
        in_specs=[SMEM, VMEM, VMEM, VMEM],
        out_specs=(VMEM, VMEM),
        scratch_shapes=[pltpu.VMEM((NY * NZ * TPN, FC, TILE), F32)],
        compiler_params=pltpu.CompilerParams(vmem_limit_bytes=24 * 2**20),
        name="backward_sums",
    )(slots, edges, source, act)


W_AT = ((4, 0), (3, 0), (2, 0))
NEAR = 3


def scatter_kernel(part, wgrad, direct, out, wout, rz, ry, rl, w1, w2, w3, w4, zs, zr, ys, yr, ws, wr):
    y, z, x, feat = place()
    oy = 1 - y
    FAR = TPN - NEAR

    def zof(k):
        return lax.rem(z + k + 2 * NZ, NZ)

    def zdev(s):
        return (node_of(y, zof(s), x), feat)

    plane = y * NX + x

    def pdev(k):
        p = lax.rem(plane + k, NY * NX)
        return (node_of(p // NX, z, lax.rem(p, NX)), feat)

    meet([zdev(k) for k in range(1, NZ)] + [pdev(k) for k in range(1, NY * NX)])
    ydev = (node_of(oy, z, x), feat)

    def term(u, k):
        if u == 2:
            return ry.at[(k + NZ) % NZ]
        return part.at[oy if u == 1 else y, zof(k), pl.ds(0, NEAR)]

    def size(u):
        return FAR if u == 2 else NEAR

    def cut(u, k):
        return pl.ds(0, 2) if k == 0 else pl.ds(2, size(u) - 2)

    def slot(s, u, d):
        return rz.at[side(s), u, d - 1, pl.ds(0, size(u))]

    def hop(s, u, d):
        i = (side(s), u, d - 1)
        src, dst = term(u, 4) if d == 4 else slot(s, u, d + 1), slot(s, u, d)
        if d == 4:
            src, dst = src.at[cut(u, side(s))], dst.at[cut(u, side(s))]
        return remote(src, dst, zs.at[i], zr.at[i], zdev(s))

    def yhop(k):
        return remote(part.at[oy, zof(k), pl.ds(NEAR, FAR)], ry.at[(k + NZ) % NZ],
                      ys.at[(k + NZ) % NZ], yr.at[(k + NZ) % NZ], ydev)

    def join(k):
        yhop(k).wait_recv()
        at = (k + NZ) % NZ
        ry[at] = (ry[at].astype(F32) + part[y, zof(k), NEAR:TPN].astype(F32)).astype(BF)

    last = remote(slot(1, 1, 1), rl, ys.at[NZ], yr.at[NZ], ydev)

    def rows(p):
        return pl.ds(pl.multiple_of(p * 16, 16), 16)

    def pof(k):
        return lax.rem(plane + k + NY * NX, NY * NX)

    def wcopy(phase, k):
        i = phase * 7 + k - 1
        peer = pdev(k) if phase in (0, 3) else zdev(k)
        src, dst = (
            (wgrad.at[rows(pof(k))], w1.at[k - 1]), (w2.at[zof(k)], w3.at[k - 1]), (w4.at[z], w4.at[z]),
            (wout.at[rows(plane)], wout.at[rows(plane)]),
        )[phase]
        return remote(src, dst, ws.at[i], wr.at[i], peer)

    def wexpect(phase, k):
        i = phase * 7 + k - 1
        dst = (w1.at[k - 1], w3.at[k - 1], w4.at[zof(-k)], wout.at[rows(pof(-k))])[phase]
        return remote(dst, dst, ws.at[i], wr.at[i], zdev(k))

    def wturn(phase):
        for k in range(1, 8):
            wexpect(phase, k).wait_recv()
        if phase == 0:
            acc = wgrad[rows(plane)]
            for k in range(1, 8):
                acc += w1[k - 1]
            for q in range(NZ):
                w2[q] = acc[2 * q:2 * q + 2]
        elif phase == 1:
            acc = w2[z]
            for k in range(1, 8):
                acc += w3[k - 1]
            w4[z] = acc
        else:
            wout[rows(plane)] = jnp.concatenate([w4[q] for q in range(NZ)], axis=0)
        for k in range(1, 8):
            wcopy(phase + 1, k).start()

    for k in range(1, 8):
        wcopy(0, k).start()
    for k in (4, 3, -3):
        yhop(k).start()
    for u in (1, 0):
        for s in BOTH:
            hop(s, u, 4).start()
    for k in (2, -2, 1, -1, 0):
        yhop(k).start()
    join(4)
    for s in BOTH:
        hop(s, 2, 4).start()
    for d in (4, 3, 2):
        for u in (1, 0, 2):
            if u == 2:
                join(d - 1)
                join(1 - d)
            for s in BOTH:
                hop(s, u, d).wait_recv()
                i = (side(s), u, d - 1)
                more = term(u, s * (d - 1))
                if d == 4:
                    a, b = cut(u, side(s)), cut(u, 1 - side(s))
                    rz[(*i, a)] = (rz[(*i, a)].astype(F32) + more[a].astype(F32)).astype(BF)
                    rz[(*i, b)] = more[b]
                else:
                    i = (*i, slice(0, size(u)))
                    rz[i] = (rz[i].astype(F32) + more[...].astype(F32)).astype(BF)
                hop(s, u, d - 1).start()
            if (d, u) in W_AT:
                wturn(W_AT.index((d, u)))

    def total(u):
        for s in BOTH:
            hop(s, u, 1).wait_recv()
        one, two = rz[0, u, 0, 0:size(u)].astype(F32), rz[1, u, 0, 0:size(u)].astype(F32)
        return term(u, 0)[...].astype(F32) + one + two

    perm = order()

    def finish(base, sums):
        flat = sums.reshape(-1, TILE)
        high = flat.astype(BF)
        back = dot(high, perm) + dot((flat - high.astype(F32)).astype(BF), perm)
        for t in range(sums.shape[0]):
            lanes = slice((base + t) * TILE, (base + t + 1) * TILE)
            out[:, lanes] = direct[:, lanes] + back[t * FC:(t + 1) * FC]

    rz[0, 1, 0, 0:NEAR] = total(1).astype(BF)
    last.start()
    join(0)
    finish(NEAR, total(2))
    sums = total(0)
    last.wait_recv()
    finish(0, sums + rl[...].astype(F32))
    for k in range(1, NZ):
        wexpect(3, k).wait_recv()
    for s in BOTH:
        for u in range(3):
            for d in range(1, 5):
                hop(s, u, d).wait_send()
    for k in range(NZ):
        yhop(k).wait_send()
    last.wait_send()
    for phase in range(4):
        for k in range(1, 8):
            wcopy(phase, k).wait_send()


def scatter(part, wgrad, direct):
    dma = pltpu.SemaphoreType.DMA
    return pl.pallas_call(
        scatter_kernel,
        out_shape=(
            jax.ShapeDtypeStruct((FC, ROWS), F32),
            jax.ShapeDtypeStruct((2 * FC, 4 * FC), F32),
        ),
        in_specs=[VMEM, VMEM, VMEM],
        out_specs=(VMEM, VMEM),
        scratch_shapes=[
            pltpu.VMEM((2, 3, 4, TPN - NEAR, FC, TILE), BF),
            pltpu.VMEM((NZ, TPN - NEAR, FC, TILE), BF),
            pltpu.VMEM((NEAR, FC, TILE), BF),
            pltpu.VMEM((NZ - 1, 16, 256), F32),
            pltpu.VMEM((NZ, 2, 256), F32), pltpu.VMEM((NZ - 1, 2, 256), F32), pltpu.VMEM((NZ, 2, 256), F32),
            dma((2, 3, 4)), dma((2, 3, 4)), dma((NZ + 1,)), dma((NZ + 1,)), dma((28,)), dma((28,)),
        ],
        compiler_params=pltpu.CompilerParams(
            collective_id=2, has_side_effects=True, vmem_limit_bytes=24 * 2**20
        ),
        name="scatter",
    )(part, wgrad, direct)


def local(features, w_self, w_neigh, tile_rows, tile_cols, tile_count, edge_bits, cotangent):
    rows, cols = tile_rows.reshape(2, TILE), tile_cols.reshape(2, TILE)
    given = [
        pltpu.with_memory_space_constraint(a, pltpu.HBM)
        for a in (features.T, w_self, w_neigh, rows, cols, edge_bits)
    ]
    full, xfull, wfull, edges, slots = gather(*given[:5], tile_count, given[5])
    part = forward(slots, edges, full)
    act, direct, scaled, wgrad = dense(part, xfull, wfull, w_self, w_neigh, cotangent.T)
    part, act = backward(slots, edges, scaled, act)
    grad, wsum = scatter(part, wgrad, direct)
    return act.T, grad.T, wsum[:FC], wsum[FC:]


def solution(mesh):
    placed = (
        P("node", "feat"),
        P("feat", None),
        P("feat", None),
        P("node"),
        P("node"),
        P("node"),
        P("node", None, None),
        P("node", "feat"),
    )
    return jax.shard_map(
        local,
        mesh=mesh,
        in_specs=placed,
        out_specs=(P("node", "feat"), P("node", "feat"), P("feat", None), P("feat", None)),
        check_vma=False,
    )
```

```python
import jax
import jax.numpy as jnp
from jax import lax
from jax.experimental import pallas as pl
from jax.experimental.pallas import tpu as pltpu
from jax.sharding import PartitionSpec as P

MESH = pl.DeviceIdType.MESH
BF = jnp.bfloat16
F32 = jnp.float32
NY, NZ, NX = 2, 8, 4
TPN = 8
FC = 64
TILE = 128
ROWS = TPN * TILE
SLOTS = 256
WORDS = 16
LISTED = 9
CNT = 16
BOTH = (1, -1)
PARTS = 4
UNROLL = 64
TURNS = TILE // UNROLL
HBM = pl.BlockSpec(memory_space=pltpu.HBM)
VMEM = pl.BlockSpec(memory_space=pltpu.VMEM)
SMEM = pl.BlockSpec(memory_space=pltpu.SMEM)
OUT = pltpu.VMEM


def place():
    node, feat = lax.axis_index("node"), lax.axis_index("feat")
    return node // (NZ * NX), lax.rem(node // NX, NZ), lax.rem(node, NX), feat


def side(s):
    return 0 if s > 0 else 1


def node_of(y, z, x):
    return (y * NZ + z) * NX + x


def across(feat):
    return lax.rem(feat + 2, 4)


def sibling(feat):
    return feat + 1 - 2 * lax.rem(feat, 2)


def meet(peers):
    barrier = pltpu.get_barrier_semaphore()
    for peer in peers:
        pl.semaphore_signal(barrier, inc=1, device_id=peer, device_id_type=MESH)
    pl.semaphore_wait(barrier, len(peers))


def remote(src, dst, send, recv, peer):
    return pltpu.make_async_remote_copy(
        src_ref=src, dst_ref=dst, send_sem=send, recv_sem=recv, device_id=peer, device_id_type=MESH
    )


def exchange(mine, slot, feat, node, sems, send, recv):
    one, two = (node, across(feat)), (node, sibling(feat))
    far, near = across(feat), sibling(feat)
    diag = across(near)
    a = remote(mine, slot(feat), send.at[sems], recv.at[sems], one)
    b = remote(mine, slot(feat), send.at[sems + 1], recv.at[sems + 1], two)
    c = remote(slot(far), slot(far), send.at[sems + 2], recv.at[sems + 2], two)
    a.start()
    b.start()

    def step():
        remote(slot(far), slot(far), send.at[sems], recv.at[sems], one).wait_recv()
        c.start()

    def finish():
        remote(slot(near), slot(near), send.at[sems + 1], recv.at[sems + 1], two).wait_recv()
        remote(slot(diag), slot(diag), send.at[sems + 2], recv.at[sems + 2], two).wait_recv()
        a.wait_send()
        b.wait_send()
        c.wait_send()

    return step, finish


def dot(a, b):
    return jnp.dot(a, b, preferred_element_type=F32)


def nt(a, b):
    return lax.dot_general(a, b, (((1,), (1,)), ((), ())), preferred_element_type=F32)


def iota(shape, dim):
    return lax.broadcasted_iota(jnp.int32, shape, dim)


def order():
    old = iota((TILE, TILE), 1)
    new = jnp.bitwise_and(old, 7) * WORDS + lax.shift_right_logical(old, 3)
    return (iota((TILE, TILE), 0) == new).astype(F32).astype(BF)


ORDER = (
    "s0", "s1", "s2", "s3", "z21", "y", "z01", "e0", "z11", "e1", "z22", "z02", "c",
    "l0", "l1", "l2", "e2", "z12", "l3", "l4", "x", "z23", "e3", "l5", "z03", "h0",
    "l6", "z13", "l7", "i", "z24", "h1", "z04", "z14",
)


def gather_kernel(feats, wself, wneigh, rows, cols, count, words, full, xfull, wfull, edges, listed,
                  raw, ids, codes, marks,
                  zs, zr, es, er, bs, br, cs, cr, ys, yr, fs, fr, ls):
    y, z, x, feat = place()
    node = node_of(y, z, x)
    oy = 1 - y
    HALF = TPN // 2

    def zof(k):
        return lax.rem(z + k + 2 * NZ, NZ)

    def xof(k):
        return lax.rem(x + k + 2 * NX, NX)

    def zdev(s):
        return (node_of(y, zof(s), x), feat)

    def xdev(s):
        return (node_of(y, z, xof(s)), feat)

    ydev = (node_of(oy, z, x), feat)
    beside = (node, sibling(feat))
    peers = [zdev(1), zdev(-1), xdev(1), xdev(-1), xdev(2), ydev, (node, across(feat)), beside]
    barrier = pltpu.get_barrier_semaphore()
    for peer in peers:
        pl.semaphore_signal(barrier, inc=1, device_id=peer, device_id_type=MESH)

    half = lax.rem(feat, 2) * (SLOTS // 2)
    other = SLOTS // 2 - half
    PART = SLOTS // 8

    def load(c):
        base = half + c * PART if c < 4 else other
        span = pl.ds(base, PART if c < 4 else SLOTS // 2)
        return pltpu.make_async_copy(words.at[span], raw.at[span], ls.at[c])

    small = [
        pltpu.make_async_copy(a, b, ls.at[5 + i])
        for i, (a, b) in enumerate((
            (feats, xfull.at[feat]), (wself, wfull.at[feat, 0]), (wneigh, wfull.at[feat, 1]),
            (rows, ids.at[0]), (cols, ids.at[1]),
        ))
    ]
    small[0].start()
    for c in range(5):
        load(c).start()
    for copy in small[1:]:
        copy.start()
    perm = order()
    small[0].wait()
    for t in range(TPN):
        full[y, z, t] = nt(xfull[feat, :, t * TILE:(t + 1) * TILE], perm).astype(BF)
    for i in range(4):
        load(i).wait()
        span = pl.ds(half + i * PART, PART)
        edges[x, span] = raw[span].astype(jnp.int16)
    for copy in small[3:]:
        copy.wait()
    at = iota((2, TILE), 0) * TILE + iota((2, TILE), 1)
    codes[...] = jnp.full_like(codes, -1)
    codes[0:2] = jnp.where(at < count[0], ids[0] * 65536 + ids[1], -1)
    marks[x] = codes[...]
    pl.semaphore_wait(barrier, len(peers))

    def block(u, zr, d, s):
        base = (0, 0, HALF)[u] + (side(s) * (HALF // 2) if d == 4 else 0)
        return full.at[oy if u == 1 else y, zof(zr), pl.ds(base, HALF // 2 if d == 4 else HALF)]

    def zhop(s, u, d, arriving=False):
        i = (side(s), u, d - 1)
        at = block(u, -s * d if arriving else -s * (d - 1), d, s)
        return remote(at, at, zs.at[i], zr.at[i], zdev(s))

    def yhop(s, d, arriving=False):
        i = d if d < 1 else 1 + side(s) * 4 + d - 1
        i = 9 if d < 0 else i
        who = oy if arriving else y
        base = 0 if d < 0 else HALF
        base = base + (side(s) * (HALF // 2) if d == 4 else 0)
        at = full.at[who, zof(-s * max(d, 0)), pl.ds(base, HALF // 2 if d == 4 else HALF)]
        return remote(at, at, ys.at[i], yr.at[i], ydev)

    def ehop(s, c, d, arriving=False):
        i = (side(s), c, d - 1)
        at = edges.at[xof(-s * d if arriving else -s * (d - 1)), pl.ds(half + c * PART, PART)]
        return remote(at, at, es.at[i], er.at[i], xdev(s))

    def ehand(s, c, d, arriving=False):
        i = (side(s), c, d - 1)
        at = edges.at[xof(-s * d), pl.ds((other if arriving else half) + c * PART, PART)]
        return remote(at, at, bs.at[i], br.at[i], beside)

    def nth(s, i):
        return i if s > 0 else (i + 2) % 4

    def chop(k, arriving=False):
        at = marks.at[xof(-k) if arriving else x]
        return remote(codes if not arriving else at, at, cs.at[k - 1], cr.at[k - 1], xdev(k))

    yhop(1, -1).start()
    for s in BOTH:
        zhop(s, 2, 1).start()
        zhop(s, 0, 1).start()
    for k in range(1, NX):
        chop(k).start()
    yhop(1, 0).start()
    xstep, xfinish = exchange(feats, lambda k: xfull.at[k], feat, node, 0, fs, fr)
    wstep, wfinish = exchange(wself, lambda k: wfull.at[k, 0], feat, node, 3, fs, fr)
    vstep, vfinish = exchange(wneigh, lambda k: wfull.at[k, 1], feat, node, 6, fs, fr)
    small[1].wait()
    small[2].wait()

    def zpass(u, d):
        for s in BOTH:
            zhop(s, u, d, True).wait_recv()
            if d < 4:
                zhop(s, u, d + 1).start()
            if u == 2:
                yhop(s, d).start()

    def eround(i):
        for s in BOTH:
            c = nth(s, i)
            ehop(s, c, 1, True).wait_recv()
            if i < 2:
                ehop(s, c, 2).start()
            ehand(s, c, 1).start()

    def efar(i):
        for s in BOTH:
            c = nth(s, i)
            ehop(s, c, 2, True).wait_recv()
            ehand(s, c, 2).start()

    def efirst(i):
        for s in BOTH:
            ehop(s, nth(s, i), 1).start()

    def ycross():
        yhop(1, -1, True).wait_recv()
        for s in BOTH:
            zhop(s, 1, 1).start()

    def passon():
        for step in (xstep, wstep, vstep):
            step()

    state = {}

    def prepare():
        load(4).wait()
        span = pl.ds(other, SLOTS // 2)
        edges[x, span] = raw[span].astype(jnp.int16)
        for k in range(1, NX):
            chop(k, True).wait_recv()
        code = jnp.concatenate([marks[b, 0:2] for b in range(NX)], axis=0)
        col = jnp.bitwise_and(code, 511)
        mine = jnp.where(
            jnp.logical_and(code >= 0, jnp.bitwise_and(lax.shift_right_logical(col, 3), 3) == x), 1.0, 0.0
        )
        slot = iota((8, TILE), 0) * TILE + iota((8, TILE), 1)
        row = lax.shift_right_logical(slot, 8) * TPN + jnp.bitwise_and(lax.shift_right_arithmetic(code, 16), 7)
        near = lax.shift_left(lax.shift_right_logical(col, 5), 3) + jnp.bitwise_and(col, 7)
        upto = jnp.where(iota((TILE, TILE), 0) <= iota((TILE, TILE), 1), 1.0, 0.0).astype(BF)
        tile = jnp.bitwise_and(row, 7)
        runs, begin, places = [], jnp.zeros((1, TILE), F32), []
        for b in range(NX):
            seen = jnp.zeros((TPN, 1), F32)
            for r in (2 * b, 2 * b + 1):
                hot = jnp.where(iota((TPN, TILE), 0) == tile[r:r + 1], mine[r:r + 1], 0.0)
                rank = dot(hot.astype(BF), upto) + seen
                runs.append((hot, rank))
                seen = rank[:, TILE - 1:TILE]
            even = jnp.broadcast_to(2.0 * jnp.floor((seen + 1.0) * 0.5), (TPN, TILE))
            starts = []
            for j in range(TPN):
                starts.append(begin)
                begin = begin + even[j:j + 1]
            start = jnp.concatenate(starts, axis=0) - 1.0
            for r in (2 * b, 2 * b + 1):
                hot, rank = runs[r]
                place = jnp.sum(hot * (start + rank), axis=0, keepdims=True)
                places.append(jnp.where(mine[r:r + 1] > 0.0, place, -1.0e6))
        base = begin
        pos = jnp.concatenate(places + [jnp.zeros((TILE - 8, TILE), F32)], axis=0).T
        wide = iota((TILE, LISTED * TILE), 1).astype(F32)
        picked = jnp.zeros((8, LISTED * TILE), F32)
        fields = (jnp.bitwise_and(slot, 255), lax.shift_right_logical(slot, 8), row, near + 128)
        state.update(pos=pos, base=base, wide=wide, picked=picked, fields=fields)

    def pick(r):
        pos, wide, fields = state["pos"], state["wide"], state["fields"]
        hot = jnp.where(pos[:, r:r + 1] == wide, 1.0, 0.0).astype(BF)
        stack = jnp.concatenate([f[r:r + 1].astype(F32) for f in fields] + [jnp.zeros((4, TILE), F32)], axis=0)
        state["picked"] += dot(stack.astype(BF), hot)

    def enlist():
        picked, base = state["picked"], state["base"]
        items = (picked[0:1] + 256.0 * picked[1:2] + 1024.0 * picked[2:3] + 32768.0 * picked[3:4]).astype(jnp.int32)
        for r in range(LISTED):
            listed[r:r + 1] = items[:, r * TILE:(r + 1) * TILE]
        listed[LISTED:16] = jnp.broadcast_to(base, (16 - LISTED, TILE)).astype(jnp.int32)

    steps = {"z": zpass, "e": eround, "h": efar, "s": efirst, "y": ycross, "x": passon, "c": prepare, "l": pick, "i": enlist}
    for step in ORDER:
        steps[step[0]](*(int(digit) for digit in step[1:]))
    for s in BOTH:
        for i in range(4):
            c = nth(s, i)
            for d in (1, 2) if i < 2 else (1,):
                ehand(s, c, d, True).wait_recv()
                ehand(s, c, d).wait_send()
                ehop(s, c, d).wait_send()
        for d in range(1, 5):
            for u in range(3):
                zhop(s, u, d).wait_send()
            yhop(s, d, True).wait_recv()
            yhop(s, d).wait_send()
    yhop(1, 0, True).wait_recv()
    yhop(1, 0).wait_send()
    yhop(1, -1).wait_send()
    for k in range(1, NX):
        chop(k).wait_send()
    xfinish()
    wfinish()
    vfinish()


def gather(feats, wself, wneigh, rows, cols, count, words):
    dma = pltpu.SemaphoreType.DMA
    return pl.pallas_call(
        gather_kernel,
        out_shape=(
            OUT((NY, NZ, TPN, FC, TILE), BF),
            OUT((4, FC, ROWS), BF),
            OUT((4, 2, FC, 4 * FC), BF),
            OUT((NX, *words.shape), jnp.int16),
            jax.ShapeDtypeStruct((16, TILE), jnp.int32),
        ),
        in_specs=[HBM] * 5 + [SMEM, HBM],
        out_specs=(VMEM,) * 5,
        scratch_shapes=[
            pltpu.VMEM(words.shape, jnp.int32), pltpu.VMEM((2, 2, TILE), jnp.int32),
            pltpu.VMEM((8, TILE), jnp.int32), pltpu.VMEM((NX, 8, TILE), jnp.int32),
            dma((2, 3, 4)), dma((2, 3, 4)), dma((2, 4, 2)), dma((2, 4, 2)), dma((2, 4, 2)), dma((2, 4, 2)),
            dma((3,)), dma((3,)), dma((10,)), dma((10,)), dma((9,)), dma((9,)), dma((10,)),
        ],
        compiler_params=pltpu.CompilerParams(
            collective_id=0, has_side_effects=True, vmem_limit_bytes=24 * 2**20
        ),
        name="gather",
    )(feats, wself, wneigh, rows, cols, count, words)


def planes_of(words):
    one, zero = jnp.ones(words.shape, BF), jnp.zeros(words.shape, BF)
    return jnp.concatenate(
        [jnp.where(jnp.bitwise_and(words, jnp.int16(1 << b)) != 0, one, zero) for b in range(8)], axis=0
    )


def entry(slots, group, u, edges):
    item = slots[group // TURNS, lax.rem(group, TURNS) * UNROLL + u]
    words = edges[jnp.bitwise_and(lax.shift_right_logical(item, 8), 3), jnp.bitwise_and(item, 255)]
    planes = planes_of(jnp.where(item > 0, words, jnp.zeros_like(words)))
    row, col = lax.shift_right_logical(item, 10), lax.shift_right_logical(item, 15)
    return jnp.bitwise_and(row, 31), jnp.bitwise_and(col, 127), planes


def forward_kernel(slots, edges, full, acc):
    acc[...] = jnp.zeros_like(acc)
    count = slots[LISTED, 0]
    ones = jnp.ones((CNT, TILE), BF)

    def source(col):
        near, t = lax.shift_right_logical(col, 3), jnp.bitwise_and(col, 7)
        return jnp.concatenate([full[lax.shift_right_logical(near, 3), jnp.bitwise_and(near, 7), t], ones], axis=0)

    def group(g, _):
        for u in range(0, UNROLL, 2):
            row, one, first = entry(slots, g, u, edges)
            _, two, second = entry(slots, g, u + 1, edges)
            acc[lax.shift_right_logical(row, 3), jnp.bitwise_and(row, 7)] += dot(
                jnp.concatenate([source(one), source(two)], axis=1), jnp.concatenate([first, second], axis=0)
            )
        return 0

    lax.fori_loop(0, (count + UNROLL - 1) // UNROLL, group, 0)


def forward(slots, edges, full):
    return pl.pallas_call(
        forward_kernel,
        out_shape=OUT((NX, TPN, FC + CNT, TILE), F32),
        in_specs=[SMEM, VMEM, VMEM],
        out_specs=VMEM,
        compiler_params=pltpu.CompilerParams(vmem_limit_bytes=24 * 2**20),
        name="forward_sums",
    )(slots, edges, full)


DENSE = (
    "a0", "a1", "b0", "a2", "b1", "g0", "a3", "b2", "g1", "h0",
    "b3", "g2", "h1", "s0", "g3", "h2", "s1", "h3", "s2", "s3",
)


def dense_kernel(part, xfull, wfull, wself, wneigh, cot, act, direct, scaled, wgrad,
                 pq, pm, rq, rm, av, gr, send, recv, rs, rr, ss, sr):
    y, z, x, feat = place()
    node = node_of(y, z, x)
    CT = TPN // PARTS
    SPAN = ROWS // PARTS

    def xof(k):
        return lax.rem(x + k + 2 * NX, NX)

    def xdev(s):
        return (node_of(y, z, xof(s)), feat)

    peers = [xdev(1), xdev(-1), xdev(2), (node, across(feat)), (node, sibling(feat))]
    barrier = pltpu.get_barrier_semaphore()
    for peer in peers:
        pl.semaphore_signal(barrier, inc=1, device_id=peer, device_id_type=MESH)

    def pack(c, k):
        block = xof(k)
        for q in range(CT):
            r = c * CT + q
            sums = part[block, r, 0:FC]
            most = jnp.maximum(jnp.max(jnp.abs(sums), axis=0, keepdims=True), 1e-30)
            pq[c, k - 1, q] = jnp.round(sums * (32766.0 / most)).astype(jnp.int32).astype(jnp.int16)
            pm[c, k - 1, q:q + 1] = most * (1.0 / 32766.0)
            pm[c, k - 1, CT + q:CT + q + 1] = part[block, r, FC:FC + 1]

    def hop(c, k, what):
        i = (c, k - 1, what)
        src, dst = ((pq, rq), (pm, rm))[what]
        return remote(src.at[c, k - 1], dst.at[c, k - 1], rs.at[i], rr.at[i], xdev(k))

    ORDER = (2, 1, 3)
    for k in ORDER:
        pack(0, k)
    pl.semaphore_wait(barrier, len(peers))
    for c in range(PARTS):
        for k in ORDER:
            if c > 0:
                pack(c, k)
            hop(c, k, 1).start()
            hop(c, k, 0).start()

    choose = (iota((FC, 4 * FC), 1) == iota((FC, 4 * FC), 0) + feat * FC).astype(F32).astype(BF)

    def cols_of(k, which):
        return nt(choose, wfull[k, which]).astype(BF)

    itself = jnp.concatenate([cols_of(k, 0) for k in range(4)], axis=1)
    neigh = jnp.concatenate([cols_of(k, 1) for k in range(4)], axis=1)
    pre = dot(itself, xfull[...].reshape(4 * FC, ROWS))

    def share(ref, stage, c):
        return exchange(
            ref.at[c, feat], lambda k: ref.at[c, k], feat, node, 3 * (stage * PARTS + c), send, recv
        )

    degrees, first, second = {}, {}, {}

    def average(c):
        for k in ORDER:
            for what in (1, 0):
                hop(c, k, what).wait_recv()
        for q in range(CT):
            r = c * CT + q
            total = part[x, r, 0:FC]
            degree = part[x, r, FC:FC + 1]
            for k in range(3):
                total += rq[c, k, q].astype(jnp.int32).astype(F32) * rm[c, k, q:q + 1]
                degree += rm[c, k, CT + q:CT + q + 1]
            degrees[r] = jnp.maximum(degree, 1.0)
            av[c, feat, :, q * TILE:(q + 1) * TILE] = (total / degrees[r]).astype(BF)
        first[c] = share(av, 0, c)

    def gradient(c):
        first[c][1]()
        span = slice(c * SPAN, (c + 1) * SPAN)
        own = pre[:, span] + dot(neigh, av[c].reshape(4 * FC, SPAN))
        sig = jax.nn.sigmoid(own)
        grad = cot[:, span] * sig * (1.0 + own * (1.0 - sig))
        gr[c, feat] = grad.astype(BF)
        second[c] = share(gr, 1, c)
        act[:, span] = own * sig

    def shop(c, k, arriving=False):
        at = scaled.at[xof(-k) if arriving else x, pl.ds(c * CT, CT)]
        return remote(at, at, ss.at[c, k - 1], sr.at[c, k - 1], xdev(k))

    def scale(c):
        second[c][1]()
        sums = dot(wneigh[...], gr[c].reshape(4 * FC, SPAN))
        for q in range(CT):
            r = c * CT + q
            scaled[x, r] = (sums[:, q * TILE:(q + 1) * TILE] / degrees[r]).astype(BF)
        for k in ORDER:
            shop(c, k).start()

    steps = {
        "a": average, "b": lambda c: first[c][0](), "g": gradient, "h": lambda c: second[c][0](), "s": scale
    }
    for step in DENSE:
        steps[step[0]](int(step[1]))
    for c in range(PARTS):
        direct[:, c * SPAN:(c + 1) * SPAN] = dot(wself[...], gr[c].reshape(4 * FC, SPAN))
    mine, near = jnp.zeros((FC, 4 * FC), F32), jnp.zeros((FC, 4 * FC), F32)
    for c in range(PARTS):
        grads = gr[c].reshape(4 * FC, SPAN)
        mine += nt(xfull[feat, :, c * SPAN:(c + 1) * SPAN], grads)
        near += nt(av[c, feat], grads)
    wgrad[0:FC] = mine
    wgrad[FC:2 * FC] = near
    for c in range(PARTS):
        for k in ORDER:
            shop(c, k, True).wait_recv()
            shop(c, k).wait_send()
            for what in range(2):
                hop(c, k, what).wait_send()


def dense(part, xfull, wfull, wself, wneigh, cot):
    dma = pltpu.SemaphoreType.DMA
    return pl.pallas_call(
        dense_kernel,
        out_shape=(
            jax.ShapeDtypeStruct((FC, ROWS), F32),
            OUT((FC, ROWS), F32),
            OUT((NX, TPN, FC, TILE), BF),
            OUT((2 * FC, 4 * FC), F32),
        ),
        in_specs=[VMEM] * 6,
        out_specs=(VMEM,) * 4,
        scratch_shapes=[
            pltpu.VMEM((PARTS, 3, TPN // PARTS, FC, TILE), jnp.int16), pltpu.VMEM((PARTS, 3, 8, TILE), F32),
            pltpu.VMEM((PARTS, 3, TPN // PARTS, FC, TILE), jnp.int16), pltpu.VMEM((PARTS, 3, 8, TILE), F32),
            pltpu.VMEM((PARTS, 4, FC, ROWS // PARTS), BF), pltpu.VMEM((PARTS, 4, FC, ROWS // PARTS), BF),
            dma((6 * PARTS,)), dma((6 * PARTS,)), dma((PARTS, 3, 2)), dma((PARTS, 3, 2)),
            dma((PARTS, 3)), dma((PARTS, 3)),
        ],
        compiler_params=pltpu.CompilerParams(
            collective_id=1, has_side_effects=True, vmem_limit_bytes=24 * 2**20
        ),
        name="dense",
    )(part, xfull, wfull, wself, wneigh, cot)


def backward_kernel(slots, edges, source, act, out, acted, acc):
    acted[...] = act[...]
    acc[...] = jnp.zeros_like(acc)
    count = slots[LISTED, 0]

    def group(g, _):
        for u in range(0, UNROLL, 2):
            row, one, first = entry(slots, g, u, edges)
            _, two, second = entry(slots, g, u + 1, edges)
            sums = nt(
                source[lax.shift_right_logical(row, 3), jnp.bitwise_and(row, 7)],
                jnp.concatenate([first, second], axis=0),
            )
            acc[one] += sums[:, 0:TILE]
            acc[two] += sums[:, TILE:2 * TILE]
        return 0

    lax.fori_loop(0, (count + UNROLL - 1) // UNROLL, group, 0)
    for y in range(NY):
        for z in range(NZ):
            base = (y * NZ + z) * TPN
            out[y, z] = acc[base:base + TPN].astype(BF)


def backward(slots, edges, source, act):
    return pl.pallas_call(
        backward_kernel,
        out_shape=(OUT((NY, NZ, TPN, FC, TILE), BF), jax.ShapeDtypeStruct((FC, ROWS), F32)),
        in_specs=[SMEM, VMEM, VMEM, VMEM],
        out_specs=(VMEM, VMEM),
        scratch_shapes=[pltpu.VMEM((NY * NZ * TPN, FC, TILE), F32)],
        compiler_params=pltpu.CompilerParams(vmem_limit_bytes=24 * 2**20),
        name="backward_sums",
    )(slots, edges, source, act)


W_AT = ((4, 0), (3, 0), (2, 0))
NEAR = 3


def scatter_kernel(part, wgrad, direct, out, wout, rz, ry, rl, w1, w2, w3, w4, zs, zr, ys, yr, ws, wr):
    y, z, x, feat = place()
    oy = 1 - y
    FAR = TPN - NEAR

    def zof(k):
        return lax.rem(z + k + 2 * NZ, NZ)

    def zdev(s):
        return (node_of(y, zof(s), x), feat)

    plane = y * NX + x

    def pdev(k):
        p = lax.rem(plane + k, NY * NX)
        return (node_of(p // NX, z, lax.rem(p, NX)), feat)

    meet([zdev(k) for k in range(1, NZ)] + [pdev(k) for k in range(1, NY * NX)])
    ydev = (node_of(oy, z, x), feat)

    def term(u, k):
        if u == 2:
            return ry.at[(k + NZ) % NZ]
        return part.at[oy if u == 1 else y, zof(k), pl.ds(0, NEAR)]

    def size(u):
        return FAR if u == 2 else NEAR

    def cut(u, k):
        return pl.ds(0, 2) if k == 0 else pl.ds(2, size(u) - 2)

    def slot(s, u, d):
        return rz.at[side(s), u, d - 1, pl.ds(0, size(u))]

    def hop(s, u, d):
        i = (side(s), u, d - 1)
        src, dst = term(u, 4) if d == 4 else slot(s, u, d + 1), slot(s, u, d)
        if d == 4:
            src, dst = src.at[cut(u, side(s))], dst.at[cut(u, side(s))]
        return remote(src, dst, zs.at[i], zr.at[i], zdev(s))

    def yhop(k):
        return remote(part.at[oy, zof(k), pl.ds(NEAR, FAR)], ry.at[(k + NZ) % NZ],
                      ys.at[(k + NZ) % NZ], yr.at[(k + NZ) % NZ], ydev)

    def join(k):
        yhop(k).wait_recv()
        at = (k + NZ) % NZ
        ry[at] = (ry[at].astype(F32) + part[y, zof(k), NEAR:TPN].astype(F32)).astype(BF)

    last = remote(slot(1, 1, 1), rl, ys.at[NZ], yr.at[NZ], ydev)

    def rows(p):
        return pl.ds(pl.multiple_of(p * 16, 16), 16)

    def pof(k):
        return lax.rem(plane + k + NY * NX, NY * NX)

    def wcopy(phase, k):
        i = phase * 7 + k - 1
        peer = pdev(k) if phase in (0, 3) else zdev(k)
        src, dst = (
            (wgrad.at[rows(pof(k))], w1.at[k - 1]), (w2.at[zof(k)], w3.at[k - 1]), (w4.at[z], w4.at[z]),
            (wout.at[rows(plane)], wout.at[rows(plane)]),
        )[phase]
        return remote(src, dst, ws.at[i], wr.at[i], peer)

    def wexpect(phase, k):
        i = phase * 7 + k - 1
        dst = (w1.at[k - 1], w3.at[k - 1], w4.at[zof(-k)], wout.at[rows(pof(-k))])[phase]
        return remote(dst, dst, ws.at[i], wr.at[i], zdev(k))

    def wturn(phase):
        for k in range(1, 8):
            wexpect(phase, k).wait_recv()
        if phase == 0:
            acc = wgrad[rows(plane)]
            for k in range(1, 8):
                acc += w1[k - 1]
            for q in range(NZ):
                w2[q] = acc[2 * q:2 * q + 2]
        elif phase == 1:
            acc = w2[z]
            for k in range(1, 8):
                acc += w3[k - 1]
            w4[z] = acc
        else:
            wout[rows(plane)] = jnp.concatenate([w4[q] for q in range(NZ)], axis=0)
        for k in range(1, 8):
            wcopy(phase + 1, k).start()

    for k in range(1, 8):
        wcopy(0, k).start()
    for k in (4, 3, -3):
        yhop(k).start()
    for u in (1, 0):
        for s in BOTH:
            hop(s, u, 4).start()
    for k in (2, -2, 1, -1, 0):
        yhop(k).start()
    join(4)
    for s in BOTH:
        hop(s, 2, 4).start()
    for d in (4, 3, 2):
        for u in (1, 0, 2):
            if u == 2:
                join(d - 1)
                join(1 - d)
            for s in BOTH:
                hop(s, u, d).wait_recv()
                i = (side(s), u, d - 1)
                more = term(u, s * (d - 1))
                if d == 4:
                    a, b = cut(u, side(s)), cut(u, 1 - side(s))
                    rz[(*i, a)] = (rz[(*i, a)].astype(F32) + more[a].astype(F32)).astype(BF)
                    rz[(*i, b)] = more[b]
                else:
                    i = (*i, slice(0, size(u)))
                    rz[i] = (rz[i].astype(F32) + more[...].astype(F32)).astype(BF)
                hop(s, u, d - 1).start()
            if (d, u) in W_AT:
                wturn(W_AT.index((d, u)))

    def total(u):
        for s in BOTH:
            hop(s, u, 1).wait_recv()
        one, two = rz[0, u, 0, 0:size(u)].astype(F32), rz[1, u, 0, 0:size(u)].astype(F32)
        return term(u, 0)[...].astype(F32) + one + two

    perm = order()

    def finish(base, sums):
        flat = sums.reshape(-1, TILE)
        high = flat.astype(BF)
        back = dot(high, perm) + dot((flat - high.astype(F32)).astype(BF), perm)
        for t in range(sums.shape[0]):
            lanes = slice((base + t) * TILE, (base + t + 1) * TILE)
            out[:, lanes] = direct[:, lanes] + back[t * FC:(t + 1) * FC]

    rz[0, 1, 0, 0:NEAR] = total(1).astype(BF)
    last.start()
    join(0)
    finish(NEAR, total(2))
    sums = total(0)
    last.wait_recv()
    finish(0, sums + rl[...].astype(F32))
    for k in range(1, NZ):
        wexpect(3, k).wait_recv()
    for s in BOTH:
        for u in range(3):
            for d in range(1, 5):
                hop(s, u, d).wait_send()
    for k in range(NZ):
        yhop(k).wait_send()
    last.wait_send()
    for phase in range(4):
        for k in range(1, 8):
            wcopy(phase, k).wait_send()


def scatter(part, wgrad, direct):
    dma = pltpu.SemaphoreType.DMA
    return pl.pallas_call(
        scatter_kernel,
        out_shape=(
            jax.ShapeDtypeStruct((FC, ROWS), F32),
            jax.ShapeDtypeStruct((2 * FC, 4 * FC), F32),
        ),
        in_specs=[VMEM, VMEM, VMEM],
        out_specs=(VMEM, VMEM),
        scratch_shapes=[
            pltpu.VMEM((2, 3, 4, TPN - NEAR, FC, TILE), BF),
            pltpu.VMEM((NZ, TPN - NEAR, FC, TILE), BF),
            pltpu.VMEM((NEAR, FC, TILE), BF),
            pltpu.VMEM((NZ - 1, 16, 256), F32),
            pltpu.VMEM((NZ, 2, 256), F32), pltpu.VMEM((NZ - 1, 2, 256), F32), pltpu.VMEM((NZ, 2, 256), F32),
            dma((2, 3, 4)), dma((2, 3, 4)), dma((NZ + 1,)), dma((NZ + 1,)), dma((28,)), dma((28,)),
        ],
        compiler_params=pltpu.CompilerParams(
            collective_id=2, has_side_effects=True, vmem_limit_bytes=24 * 2**20
        ),
        name="scatter",
    )(part, wgrad, direct)


def local(features, w_self, w_neigh, tile_rows, tile_cols, tile_count, edge_bits, cotangent):
    rows, cols = tile_rows.reshape(2, TILE), tile_cols.reshape(2, TILE)
    given = [
        pltpu.with_memory_space_constraint(a, pltpu.HBM)
        for a in (features.T, w_self, w_neigh, rows, cols, edge_bits)
    ]
    full, xfull, wfull, edges, slots = gather(*given[:5], tile_count, given[5])
    part = forward(slots, edges, full)
    act, direct, scaled, wgrad = dense(part, xfull, wfull, w_self, w_neigh, cotangent.T)
    part, act = backward(slots, edges, scaled, act)
    grad, wsum = scatter(part, wgrad, direct)
    return act.T, grad.T, wsum[:FC], wsum[FC:]


def solution(mesh):
    placed = (
        P("node", "feat"),
        P("feat", None),
        P("feat", None),
        P("node"),
        P("node"),
        P("node"),
        P("node", None, None),
        P("node", "feat"),
    )
    return jax.shard_map(
        local,
        mesh=mesh,
        in_specs=placed,
        out_specs=(P("node", "feat"), P("node", "feat"), P("feat", None), P("feat", None)),
        check_vma=False,
    )
```
